512 devices in a mesh: cube: 32 (over x, z_lo, core), wide: 16 (over z_hi, y).
Axes of the slice: x: 4, y: 4, z: 16 (z_hi: 4, z_lo: 4; z = z_hi * 4 + z_lo), core: 2. Of those that a mesh axis runs over, the one named last changes fastest.
Arguments:
- leaf_updates: float32 [32, 2048, 2048], P('cube', 'wide'), may hold values from -1 to 1, as said below
- level1_entries: float32 [2048, 32, 2, 512], P('wide', 'cube'), may hold values from -1 to 1, as said below
- level2_entries: float32 [2048, 32, 512], P('wide', 'cube'), may hold values from -1 to 97, as said below
- leaf_maps: int32 [32, 2048], replicated, may hold values from 0 to 2047, as said below
- leaf_live: int32 [32, 16], replicated, may hold values from 32 to 128
- parent_maps: int32 [16, 2048], replicated, may hold values from 0 to 2047, as said below
- parent_live: int32 [16, 16], replicated, may hold values from 32 to 128
Outputs:
- panel_factor: float32 [32, 512, 128], P('cube', 'wide')
- schur_rows: float32 [2048, 32, 512], P('wide', 'cube')
The draws below stay inside these ranges and needn't reach their ends.
Inputs may be any that keep to these rules, and one draw needn't show every extreme that they name: Within each index block, leaf_maps[c, b * 128 to (b + 1) * 128 - 1] is a permutation of the same range of indices. Within each index block, parent_maps[p, b * 128 to (b + 1) * 128 - 1] is a permutation of the same range of indices. `leaf_updates`: each leaf update matrix is symmetric. `level1_entries`: each level-1 front's initial entries form a symmetric matrix. `level2_entries`: each level-2 front's initial entries form a symmetric matrix; its diagonal entries at the indices of P are at least 47.
All inputs are finite; a program needn't handle non-finite values.
Results may differ from the reference program's by a relative error of at most 0.0003.
Values sent between devices are 32-bit elements; how exact they have to be, the bound alone decides.
A program may use at most 64 MiB of HBM per device.

```python
import jax
import jax.numpy as jnp
from jax import lax

BLOCK = 128
CYCLIC = 8
PANEL = 128
ORDER = 2048
QUART = 512
BLOCKS = 16
LEAVES = 32
PARENTS = 16
N_CUBE = 32
N_WIDE = 16


def symmetric_uniform(subkey, count, front_order):
    values = jax.random.uniform(subkey, (count, front_order, front_order), jnp.float32, -1.0, 1.0)
    return 0.5 * (values + jnp.swapaxes(values, 1, 2))


def block_permutations(subkey, count):
    subkeys = jax.random.split(subkey, count * BLOCKS)

    def permute_one(single_key):
        return jax.random.permutation(single_key, BLOCK)
    permuted = jax.vmap(permute_one)(subkeys).astype(jnp.int32)
    starts = jnp.arange(count * BLOCKS, dtype=jnp.int32) % BLOCKS * BLOCK
    return (permuted + starts[:, None]).reshape(count, ORDER).astype(jnp.int32)


def block_live_draw(subkey, count):
    counts = jax.random.randint(subkey, (count, BLOCKS), BLOCK // 4, BLOCK + 1, dtype=jnp.int32)
    counts = counts.at[:, 0].set(BLOCK)
    counts = counts.at[:, 1].set(BLOCK // 4)
    return counts


def draw_leaf_updates(key, part):
    return symmetric_uniform(jax.random.fold_in(key, 5), LEAVES, ORDER)


def draw_level1_entries(key, part):
    fronts = symmetric_uniform(jax.random.fold_in(key, 6), PARENTS, ORDER)
    fronts = fronts.reshape(PARENTS, ORDER, 2, 2, QUART)
    fronts = jnp.transpose(fronts, (1, 0, 3, 2, 4))
    return fronts.reshape(ORDER, LEAVES, 2, QUART)


def draw_level2_entries(key, part):
    fronts = symmetric_uniform(jax.random.fold_in(key, 7), LEAVES // 4, ORDER)
    extra = jax.random.uniform(jax.random.fold_in(key, 8), (LEAVES // 4, ORDER), jnp.float32, 48.0, 96.0)
    positions = jnp.arange(ORDER, dtype=jnp.int32)
    extra = jnp.where(positions[None, :] % QUART < PANEL // 4, extra, 0.0)
    diagonal = (positions[:, None] == positions[None, :]).astype(jnp.float32)
    fronts = fronts + extra[:, :, None] * diagonal[None, :, :]
    fronts = fronts.reshape(LEAVES // 4, ORDER, 4, QUART)
    fronts = jnp.transpose(fronts, (1, 0, 2, 3))
    return fronts.reshape(ORDER, LEAVES, QUART)


def draw_leaf_maps(key, part):
    return block_permutations(jax.random.fold_in(key, 1), LEAVES)


def draw_leaf_live(key, part):
    return block_live_draw(jax.random.fold_in(key, 2), LEAVES)


def draw_parent_maps(key, part):
    return block_permutations(jax.random.fold_in(key, 3), PARENTS)


def draw_parent_live(key, part):
    return block_live_draw(jax.random.fold_in(key, 4), PARENTS)


def setup_inputs(seed: int = 0) -> dict:
    streams_of = jax.random.split(jax.random.key(seed), 8)
    return {
        "leaf_updates": draw_leaf_updates(jax.random.fold_in(streams_of[7], 71), 0),
        "level1_entries": draw_level1_entries(jax.random.fold_in(streams_of[7], 71), 0),
        "level2_entries": draw_level2_entries(jax.random.fold_in(streams_of[7], 71), 0),
        "leaf_maps": draw_leaf_maps(jax.random.fold_in(streams_of[7], 71), 0),
        "leaf_live": draw_leaf_live(jax.random.fold_in(streams_of[7], 71), 0),
        "parent_maps": draw_parent_maps(jax.random.fold_in(streams_of[7], 71), 0),
        "parent_live": draw_parent_live(jax.random.fold_in(streams_of[7], 71), 0),
    }


HIGHEST = lax.Precision.HIGHEST

def block_onehot(offsets_map, live_amounts, block_rows):
    block_count = offsets_map.shape[0] // block_rows
    offsets = offsets_map.reshape(block_count, block_rows) - (jnp.arange(block_count, dtype=jnp.int32) * block_rows)[:, None]
    living = jnp.arange(block_rows, dtype=jnp.int32)[None, :] < live_amounts[:, None]
    matched = (offsets[:, :, None] == jnp.arange(block_rows, dtype=jnp.int32)[None, None, :]) & living[:, :, None]
    return matched.astype(jnp.float32)

def extend_full(matrix, onehot):
    front_order = matrix.shape[0]
    block_count = onehot.shape[0]
    block_rows = onehot.shape[1]
    mapped_rows = jnp.einsum('bik,bif->bkf', onehot, matrix.reshape(block_count, block_rows, front_order), precision=HIGHEST)
    mapped_rows = mapped_rows.reshape(front_order, block_count, block_rows)
    mapped = jnp.einsum('fbj,bjk->fbk', mapped_rows, onehot, precision=HIGHEST)
    return mapped.reshape(front_order, front_order)

def reference(leaf_updates, level1_entries, level2_entries, leaf_maps, leaf_live, parent_maps, parent_live):
    groups = N_CUBE // 4
    updates = leaf_updates.reshape(groups, 4, ORDER, ORDER)
    first_level = jnp.moveaxis(level1_entries.reshape(ORDER, groups, 2, 2, 2, QUART), 1, 0)
    second_level = jnp.moveaxis(level2_entries.reshape(ORDER, groups, 4, QUART), 1, 0)
    leaf_offsets = leaf_maps.reshape(groups, 4, ORDER)
    leaf_counts = leaf_live.reshape(groups, 4, BLOCKS)
    parent_offsets = parent_maps.reshape(groups, 2, ORDER)
    parent_counts = parent_live.reshape(groups, 2, BLOCKS)
    pivot_index = (jnp.arange(4, dtype=jnp.int32)[:, None] * QUART + jnp.arange(PANEL // 4, dtype=jnp.int32)[None, :]).reshape(PANEL)

    def one_group(group_items):
        updates_g, first_g, second_g, leaf_off, leaf_cnt, parent_off, parent_cnt = group_items
        second_front = second_g.reshape(ORDER, ORDER)
        for parent_slot in range(2):
            assembled = jnp.transpose(first_g[:, parent_slot], (0, 2, 1, 3)).reshape(ORDER, ORDER)
            for sibling in range(2):
                child = 2 * parent_slot + sibling
                assembled = assembled + extend_full(updates_g[child], block_onehot(leaf_off[child], leaf_cnt[child], BLOCK))
            second_front = second_front + extend_full(assembled, block_onehot(parent_off[parent_slot], parent_cnt[parent_slot], BLOCK))
        pivot_cols = second_front[:, pivot_index]
        pivot_block = jnp.linalg.cholesky(pivot_cols[pivot_index])
        panel_cols = lax.linalg.triangular_solve(pivot_block, pivot_cols, left_side=False, lower=True, transpose_a=True)
        schur_part = second_front - jnp.dot(panel_cols, panel_cols.T, precision=HIGHEST)
        positions = jnp.arange(ORDER, dtype=jnp.int32)
        outside = positions % QUART >= PANEL // 4
        kept_mask = outside[:, None] & outside[None, :]
        schur_part = jnp.where(kept_mask, schur_part, jnp.zeros_like(schur_part))
        cyclic_order = positions.reshape(ORDER // (CYCLIC * N_WIDE), N_WIDE, CYCLIC).transpose(1, 0, 2).reshape(ORDER)
        schur_part = schur_part[cyclic_order]
        return (panel_cols.reshape(4, QUART, PANEL), schur_part.reshape(ORDER, 4, QUART))
    panels, schurs = lax.map(one_group, (updates, first_level, second_level, leaf_offsets, leaf_counts, parent_offsets, parent_counts))
    panel_factor = panels.reshape(N_CUBE, QUART, PANEL)
    schur_rows = jnp.moveaxis(schurs, 0, 1).reshape(ORDER, N_CUBE, QUART)
    return (panel_factor, schur_rows)
```

```python
import jax
import jax.numpy as jnp
from jax import lax
from jax.experimental import pallas as pl
from jax.experimental.pallas import tpu as pltpu
from jax.sharding import PartitionSpec as P

F32 = jnp.float32
BF16 = jnp.bfloat16
MESH = pl.DeviceIdType.MESH
HIGHEST = lax.Precision.HIGHEST
B = 128
Q = 512
PIV = 32
CYC = 8


def iota(shape, dim):
    return lax.broadcasted_iota(jnp.int32, shape, dim)


def kernel(
    x_hbm, l1_hbm, l2_hbm, lm_hbm, ll_hbm, pm_hbm, pv_hbm,
    panel_hbm, schur_hbm,
    x_v, l1_v, l2_v, lm_v, pm_v, ll_s, pv_s,
    zs, zo, zr, us, uk, ur, f2, f2r, at, lt, msg, msgs, mat, linv, tr_v, out_v, panel_v,
    in_sem, e1_send, e1_recv, e2_send, e2_recv, aa_send, aa_recv,
    sc_send, sc_recv, zg_send, yg_send, pg_recv, cb_send, cb_recv, out_sem,
):
    cube = lax.axis_index("cube")
    wide = lax.axis_index("wide")
    low = cube % 2
    high = cube // 2 % 2
    quarter = cube % 4
    group = cube - quarter
    z_hi = wide // 4
    y = wide % 4
    parent = cube // 2

    lm_base = pl.multiple_of(cube // 8 * 8, 8)
    pm_base = pl.multiple_of(parent // 8 * 8, 8)
    loads = [
        pltpu.make_async_copy(lm_hbm.at[pl.ds(lm_base, 8)], lm_v, in_sem.at[0]),
        pltpu.make_async_copy(ll_hbm, ll_s, in_sem.at[1]),
        pltpu.make_async_copy(x_hbm.at[0], x_v, in_sem.at[2]),
        pltpu.make_async_copy(l1_hbm, l1_v, in_sem.at[3]),
        pltpu.make_async_copy(pm_hbm.at[pl.ds(pm_base, 8)], pm_v, in_sem.at[4]),
        pltpu.make_async_copy(pv_hbm, pv_s, in_sem.at[5]),
        pltpu.make_async_copy(l2_hbm, l2_v, in_sem.at[6]),
    ]
    for load in loads:
        load.start()

    barrier = pltpu.get_barrier_semaphore()
    for d in range(1, 4):
        pl.semaphore_signal(barrier, inc=1, device_id=(cube ^ d, wide), device_id_type=MESH)

    @pl.loop(1, 16)
    def _(d):
        pl.semaphore_signal(barrier, inc=1, device_id=(cube, (wide + d) % 16), device_id_type=MESH)

    def one_hot(map_ref, live_ref, live_row, block):
        lanes = pl.multiple_of(block * B, B)
        entry = map_ref[:1, pl.ds(lanes, B)] - lanes
        live = live_ref[block, live_row] if live_ref is ll_s else live_ref[live_row, block]
        hit = (entry == iota((B, B), 0)) & (iota((B, B), 1) < live)
        return jnp.where(hit, 1.0, 0.0).astype(BF16)

    def map_quarter(values, row_hot, hots):
        top = values.astype(BF16)
        rest = (values - top.astype(F32)).astype(BF16)
        top = jnp.dot(row_hot, top, preferred_element_type=F32).astype(BF16)
        rest = jnp.dot(row_hot, rest, preferred_element_type=F32).astype(BF16)
        parts = []
        for i in range(4):
            both = jnp.concatenate((top[:, i * B : (i + 1) * B], rest[:, i * B : (i + 1) * B]), axis=0)
            got = lax.dot_general(both, hots[i], (((1,), (1,)), ((), ())), preferred_element_type=F32)
            parts.append(got[:B] + got[B:])
        return jnp.concatenate(parts, axis=1)

    loads[0].wait()
    loads[1].wait()
    lm_v[:1, :] = lm_v[pl.ds(cube - lm_base, 1), :]
    row_hot = one_hot(lm_v, ll_s, cube, wide)
    loads[2].wait()

    def leaf_quarter(at_quarter):
        hots = [one_hot(lm_v, ll_s, cube, at_quarter * 4 + i) for i in range(4)]
        values = x_v[:, pl.ds(pl.multiple_of(at_quarter * Q, Q), Q)]
        return map_quarter(values, row_hot, hots)

    def exchange1(n):
        return pltpu.make_async_remote_copy(
            src_ref=zs.at[n], dst_ref=zr.at[n], send_sem=e1_send.at[n], recv_sem=e1_recv.at[n],
            device_id=(cube ^ 1, wide), device_id_type=MESH,
        )

    for n in range(2):
        half = 1 - high if n == 0 else high
        zs[n] = leaf_quarter(2 * half + 1 - low)
        if n == 0:
            pl.semaphore_wait(barrier, 18)
        exchange1(n).start()
    for n in range(2):
        half = 1 - high if n == 0 else high
        zo[n] = leaf_quarter(2 * half + low)

    for n in range(3, 7):
        loads[n].wait()
    pm_v[:1, :] = pm_v[pl.ds(parent - pm_base, 1), :]
    up_row_hot = one_hot(pm_v, pv_s, parent, wide)

    def upper_quarter(n):
        half = 1 - high if n == 0 else high
        first = jnp.where(half == 0, l1_v[:, 0, 0, :], l1_v[:, 0, 1, :])
        values = first + zo[n] + zr[n]
        hots = [one_hot(pm_v, pv_s, parent, (2 * half + low) * 4 + i) for i in range(4)]
        return map_quarter(values, up_row_hot, hots)

    def exchange2(i):
        rows = pl.ds(pl.multiple_of(i * 32, 32), 32)
        return pltpu.make_async_remote_copy(
            src_ref=us.at[rows], dst_ref=ur.at[rows], send_sem=e2_send.at[i], recv_sem=e2_recv.at[i],
            device_id=(cube ^ 2, wide), device_id_type=MESH,
        )

    exchange1(0).wait_recv()
    us[...] = upper_quarter(0)
    exchange2(0).start()
    order = (2, 1, 3, 0)
    for o in order:
        chunk = (z_hi + o) % 4

        @pl.when(chunk != 0)
        def _():
            exchange2(chunk).start()

    exchange1(1).wait_recv()
    uk[...] = upper_quarter(1) + l2_v[:, 0, :]

    def finish_chunk(i):
        exchange2(i).wait_recv()
        rows = pl.ds(pl.multiple_of(i * 32, 32), 32)
        f2[rows, :] = uk[rows, :] + ur[rows, :]

    def rows_of(w):
        return pl.ds(pl.multiple_of(w * CYC, CYC), CYC)

    def spread(w):
        return pltpu.make_async_remote_copy(
            src_ref=f2.at[rows_of(w)], dst_ref=f2r.at[rows_of(wide)],
            send_sem=aa_send.at[w], recv_sem=aa_recv.at[wide],
            device_id=(cube, w), device_id_type=MESH,
        )

    def spread_from(w):
        return pltpu.make_async_remote_copy(
            src_ref=f2.at[rows_of(w)], dst_ref=f2r.at[rows_of(w)],
            send_sem=aa_send.at[w], recv_sem=aa_recv.at[w],
            device_id=(cube, w), device_id_type=MESH,
        )

    finish_chunk(0)

    def scatter(j):
        return pltpu.make_async_remote_copy(
            src_ref=f2.at[pl.ds(j * CYC, CYC)], dst_ref=at.at[rows_of(4 * z_hi + j)],
            send_sem=sc_send.at[j], recv_sem=sc_recv.at[0],
            device_id=(cube, 4 * z_hi + j), device_id_type=MESH,
        )

    def along_z(d):
        return pltpu.make_async_remote_copy(
            src_ref=at.at[rows_of(wide)], dst_ref=at.at[rows_of(wide)],
            send_sem=zg_send.at[d], recv_sem=pg_recv.at[wide],
            device_id=(cube, (wide + 4 * d) % 16), device_id_type=MESH,
        )

    def along_y(piece_z, d):
        piece = 4 * piece_z + y
        return pltpu.make_async_remote_copy(
            src_ref=at.at[rows_of(piece)], dst_ref=at.at[rows_of(piece)],
            send_sem=yg_send.at[piece_z, d], recv_sem=pg_recv.at[piece],
            device_id=(cube, 4 * z_hi + (y + d) % 4), device_id_type=MESH,
        )

    def piece_from(piece):
        return pltpu.make_async_remote_copy(
            src_ref=at.at[rows_of(piece)], dst_ref=at.at[rows_of(piece)],
            send_sem=zg_send.at[0], recv_sem=pg_recv.at[piece],
            device_id=(cube, piece), device_id_type=MESH,
        )

    @pl.when(y == 0)
    def _():
        for j in range(1, 4):
            scatter(j).start()
        at[rows_of(wide), :] = f2[:CYC, :]

    @pl.when(y != 0)
    def _():
        pltpu.make_async_remote_copy(
            src_ref=f2.at[pl.ds(0, CYC)], dst_ref=at.at[rows_of(wide)],
            send_sem=sc_send.at[0], recv_sem=sc_recv.at[0],
            device_id=(cube, 4 * z_hi), device_id_type=MESH,
        ).wait_recv()

    for d in (2, 1, 3):
        along_z(d).start()
    for d in (2, 1, 3):
        along_y(z_hi, d).start()

    for o in order:
        chunk = (z_hi + o) % 4

        @pl.when(chunk != 0)
        def _():
            finish_chunk(chunk)

        for k in range(4):
            w = 4 * chunk + k

            @pl.when(w != wide)
            def _():
                spread(w).start()

    f2r[rows_of(wide), :] = f2[rows_of(wide), :]

    for o in (1, 3, 2):
        piece_z = (z_hi + o) % 4
        piece_from(4 * piece_z + y).wait_recv()
        for d in (2, 1, 3):
            along_y(piece_z, d).start()

    @pl.loop(0, 16)
    def _(piece):
        @pl.when(piece % 4 != y)
        def _():
            piece_from(piece).wait_recv()

    lane = iota((B, B), 1)
    packed = at[:, :B]
    for i in range(4):
        shift = (PIV + CYC * i - CYC * wide + B) % B
        moved = pltpu.roll(at[:, i * B : (i + 1) * B], shift, 1)
        packed = jnp.where((lane >= PIV + CYC * i) & (lane < PIV + CYC * (i + 1)), moved, packed)
    msg[...] = jnp.where(lane[:64] < 64, packed[:64], pltpu.roll(packed[64:], 64, 1))

    def share(d):
        return pltpu.make_async_remote_copy(
            src_ref=msg, dst_ref=msgs.at[quarter], send_sem=cb_send.at[d], recv_sem=cb_recv.at[quarter],
            device_id=(cube ^ d, wide), device_id_type=MESH,
        )

    for d in range(1, 4):
        share(d).start()
    msgs[quarter] = msg[...]

    for d in range(1, 4):
        other = quarter ^ d
        pltpu.make_async_remote_copy(
            src_ref=msg, dst_ref=msgs.at[other], send_sem=cb_send.at[d], recv_sem=cb_recv.at[other],
            device_id=(group + other, wide), device_id_type=MESH,
        ).wait_recv()

    def unpack(first_lane):
        got = jnp.zeros((64, B), F32)
        for i in range(4):
            moved = pltpu.roll(msgs[i], (PIV * i - first_lane) % B, 1)
            got = jnp.where((lane[:64] >= PIV * i) & (lane[:64] < PIV * (i + 1)), moved, got)
        return got

    mat[:64, :B] = unpack(0)
    mat[64:, :B] = unpack(64)
    rows_t = jnp.concatenate((unpack(32), unpack(96)), axis=0)
    mat[:, B:] = jnp.where(iota((B, B), 0) == lane, 1.0, 0.0)

    @pl.loop(0, 4)
    def _(step):
        left = mat[:PIV, :B]
        right = mat[:PIV, B:]
        row_id = iota((PIV, 1), 0)
        diag = jnp.ones((PIV, 1), F32)
        for j in range(PIV):
            pivot = left[j : j + 1, j : j + 1]
            column = left[:, j : j + 1]
            diag = jnp.where(row_id == j, pivot, diag)
            factor = jnp.where(row_id > j, column * (1.0 / pivot), 0.0)
            left = left - factor * left[j : j + 1, :]
            right = right - factor * right[j : j + 1, :]
        scale = lax.rsqrt(diag)
        left = pltpu.roll(left * scale, B - PIV, 1)
        left = jnp.where(lane[:PIV] < B - PIV, left, 0.0)
        right = right * scale
        linv[pl.ds(pl.multiple_of(step * PIV, PIV), PIV), :] = right
        both = jnp.concatenate((left, right), axis=1)
        change = lax.dot_general(
            left, both, (((0,), (0,)), ((), ())), precision=HIGHEST, preferred_element_type=F32
        )
        trail_left = pltpu.roll(mat[PIV:, :B], B - PIV, 1)
        trail_right = mat[PIV:, B:]
        mat[: B - PIV, :B] = trail_left - change[: B - PIV, :B]
        mat[: B - PIV, B:] = trail_right - change[: B - PIV, B:]

    lower = linv[...]
    own_t = jnp.dot(lower, rows_t, precision=HIGHEST, preferred_element_type=F32)
    lt[...] = jnp.dot(lower, at[...], precision=HIGHEST, preferred_element_type=F32)
    tr_v[...] = lt[:, pl.ds(pl.multiple_of(wide // 4 * B, B), B)].T
    panel_v[0] = tr_v[pl.ds(pl.multiple_of(wide % 4 * PIV, PIV), PIV), :]
    panel_out = pltpu.make_async_copy(panel_v, panel_hbm, out_sem.at[0])
    panel_out.start()
    update = lax.dot_general(
        own_t, lt[...], (((0,), (0,)), ((), ())), precision=HIGHEST, preferred_element_type=F32
    )

    @pl.loop(0, 16)
    def _(w):
        @pl.when(w != wide)
        def _():
            spread_from(w).wait_recv()

    row = iota((B, Q), 0)
    inside = (row // CYC % 4 == 0) & (wide * CYC + row % CYC < PIV)
    dropped = inside | (iota((B, Q), 1) < PIV)
    out_v[:, 0, :] = jnp.where(dropped, 0.0, f2r[...] - update)
    schur_out = pltpu.make_async_copy(out_v, schur_hbm, out_sem.at[1])
    schur_out.start()

    for n in range(2):
        exchange1(n).wait_send()
    for i in range(4):
        exchange2(i).wait_send()

    @pl.when(y == 0)
    def _():
        for j in range(1, 4):
            scatter(j).wait_send()

    for d in range(1, 4):
        along_z(d).wait_send()
        share(d).wait_send()
        for piece_z in range(4):
            along_y(piece_z, d).wait_send()

    @pl.loop(0, 16)
    def _(w):
        @pl.when(w != wide)
        def _():
            spread(w).wait_send()

    panel_out.wait()
    schur_out.wait()


def on_device(updates, entries1, entries2, leaf_maps, leaf_live, parent_maps, parent_live):
    operands = (updates, entries1, entries2, leaf_maps, leaf_live.T, parent_maps, parent_live)
    dma = pltpu.SemaphoreType.DMA
    vmem = pltpu.VMEM
    return pl.pallas_call(
        kernel,
        out_shape=(
            jax.ShapeDtypeStruct((1, PIV, B), F32),
            jax.ShapeDtypeStruct((B, 1, Q), F32),
        ),
        in_specs=[pl.BlockSpec(memory_space=pl.ANY)] * 7,
        out_specs=(pl.BlockSpec(memory_space=pl.ANY),) * 2,
        scratch_shapes=[
            vmem((B, 4 * Q), F32), vmem((B, 1, 2, Q), F32), vmem((B, 1, Q), F32),
            vmem((8, 4 * Q), jnp.int32), vmem((8, 4 * Q), jnp.int32),
            pltpu.SMEM((16, 32), jnp.int32), pltpu.SMEM((16, 16), jnp.int32),
            vmem((2, B, Q), F32), vmem((2, B, Q), F32), vmem((2, B, Q), F32),
            vmem((B, Q), F32), vmem((B, Q), F32), vmem((B, Q), F32), vmem((B, Q), F32),
            vmem((B, Q), F32), vmem((B, Q), F32), vmem((B, Q), F32),
            vmem((64, B), F32), vmem((4, 64, B), F32), vmem((B, 2 * B), F32), vmem((B, B), F32),
            vmem((B, B), F32), vmem((B, 1, Q), F32), vmem((1, PIV, B), F32),
            dma((7,)), dma((2,)), dma((2,)), dma((4,)), dma((4,)), dma((16,)), dma((16,)),
            dma((4,)), dma((1,)), dma((4,)), dma((4, 4)), dma((16,)), dma((4,)), dma((4,)), dma((2,)),
        ],
        compiler_params=pltpu.CompilerParams(
            collective_id=0, has_side_effects=True, vmem_limit_bytes=60 * 1024 * 1024
        ),
        cost_estimate=pl.CostEstimate(flops=600_000_000, bytes_accessed=3_000_000, transcendentals=0),
    )(*operands)


def solution(mesh):
    placed = (
        P("cube", "wide", None),
        P("wide", "cube", None, None),
        P("wide", "cube", None),
        P(),
        P(),
        P(),
        P(),
    )
    return jax.shard_map(
        on_device,
        mesh=mesh,
        in_specs=placed,
        out_specs=(P("cube", "wide", None), P("wide", "cube", None)),
        check_vma=False,
    )
```

```python
import jax
import jax.numpy as jnp
from jax import lax
from jax.experimental import pallas as pl
from jax.experimental.pallas import tpu as pltpu
from jax.sharding import PartitionSpec as P

F32 = jnp.float32
BF16 = jnp.bfloat16
MESH = pl.DeviceIdType.MESH
HIGHEST = lax.Precision.HIGHEST
B = 128
Q = 512
PIV = 32
CYC = 8


def iota(shape, dim):
    return lax.broadcasted_iota(jnp.int32, shape, dim)


def kernel(
    x_hbm, l1_hbm, l2_hbm, lm_hbm, ll_hbm, pm_hbm, pv_hbm,
    panel_hbm, schur_hbm,
    x_v, l1_v, l2_v, lm_v, pm_v, ll_s, pv_s,
    zs, zo, zr, us, uk, ur, f2, f2r, at, lt, tiles, msgs, mat, linv, tr_v, out_v, panel_v,
    in_sem, e1_send, e1_recv, e2_send, e2_recv, aa_send, aa_recv,
    sc_send, sc_recv, zg_send, yg_send, pg_recv, cb_send, cb_recv,
    co_send, co_recv, cs_send, cs_recv, out_sem,
):
    cube = lax.axis_index("cube")
    wide = lax.axis_index("wide")
    low = cube % 2
    high = cube // 2 % 2
    quarter = cube % 4
    group = cube - quarter
    z_hi = wide // 4
    y = wide % 4
    parent = cube // 2
    lane = iota((B, B), 1)

    lm_base = pl.multiple_of(cube // 8 * 8, 8)
    pm_base = pl.multiple_of(parent // 8 * 8, 8)
    loads = [
        pltpu.make_async_copy(lm_hbm.at[pl.ds(lm_base, 8)], lm_v, in_sem.at[0]),
        pltpu.make_async_copy(ll_hbm, ll_s, in_sem.at[1]),
        pltpu.make_async_copy(x_hbm.at[0], x_v, in_sem.at[2]),
        pltpu.make_async_copy(l1_hbm, l1_v, in_sem.at[3]),
        pltpu.make_async_copy(pm_hbm.at[pl.ds(pm_base, 8)], pm_v, in_sem.at[4]),
        pltpu.make_async_copy(pv_hbm, pv_s, in_sem.at[5]),
        pltpu.make_async_copy(l2_hbm, l2_v, in_sem.at[6]),
    ]
    for load in loads:
        load.start()

    barrier = pltpu.get_barrier_semaphore()
    for d in range(1, 4):
        pl.semaphore_signal(barrier, inc=1, device_id=(cube ^ d, wide), device_id_type=MESH)

    @pl.loop(1, 16)
    def _(d):
        pl.semaphore_signal(barrier, inc=1, device_id=(cube, (wide + d) % 16), device_id_type=MESH)

    def one_hot(map_ref, live_ref, live_row, block):
        lanes = pl.multiple_of(block * B, B)
        entry = map_ref[:1, pl.ds(lanes, B)] - lanes
        live = live_ref[block, live_row] if live_ref is ll_s else live_ref[live_row, block]
        hit = (entry == iota((B, B), 0)) & (iota((B, B), 1) < live)
        return jnp.where(hit, 1.0, 0.0).astype(BF16)

    def map_quarter(values, row_hot, hots):
        top = values.astype(BF16)
        rest = (values - top.astype(F32)).astype(BF16)
        top = jnp.dot(row_hot, top, preferred_element_type=F32).astype(BF16)
        rest = jnp.dot(row_hot, rest, preferred_element_type=F32).astype(BF16)
        parts = []
        for i in range(4):
            both = jnp.concatenate((top[:, i * B : (i + 1) * B], rest[:, i * B : (i + 1) * B]), axis=0)
            got = lax.dot_general(both, hots[i], (((1,), (1,)), ((), ())), preferred_element_type=F32)
            parts.append(got[:B] + got[B:])
        return jnp.concatenate(parts, axis=1)

    loads[0].wait()
    loads[1].wait()
    lm_v[:1, :] = lm_v[pl.ds(cube - lm_base, 1), :]
    row_hot = one_hot(lm_v, ll_s, cube, wide)
    loads[2].wait()

    def leaf_quarter(at_quarter):
        hots = [one_hot(lm_v, ll_s, cube, at_quarter * 4 + i) for i in range(4)]
        values = x_v[:, pl.ds(pl.multiple_of(at_quarter * Q, Q), Q)]
        return map_quarter(values, row_hot, hots)

    def exchange1(n):
        return pltpu.make_async_remote_copy(
            src_ref=zs.at[n], dst_ref=zr.at[n], send_sem=e1_send.at[n], recv_sem=e1_recv.at[n],
            device_id=(cube ^ 1, wide), device_id_type=MESH,
        )

    for n in range(2):
        half = 1 - high if n == 0 else high
        zs[n] = leaf_quarter(2 * half + 1 - low)
        if n == 0:
            pl.semaphore_wait(barrier, 18)
        exchange1(n).start()
    for n in range(2):
        half = 1 - high if n == 0 else high
        zo[n] = leaf_quarter(2 * half + low)

    for n in range(3, 7):
        loads[n].wait()
    pm_v[:1, :] = pm_v[pl.ds(parent - pm_base, 1), :]
    up_row_hot = one_hot(pm_v, pv_s, parent, wide)

    def upper_quarter(n):
        half = 1 - high if n == 0 else high
        first = jnp.where(half == 0, l1_v[:, 0, 0, :], l1_v[:, 0, 1, :])
        values = first + zo[n] + zr[n]
        hots = [one_hot(pm_v, pv_s, parent, (2 * half + low) * 4 + i) for i in range(4)]
        return map_quarter(values, up_row_hot, hots)

    def exchange2(i):
        rows = pl.ds(pl.multiple_of(i * 32, 32), 32)
        return pltpu.make_async_remote_copy(
            src_ref=us.at[rows], dst_ref=ur.at[rows], send_sem=e2_send.at[i], recv_sem=e2_recv.at[i],
            device_id=(cube ^ 2, wide), device_id_type=MESH,
        )

    exchange1(0).wait_recv()
    us[...] = upper_quarter(0)
    exchange2(0).start()
    order = (2, 1, 3, 0)
    for o in order:
        chunk = (z_hi + o) % 4

        @pl.when(chunk != 0)
        def _():
            exchange2(chunk).start()

    exchange1(1).wait_recv()
    uk[...] = upper_quarter(1) + l2_v[:, 0, :]

    def finish_chunk(i):
        exchange2(i).wait_recv()
        rows = pl.ds(pl.multiple_of(i * 32, 32), 32)
        f2[rows, :] = uk[rows, :] + ur[rows, :]

    def rows_of(w):
        return pl.ds(pl.multiple_of(w * CYC, CYC), CYC)

    def spread(w):
        return pltpu.make_async_remote_copy(
            src_ref=f2.at[rows_of(w)], dst_ref=f2r.at[rows_of(wide)],
            send_sem=aa_send.at[w], recv_sem=aa_recv.at[wide],
            device_id=(cube, w), device_id_type=MESH,
        )

    def spread_from(w):
        return pltpu.make_async_remote_copy(
            src_ref=f2.at[rows_of(w)], dst_ref=f2r.at[rows_of(w)],
            send_sem=aa_send.at[w], recv_sem=aa_recv.at[w],
            device_id=(cube, w), device_id_type=MESH,
        )

    finish_chunk(0)

    def scatter(j):
        return pltpu.make_async_remote_copy(
            src_ref=f2.at[pl.ds(j * CYC, CYC)], dst_ref=at.at[rows_of(4 * z_hi + j)],
            send_sem=sc_send.at[j], recv_sem=sc_recv.at[0],
            device_id=(cube, 4 * z_hi + j), device_id_type=MESH,
        )

    def along_z(d):
        return pltpu.make_async_remote_copy(
            src_ref=at.at[rows_of(wide)], dst_ref=at.at[rows_of(wide)],
            send_sem=zg_send.at[d], recv_sem=pg_recv.at[wide],
            device_id=(cube, (wide + 4 * d) % 16), device_id_type=MESH,
        )

    def along_y(piece_z, d):
        piece = 4 * piece_z + y
        return pltpu.make_async_remote_copy(
            src_ref=at.at[rows_of(piece)], dst_ref=at.at[rows_of(piece)],
            send_sem=yg_send.at[piece_z, d], recv_sem=pg_recv.at[piece],
            device_id=(cube, 4 * z_hi + (y + d) % 4), device_id_type=MESH,
        )

    def piece_from(piece):
        return pltpu.make_async_remote_copy(
            src_ref=at.at[rows_of(piece)], dst_ref=at.at[rows_of(piece)],
            send_sem=zg_send.at[0], recv_sem=pg_recv.at[piece],
            device_id=(cube, piece), device_id_type=MESH,
        )

    def corner_to(w):
        return pltpu.make_async_remote_copy(
            src_ref=tiles.at[quarter, z_hi], dst_ref=tiles.at[quarter, z_hi],
            send_sem=co_send.at[w], recv_sem=co_recv.at[z_hi],
            device_id=(cube, w), device_id_type=MESH,
        )

    @pl.when(y == 0)
    def _():
        tile = f2[:CYC, :B]
        for r in range(1, 4):
            moved = pltpu.roll(f2[CYC * r : CYC * (r + 1), :B], PIV * r, 1)
            tile = jnp.where(lane[:CYC] >= PIV * r, moved, tile)
        tiles[quarter, z_hi] = tile

        @pl.loop(0, 15)
        def _(n):
            corner_to((wide + 8 + n + (n >= 8)) % 16).start()

        for j in range(1, 4):
            scatter(j).start()
        at[rows_of(wide), :] = f2[:CYC, :]

    @pl.when(y != 0)
    def _():
        pltpu.make_async_remote_copy(
            src_ref=f2.at[pl.ds(0, CYC)], dst_ref=at.at[rows_of(wide)],
            send_sem=sc_send.at[0], recv_sem=sc_recv.at[0],
            device_id=(cube, 4 * z_hi), device_id_type=MESH,
        ).wait_recv()

    for d in (2, 1, 3):
        along_z(d).start()
    for d in (2, 1, 3):
        along_y(z_hi, d).start()

    def share_corner(d):
        return pltpu.make_async_remote_copy(
            src_ref=tiles.at[quarter], dst_ref=tiles.at[quarter],
            send_sem=cs_send.at[d], recv_sem=cs_recv.at[quarter],
            device_id=(cube ^ d, wide), device_id_type=MESH,
        )

    def corner_from(q):
        return pltpu.make_async_remote_copy(
            src_ref=tiles.at[quarter, q], dst_ref=tiles.at[quarter, q],
            send_sem=co_send.at[0], recv_sem=co_recv.at[q],
            device_id=(cube, 4 * q), device_id_type=MESH,
        )

    for o in order:
        if o == 3:
            for q in range(4):

                @pl.when(wide != 4 * q)
                def _():
                    corner_from(q).wait_recv()

            for d in (2, 3, 1):
                share_corner(d).start()

        chunk = (z_hi + o) % 4

        @pl.when(chunk != 0)
        def _():
            finish_chunk(chunk)

        for k in range(4):
            w = 4 * chunk + k

            @pl.when(w != wide)
            def _():
                spread(w).start()

    f2r[rows_of(wide), :] = f2[rows_of(wide), :]

    for o in (1, 3, 2):
        piece_z = (z_hi + o) % 4
        piece_from(4 * piece_z + y).wait_recv()
        for d in (2, 1, 3):
            along_y(piece_z, d).start()

    for d in range(1, 4):
        other = quarter ^ d
        pltpu.make_async_remote_copy(
            src_ref=tiles.at[other], dst_ref=tiles.at[other],
            send_sem=cs_send.at[d], recv_sem=cs_recv.at[other],
            device_id=(group + other, wide), device_id_type=MESH,
        ).wait_recv()

    def gathered(parts, r):
        got = parts[0]
        if r:
            got = pltpu.roll(got, B - PIV * r, 1)
        for c in range(1, 4):
            moved = parts[c] if c == r else pltpu.roll(parts[c], PIV * (c - r) % B, 1)
            got = jnp.where(lane[:PIV] >= PIV * c, moved, got)
        return got

    corners = [tiles[c].reshape(PIV, B) for c in range(4)]
    for r in range(4):
        got = gathered(corners, r)
        for q in range(4):
            mat[PIV * q + CYC * r : PIV * q + CYC * (r + 1), :B] = got[CYC * q : CYC * (q + 1)]
    mat[:, B:] = jnp.where(iota((B, B), 0) == lane, 1.0, 0.0)

    def share(d):
        return pltpu.make_async_remote_copy(
            src_ref=msgs.at[quarter], dst_ref=msgs.at[quarter],
            send_sem=cb_send.at[d], recv_sem=cb_recv.at[quarter],
            device_id=(cube ^ d, wide), device_id_type=MESH,
        )

    @pl.loop(0, 4)
    def _(step):
        @pl.when(step == 2)
        def _():
            @pl.loop(0, 16)
            def _(piece):
                @pl.when(piece % 4 != y)
                def _():
                    piece_from(piece).wait_recv()

            packed = jnp.zeros((PIV, B), F32)
            for r in range(4):
                for i in range(4):
                    first = PIV * r + CYC * i
                    part = at[PIV * r : PIV * (r + 1), B * i : B * (i + 1)]
                    moved = pltpu.roll(part, (first + B - CYC * wide) % B, 1)
                    packed = jnp.where(lane[:PIV] >= first, moved, packed)
            msgs[quarter] = packed
            for d in (2, 3, 1):
                share(d).start()

        left = mat[:PIV, :B]
        right = mat[:PIV, B:]
        row_id = iota((PIV, B), 0)
        diag = jnp.ones((PIV, B), F32)
        for first in range(0, PIV, CYC):
            columns = [jnp.broadcast_to(left[:, first + n : first + n + 1], (PIV, B)) for n in range(CYC)]
            for n in range(CYC):
                j = first + n
                pivot = columns[n][j : j + 1, :]
                diag = jnp.where(row_id == j, pivot, diag)
                factor = jnp.where(row_id > j, columns[n] * (1.0 / pivot), 0.0)
                for m in range(n + 1, CYC):
                    columns[m] = columns[m] - factor * columns[m][j : j + 1, :]
                left = left - factor * left[j : j + 1, :]
                right = right - factor * right[j : j + 1, :]
        scale = lax.rsqrt(diag)
        right = right * scale
        linv[pl.ds(pl.multiple_of(step * PIV, PIV), PIV), :] = right

        @pl.when(step < 3)
        def _():
            moved = pltpu.roll(left * scale, B - PIV, 1)
            moved = jnp.where(lane[:PIV] < B - PIV, moved, 0.0)
            both = jnp.concatenate((moved, right), axis=1)
            change = lax.dot_general(
                moved, both, (((0,), (0,)), ((), ())), precision=HIGHEST, preferred_element_type=F32
            )
            trail_left = pltpu.roll(mat[PIV:, :B], B - PIV, 1)
            trail_right = mat[PIV:, B:]
            mat[: B - PIV, :B] = trail_left - change[: B - PIV, :B]
            mat[: B - PIV, B:] = trail_right - change[: B - PIV, B:]

    lower = linv[...]
    lt[...] = jnp.dot(lower, at[...], precision=HIGHEST, preferred_element_type=F32)
    tr_v[...] = lt[:, pl.ds(pl.multiple_of(wide // 4 * B, B), B)].T
    panel_hbm[0] = tr_v[pl.ds(pl.multiple_of(wide % 4 * PIV, PIV), PIV), :]
    for d in range(1, 4):
        other = quarter ^ d
        pltpu.make_async_remote_copy(
            src_ref=msgs.at[other], dst_ref=msgs.at[other],
            send_sem=cb_send.at[d], recv_sem=cb_recv.at[other],
            device_id=(group + other, wide), device_id_type=MESH,
        ).wait_recv()

    shared = [msgs[c] for c in range(4)]
    rows_t = jnp.concatenate([gathered(shared, r) for r in range(4)], axis=0)
    own_t = jnp.dot(lower, rows_t, precision=HIGHEST, preferred_element_type=F32)
    update = lax.dot_general(
        own_t, lt[...], (((0,), (0,)), ((), ())), precision=HIGHEST, preferred_element_type=F32
    )

    @pl.loop(0, 16)
    def _(w):
        @pl.when(w != wide)
        def _():
            spread_from(w).wait_recv()

    row = iota((B, Q), 0)
    inside = (row // CYC % 4 == 0) & (wide * CYC + row % CYC < PIV)
    dropped = inside | (iota((B, Q), 1) < PIV)
    schur_hbm[:, 0, :] = jnp.where(dropped, 0.0, f2r[...] - update)

    for n in range(2):
        exchange1(n).wait_send()
    for i in range(4):
        exchange2(i).wait_send()

    @pl.when(y == 0)
    def _():
        for j in range(1, 4):
            scatter(j).wait_send()

        @pl.loop(1, 16)
        def _(d):
            corner_to((wide + d) % 16).wait_send()

    for d in range(1, 4):
        along_z(d).wait_send()
        share(d).wait_send()
        share_corner(d).wait_send()
        for piece_z in range(4):
            along_y(piece_z, d).wait_send()

    @pl.loop(0, 16)
    def _(w):
        @pl.when(w != wide)
        def _():
            spread(w).wait_send()


def on_device(updates, entries1, entries2, leaf_maps, leaf_live, parent_maps, parent_live):
    operands = (updates, entries1, entries2, leaf_maps, leaf_live.T, parent_maps, parent_live)
    operands = tuple(pltpu.with_memory_space_constraint(o, pltpu.HBM) for o in operands)
    dma = pltpu.SemaphoreType.DMA
    vmem = pltpu.VMEM
    return pl.pallas_call(
        kernel,
        out_shape=(
            jax.ShapeDtypeStruct((1, PIV, B), F32),
            jax.ShapeDtypeStruct((B, 1, Q), F32),
        ),
        in_specs=[pl.BlockSpec(memory_space=pltpu.HBM)] * 7,
        out_specs=(pl.BlockSpec(memory_space=pltpu.VMEM),) * 2,
        scratch_shapes=[
            vmem((B, 4 * Q), F32), vmem((B, 1, 2, Q), F32), vmem((B, 1, Q), F32),
            vmem((8, 4 * Q), jnp.int32), vmem((8, 4 * Q), jnp.int32),
            pltpu.SMEM((16, 32), jnp.int32), pltpu.SMEM((16, 16), jnp.int32),
            vmem((2, B, Q), F32), vmem((2, B, Q), F32), vmem((2, B, Q), F32),
            vmem((B, Q), F32), vmem((B, Q), F32), vmem((B, Q), F32), vmem((B, Q), F32),
            vmem((B, Q), F32), vmem((B, Q), F32), vmem((B, Q), F32),
            vmem((4, 4, CYC, B), F32), vmem((4, PIV, B), F32), vmem((B, 2 * B), F32), vmem((B, B), F32),
            vmem((B, B), F32), vmem((B, 1, Q), F32), vmem((1, PIV, B), F32),
            dma((7,)), dma((2,)), dma((2,)), dma((4,)), dma((4,)), dma((16,)), dma((16,)),
            dma((4,)), dma((1,)), dma((4,)), dma((4, 4)), dma((16,)), dma((4,)), dma((4,)),
            dma((16,)), dma((4,)), dma((4,)), dma((4,)), dma((2,)),
        ],
        compiler_params=pltpu.CompilerParams(
            collective_id=0, has_side_effects=True, vmem_limit_bytes=16 * 1024 * 1024
        ),
        cost_estimate=pl.CostEstimate(flops=600_000_000, bytes_accessed=3_000_000, transcendentals=0),
    )(*operands)


def solution(mesh):
    placed = (
        P("cube", "wide", None),
        P("wide", "cube", None, None),
        P("wide", "cube", None),
        P(),
        P(),
        P(),
        P(),
    )
    return jax.shard_map(
        on_device,
        mesh=mesh,
        in_specs=placed,
        out_specs=(P("cube", "wide", None), P("wide", "cube", None)),
        check_vma=False,
    )
```

```python
import jax
import jax.numpy as jnp
from jax import lax
from jax.experimental import pallas as pl
from jax.experimental.pallas import tpu as pltpu
from jax.sharding import PartitionSpec as P

F32 = jnp.float32
BF16 = jnp.bfloat16
MESH = pl.DeviceIdType.MESH
HIGHEST = lax.Precision.HIGHEST
B = 128
Q = 512
PIV = 32
CYC = 8


def iota(shape, dim):
    return lax.broadcasted_iota(jnp.int32, shape, dim)


def kernel(
    x_hbm, l1_hbm, l2_hbm, lm_hbm, ll_hbm, pm_hbm, pv_hbm,
    panel_hbm, schur_hbm,
    x_v, l1_v, l2_v, lm_v, pm_v, ll_s, pv_s,
    zs, zo, zr, us, uk, ur, f2, f2r, tt, at, lt, cr, terms, tiles, msgs, mat, linv, tr_v,
    in_sem, e1_send, e1_recv, e2_send, e2_recv, aa_send, aa_recv, ac_send,
    cr_send, cr_recv, pa_send, pb_send, pa_recv, zg_send, yg_send, pg_recv, cb_send, cb_recv,
    co_send, co_recv, cs_send, cs_recv,
):
    cube = lax.axis_index("cube")
    wide = lax.axis_index("wide")
    low = cube % 2
    high = cube // 2 % 2
    quarter = cube % 4
    group = cube - quarter
    z_hi = wide // 4
    y = wide % 4
    parent = cube // 2
    lane = iota((B, B), 1)

    def ring(a, b):
        m = (a - b + 4) % 4
        return m - m // 3 * 2

    def by_rows(part, home, at_z):
        return ring(part, at_z) <= ring(home, at_z)

    lm_base = pl.multiple_of(cube // 8 * 8, 8)
    pm_base = pl.multiple_of(parent // 8 * 8, 8)
    loads = [
        pltpu.make_async_copy(lm_hbm.at[pl.ds(lm_base, 8)], lm_v, in_sem.at[0]),
        pltpu.make_async_copy(ll_hbm, ll_s, in_sem.at[1]),
        pltpu.make_async_copy(x_hbm.at[0], x_v, in_sem.at[2]),
        pltpu.make_async_copy(l1_hbm, l1_v, in_sem.at[3]),
        pltpu.make_async_copy(pm_hbm.at[pl.ds(pm_base, 8)], pm_v, in_sem.at[4]),
        pltpu.make_async_copy(pv_hbm, pv_s, in_sem.at[5]),
        pltpu.make_async_copy(l2_hbm, l2_v, in_sem.at[6]),
    ]
    for load in loads:
        load.start()

    barrier = pltpu.get_barrier_semaphore()

    def greet(c, w):
        pl.semaphore_signal(barrier, inc=1, device_id=(c, w), device_id_type=MESH)

    @pl.loop(0, 15)
    def _(n):
        greet(cube, (wide + 8 + n + n // 8) % 16)

    for part in range(4):

        @pl.when(jnp.logical_not(by_rows(part, quarter, z_hi)))
        def _():
            for k in range(4):
                greet(group + part, 4 * quarter + k)

    greet(cube ^ 2, 4 * z_hi)
    for d in (2, 3, 1):
        greet(cube ^ d, wide)
    apart = ring(z_hi, quarter)
    greetings = 18 + 4 * (apart % 2 * 2 + apart // 2) + 4 * (1 - (y + 3) // 4)

    def one_hot(map_ref, live_ref, live_row, block):
        lanes = pl.multiple_of(block * B, B)
        entry = map_ref[:1, pl.ds(lanes, B)] - lanes
        live = live_ref[block, live_row] if live_ref is ll_s else live_ref[live_row, block]
        hit = (entry == iota((B, B), 0)) & (iota((B, B), 1) < live)
        return jnp.where(hit, 1.0, 0.0).astype(BF16)

    def map_quarter(values, row_hot, hots):
        top = values.astype(BF16)
        rest = (values - top.astype(F32)).astype(BF16)
        top = jnp.dot(row_hot, top, preferred_element_type=F32).astype(BF16)
        rest = jnp.dot(row_hot, rest, preferred_element_type=F32).astype(BF16)
        parts = []
        for i in range(4):
            both = jnp.concatenate((top[:, i * B : (i + 1) * B], rest[:, i * B : (i + 1) * B]), axis=0)
            got = lax.dot_general(both, hots[i], (((1,), (1,)), ((), ())), preferred_element_type=F32)
            parts.append(got[:B] + got[B:])
        return jnp.concatenate(parts, axis=1)

    loads[0].wait()
    loads[1].wait()
    lm_v[:1, :] = lm_v[pl.ds(cube - lm_base, 1), :]
    row_hot = one_hot(lm_v, ll_s, cube, wide)
    loads[2].wait()

    def leaf_quarter(at_quarter):
        hots = [one_hot(lm_v, ll_s, cube, at_quarter * 4 + i) for i in range(4)]
        values = x_v[:, pl.ds(pl.multiple_of(at_quarter * Q, Q), Q)]
        return map_quarter(values, row_hot, hots)

    def exchange1(n):
        return pltpu.make_async_remote_copy(
            src_ref=zs.at[n], dst_ref=zr.at[n], send_sem=e1_send.at[n], recv_sem=e1_recv.at[n],
            device_id=(cube ^ 1, wide), device_id_type=MESH,
        )

    for n in range(2):
        half = 1 - high if n == 0 else high
        zs[n] = leaf_quarter(2 * half + 1 - low)
        if n == 0:
            pl.semaphore_wait(barrier, greetings)
        exchange1(n).start()
    for n in range(2):
        half = 1 - high if n == 0 else high
        zo[n] = leaf_quarter(2 * half + low)

    for n in range(3, 7):
        loads[n].wait()
    pm_v[:1, :] = pm_v[pl.ds(parent - pm_base, 1), :]
    up_row_hot = one_hot(pm_v, pv_s, parent, wide)

    def upper_quarter(n):
        half = 1 - high if n == 0 else high
        first = jnp.where(half == 0, l1_v[:, 0, 0, :], l1_v[:, 0, 1, :])
        values = first + zo[n] + zr[n]
        hots = [one_hot(pm_v, pv_s, parent, (2 * half + low) * 4 + i) for i in range(4)]
        return map_quarter(values, up_row_hot, hots)

    def exchange2(i):
        rows = pl.ds(pl.multiple_of(i * 32, 32), 32)
        return pltpu.make_async_remote_copy(
            src_ref=us.at[rows], dst_ref=ur.at[rows], send_sem=e2_send.at[i], recv_sem=e2_recv.at[i],
            device_id=(cube ^ 2, wide), device_id_type=MESH,
        )

    exchange1(0).wait_recv()
    us[...] = upper_quarter(0)
    def rows_of(w):
        return pl.ds(pl.multiple_of(w * CYC, CYC), CYC)

    def corner_term():
        return pltpu.make_async_remote_copy(
            src_ref=us.at[pl.ds(0, PIV), pl.ds(0, B)], dst_ref=cr, send_sem=cr_send, recv_sem=cr_recv,
            device_id=(cube ^ 2, wide), device_id_type=MESH,
        )

    def pivot_term(j):
        return pltpu.make_async_remote_copy(
            src_ref=us.at[pl.ds(j * CYC, CYC)], dst_ref=terms.at[0], send_sem=pa_send.at[j], recv_sem=pa_recv.at[0],
            device_id=(cube ^ 2, 4 * z_hi + j), device_id_type=MESH,
        )

    def own_term(j):
        return pltpu.make_async_remote_copy(
            src_ref=uk.at[pl.ds(j * CYC, CYC)], dst_ref=terms.at[1], send_sem=pb_send.at[j], recv_sem=pa_recv.at[1],
            device_id=(cube, 4 * z_hi + j), device_id_type=MESH,
        )

    @pl.when(y == 0)
    def _():
        corner_term().start()
        for j in (2, 1, 3, 0):
            pivot_term(j).start()

    order = (2, 1, 3, 0)
    for o in order:
        exchange2((z_hi + o) % 4).start()

    exchange1(1).wait_recv()
    uk[...] = upper_quarter(1) + l2_v[:, 0, :]

    def corner_to(w):
        return pltpu.make_async_remote_copy(
            src_ref=tiles.at[quarter, z_hi], dst_ref=tiles.at[quarter, z_hi],
            send_sem=co_send.at[w], recv_sem=co_recv.at[z_hi],
            device_id=(cube, w), device_id_type=MESH,
        )

    def along_z(d):
        return pltpu.make_async_remote_copy(
            src_ref=at.at[rows_of(wide)], dst_ref=at.at[rows_of(wide)],
            send_sem=zg_send.at[d], recv_sem=pg_recv.at[wide],
            device_id=(cube, (wide + 4 * d) % 16), device_id_type=MESH,
        )

    def along_y(piece_z, d):
        piece = 4 * piece_z + y
        return pltpu.make_async_remote_copy(
            src_ref=at.at[rows_of(piece)], dst_ref=at.at[rows_of(piece)],
            send_sem=yg_send.at[piece_z, d], recv_sem=pg_recv.at[piece],
            device_id=(cube, 4 * z_hi + (y + d) % 4), device_id_type=MESH,
        )

    def piece_from(piece):
        return pltpu.make_async_remote_copy(
            src_ref=at.at[rows_of(piece)], dst_ref=at.at[rows_of(piece)],
            send_sem=zg_send.at[0], recv_sem=pg_recv.at[piece],
            device_id=(cube, piece), device_id_type=MESH,
        )

    def term_from(n):
        return pltpu.make_async_remote_copy(
            src_ref=us.at[pl.ds(0, CYC)], dst_ref=terms.at[n], send_sem=pa_send.at[0], recv_sem=pa_recv.at[n],
            device_id=(cube ^ 2, 4 * z_hi), device_id_type=MESH,
        )

    @pl.when(y == 0)
    def _():
        for j in (2, 1, 3):
            own_term(j).start()
        corner_term().wait_recv()
        block = uk[:PIV, :B] + cr[...]
        tile = block[:CYC]
        for r in range(1, 4):
            moved = pltpu.roll(block[CYC * r : CYC * (r + 1)], PIV * r, 1)
            tile = jnp.where(lane[:CYC] >= PIV * r, moved, tile)
        tiles[quarter, z_hi] = tile

        @pl.loop(0, 15)
        def _(n):
            corner_to((wide + 8 + n + n // 8) % 16).start()

        term_from(0).wait_recv()
        at[rows_of(wide), :] = terms[0] + uk[:CYC, :]

    @pl.when(y != 0)
    def _():
        term_from(0).wait_recv()
        term_from(1).wait_recv()
        at[rows_of(wide), :] = terms[0] + terms[1]

    for d in (2, 1, 3):
        along_z(d).start()
    for d in (2, 1, 3):
        along_y(z_hi, d).start()

    def share_corner(d):
        return pltpu.make_async_remote_copy(
            src_ref=tiles.at[quarter], dst_ref=tiles.at[quarter],
            send_sem=cs_send.at[d], recv_sem=cs_recv.at[quarter],
            device_id=(cube ^ d, wide), device_id_type=MESH,
        )

    def corner_from(q):
        return pltpu.make_async_remote_copy(
            src_ref=tiles.at[quarter, q], dst_ref=tiles.at[quarter, q],
            send_sem=co_send.at[0], recv_sem=co_recv.at[q],
            device_id=(cube, 4 * q), device_id_type=MESH,
        )

    def spread_rows(w):
        return pltpu.make_async_remote_copy(
            src_ref=f2.at[rows_of(w)], dst_ref=f2r.at[z_hi, y],
            send_sem=aa_send.at[w], recv_sem=aa_recv.at[wide],
            device_id=(cube, w), device_id_type=MESH,
        )

    def spread_columns(w):
        return pltpu.make_async_remote_copy(
            src_ref=tt.at[:, w], dst_ref=f2r.at[quarter, :, :, pl.ds(pl.multiple_of(y * B, B), B)],
            send_sem=ac_send.at[w], recv_sem=aa_recv.at[4 * quarter + y],
            device_id=(group + z_hi, w), device_id_type=MESH,
        )

    def rows_from(part, k):
        return pltpu.make_async_remote_copy(
            src_ref=f2.at[rows_of(0)], dst_ref=f2r.at[part, k],
            send_sem=aa_send.at[0], recv_sem=aa_recv.at[4 * part + k],
            device_id=(cube, 4 * part + k), device_id_type=MESH,
        )

    def columns_from(part, k):
        return pltpu.make_async_remote_copy(
            src_ref=tt.at[:, 0], dst_ref=f2r.at[part, :, :, pl.ds(k * B, B)],
            send_sem=ac_send.at[0], recv_sem=aa_recv.at[4 * part + k],
            device_id=(group + part, 4 * quarter + k), device_id_type=MESH,
        )

    for o in order:
        chunk = (z_hi + o) % 4
        exchange2(chunk).wait_recv()
        rows = pl.ds(pl.multiple_of(chunk * 32, 32), 32)
        f2[rows, :] = uk[rows, :] + ur[rows, :]

        @pl.when(by_rows(z_hi, quarter, chunk))
        def _():
            for k in range(4):
                w = 4 * chunk + k

                @pl.when(w != wide)
                def _():
                    spread_rows(w).start()

    f2r[z_hi, y] = f2[rows_of(wide), :]

    @pl.when(z_hi != quarter)
    def _():
        for i in range(4):
            tt[i] = f2[:, i * B : (i + 1) * B].T.reshape(16, CYC, B)
        for o in (1, 3, 0):
            chunk = (z_hi + o) % 4

            @pl.when(ring(z_hi, chunk) < ring(quarter, chunk))
            def _():
                for k in range(4):
                    spread_columns(4 * chunk + k).start()

    def share_corner(d):
        return pltpu.make_async_remote_copy(
            src_ref=tiles.at[quarter], dst_ref=tiles.at[quarter],
            send_sem=cs_send.at[d], recv_sem=cs_recv.at[quarter],
            device_id=(cube ^ d, wide), device_id_type=MESH,
        )

    def corner_from(q):
        return pltpu.make_async_remote_copy(
            src_ref=tiles.at[quarter, q], dst_ref=tiles.at[quarter, q],
            send_sem=co_send.at[0], recv_sem=co_recv.at[q],
            device_id=(cube, 4 * q), device_id_type=MESH,
        )

    for q in range(4):

        @pl.when(wide != 4 * q)
        def _():
            corner_from(q).wait_recv()

    for d in (2, 3, 1):
        share_corner(d).start()

    for o in (1, 3, 2):
        piece_z = (z_hi + o) % 4
        piece_from(4 * piece_z + y).wait_recv()
        for d in (2, 1, 3):
            along_y(piece_z, d).start()

    for d in range(1, 4):
        other = quarter ^ d
        pltpu.make_async_remote_copy(
            src_ref=tiles.at[other], dst_ref=tiles.at[other],
            send_sem=cs_send.at[d], recv_sem=cs_recv.at[other],
            device_id=(group + other, wide), device_id_type=MESH,
        ).wait_recv()

    def gathered(parts, r):
        got = parts[0]
        if r:
            got = pltpu.roll(got, B - PIV * r, 1)
        for c in range(1, 4):
            moved = parts[c] if c == r else pltpu.roll(parts[c], PIV * (c - r) % B, 1)
            got = jnp.where(lane[:PIV] >= PIV * c, moved, got)
        return got

    corners = [tiles[c].reshape(PIV, B) for c in range(4)]
    for r in range(4):
        got = gathered(corners, r)
        for q in range(4):
            mat[PIV * q + CYC * r : PIV * q + CYC * (r + 1), :B] = got[CYC * q : CYC * (q + 1)]
    mat[:, B:] = jnp.where(iota((B, B), 0) == lane, 1.0, 0.0)

    def share(d):
        return pltpu.make_async_remote_copy(
            src_ref=msgs.at[quarter], dst_ref=msgs.at[quarter],
            send_sem=cb_send.at[d], recv_sem=cb_recv.at[quarter],
            device_id=(cube ^ d, wide), device_id_type=MESH,
        )

    @pl.loop(0, 4)
    def _(step):
        @pl.when(step == 2)
        def _():
            @pl.loop(0, 16)
            def _(piece):
                @pl.when(piece % 4 != y)
                def _():
                    piece_from(piece).wait_recv()

            packed = jnp.zeros((PIV, B), F32)
            for r in range(4):
                for i in range(4):
                    first = PIV * r + CYC * i
                    part = at[PIV * r : PIV * (r + 1), B * i : B * (i + 1)]
                    moved = pltpu.roll(part, (first + B - CYC * wide) % B, 1)
                    packed = jnp.where(lane[:PIV] >= first, moved, packed)
            msgs[quarter] = packed
            for d in (2, 3, 1):
                share(d).start()

        left = mat[:PIV, :B]
        right = mat[:PIV, B:]
        row_id = iota((PIV, B), 0)
        diag = jnp.ones((PIV, B), F32)
        for first in range(0, PIV, CYC):
            columns = [jnp.broadcast_to(left[:, first + n : first + n + 1], (PIV, B)) for n in range(CYC)]
            for n in range(CYC):
                j = first + n
                pivot = columns[n][j : j + 1, :]
                diag = jnp.where(row_id == j, pivot, diag)
                factor = jnp.where(row_id > j, columns[n] * (1.0 / pivot), 0.0)
                for m in range(n + 1, CYC):
                    columns[m] = columns[m] - factor * columns[m][j : j + 1, :]
                left = left - factor * left[j : j + 1, :]
                right = right - factor * right[j : j + 1, :]
        scale = lax.rsqrt(diag)
        right = right * scale
        linv[pl.ds(pl.multiple_of(step * PIV, PIV), PIV), :] = right

        @pl.when(step < 3)
        def _():
            moved = pltpu.roll(left * scale, B - PIV, 1)
            moved = jnp.where(lane[:PIV] < B - PIV, moved, 0.0)
            both = jnp.concatenate((moved, right), axis=1)
            change = lax.dot_general(
                moved, both, (((0,), (0,)), ((), ())), precision=HIGHEST, preferred_element_type=F32
            )
            trail_left = pltpu.roll(mat[PIV:, :B], B - PIV, 1)
            trail_right = mat[PIV:, B:]
            mat[: B - PIV, :B] = trail_left - change[: B - PIV, :B]
            mat[: B - PIV, B:] = trail_right - change[: B - PIV, B:]

    lower = linv[...]
    lt[...] = jnp.dot(lower, at[...], precision=HIGHEST, preferred_element_type=F32)
    tr_v[...] = lt[:, pl.ds(pl.multiple_of(wide // 4 * B, B), B)].T
    panel_hbm[0] = tr_v[pl.ds(pl.multiple_of(wide % 4 * PIV, PIV), PIV), :]
    for d in range(1, 4):
        other = quarter ^ d
        pltpu.make_async_remote_copy(
            src_ref=msgs.at[other], dst_ref=msgs.at[other],
            send_sem=cb_send.at[d], recv_sem=cb_recv.at[other],
            device_id=(group + other, wide), device_id_type=MESH,
        ).wait_recv()

    shared = [msgs[c] for c in range(4)]
    rows_t = jnp.concatenate([gathered(shared, r) for r in range(4)], axis=0)
    own_t = jnp.dot(lower, rows_t, precision=HIGHEST, preferred_element_type=F32)
    update = lax.dot_general(
        own_t, lt[...], (((0,), (0,)), ((), ())), precision=HIGHEST, preferred_element_type=F32
    )

    for part in range(4):
        as_rows = by_rows(part, quarter, z_hi)
        for k in range(4):

            @pl.when(as_rows & (wide != 4 * part + k))
            def _():
                rows_from(part, k).wait_recv()

            @pl.when(jnp.logical_not(as_rows))
            def _():
                columns_from(part, k).wait_recv()

    row = iota((B, Q), 0)
    inside = (row // CYC % 4 == 0) & (wide * CYC + row % CYC < PIV)
    dropped = inside | (iota((B, Q), 1) < PIV)
    schur_hbm[:, 0, :] = jnp.where(dropped, 0.0, f2r[...].reshape(B, Q) - update)

    for n in range(2):
        exchange1(n).wait_send()
    for i in range(4):
        exchange2(i).wait_send()

    @pl.when(y == 0)
    def _():
        corner_term().wait_send()
        for j in range(4):
            pivot_term(j).wait_send()
        for j in range(1, 4):
            own_term(j).wait_send()

        @pl.loop(1, 16)
        def _(d):
            corner_to((wide + d) % 16).wait_send()

    for d in range(1, 4):
        along_z(d).wait_send()
        share(d).wait_send()
        share_corner(d).wait_send()
        for piece_z in range(4):
            along_y(piece_z, d).wait_send()

    for o in range(4):
        chunk = (z_hi + o) % 4

        @pl.when(by_rows(z_hi, quarter, chunk))
        def _():
            for k in range(4):
                w = 4 * chunk + k

                @pl.when(w != wide)
                def _():
                    spread_rows(w).wait_send()

        @pl.when(ring(z_hi, chunk) < ring(quarter, chunk))
        def _():
            for k in range(4):
                spread_columns(4 * chunk + k).wait_send()


def on_device(updates, entries1, entries2, leaf_maps, leaf_live, parent_maps, parent_live):
    operands = (updates, entries1, entries2, leaf_maps, leaf_live.T, parent_maps, parent_live)
    operands = tuple(pltpu.with_memory_space_constraint(o, pltpu.HBM) for o in operands)
    dma = pltpu.SemaphoreType.DMA
    vmem = pltpu.VMEM
    return pl.pallas_call(
        kernel,
        out_shape=(
            jax.ShapeDtypeStruct((1, PIV, B), F32),
            jax.ShapeDtypeStruct((B, 1, Q), F32),
        ),
        in_specs=[pl.BlockSpec(memory_space=pltpu.HBM)] * 7,
        out_specs=(pl.BlockSpec(memory_space=pltpu.VMEM),) * 2,
        scratch_shapes=[
            vmem((B, 4 * Q), F32), vmem((B, 1, 2, Q), F32), vmem((B, 1, Q), F32),
            vmem((8, 4 * Q), jnp.int32), vmem((8, 4 * Q), jnp.int32),
            pltpu.SMEM((16, 32), jnp.int32), pltpu.SMEM((16, 16), jnp.int32),
            vmem((2, B, Q), F32), vmem((2, B, Q), F32), vmem((2, B, Q), F32),
            vmem((B, Q), F32), vmem((B, Q), F32), vmem((B, Q), F32), vmem((B, Q), F32),
            vmem((4, 4, CYC, Q), F32), vmem((4, 16, CYC, B), F32), vmem((B, Q), F32), vmem((B, Q), F32),
            vmem((PIV, B), F32), vmem((2, CYC, Q), F32),
            vmem((4, 4, CYC, B), F32), vmem((4, PIV, B), F32), vmem((B, 2 * B), F32), vmem((B, B), F32),
            vmem((B, B), F32),
            dma((7,)), dma((2,)), dma((2,)), dma((4,)), dma((4,)), dma((16,)), dma((16,)), dma((16,)),
            dma, dma, dma((4,)), dma((4,)), dma((2,)), dma((4,)), dma((4, 4)), dma((16,)), dma((4,)), dma((4,)),
            dma((16,)), dma((4,)), dma((4,)), dma((4,)),
        ],
        compiler_params=pltpu.CompilerParams(
            collective_id=0, has_side_effects=True, vmem_limit_bytes=16 * 1024 * 1024
        ),
        cost_estimate=pl.CostEstimate(flops=600_000_000, bytes_accessed=3_000_000, transcendentals=0),
    )(*operands)


def solution(mesh):
    placed = (
        P("cube", "wide", None),
        P("wide", "cube", None, None),
        P("wide", "cube", None),
        P(),
        P(),
        P(),
        P(),
    )
    return jax.shard_map(
        on_device,
        mesh=mesh,
        in_specs=placed,
        out_specs=(P("cube", "wide", None), P("wide", "cube", None)),
        check_vma=False,
    )
```

```python
import jax
import jax.numpy as jnp
from jax import lax
from jax.experimental import pallas as pl
from jax.experimental.pallas import tpu as pltpu
from jax.sharding import PartitionSpec as P

F32 = jnp.float32
BF16 = jnp.bfloat16
MESH = pl.DeviceIdType.MESH
HIGHEST = lax.Precision.HIGHEST
B = 128
Q = 512
PIV = 32
CYC = 8


def iota(shape, dim):
    return lax.broadcasted_iota(jnp.int32, shape, dim)


def kernel(
    x_hbm, l1_hbm, l2_hbm, lm_hbm, ll_hbm, pm_hbm, pv_hbm,
    panel_hbm, schur_hbm,
    x_v, l1_v, l2_v, lm_v, pm_v, ll_s, pv_s,
    zs, zo, zr, us, uk, ur, f2, f2r, tt, at, lt, cr, terms, tiles, msgs, mat, linv, tr_v,
    in_sem, e1_send, e1_recv, e2_send, e2_recv, aa_send, aa_recv, ac_send,
    cr_send, cr_recv, pa_send, pb_send, pa_recv, zg_send, yg_send, pg_recv, cb_send, cb_recv,
    co_send, co_recv, cs_send, cs_recv,
):
    cube = lax.axis_index("cube")
    wide = lax.axis_index("wide")
    low = cube % 2
    high = cube // 2 % 2
    quarter = cube % 4
    group = cube - quarter
    z_hi = wide // 4
    y = wide % 4
    parent = cube // 2
    lane = iota((B, B), 1)

    def ring(a, b):
        m = (a - b + 4) % 4
        return m - m // 3 * 2

    def by_rows(part, home, at_z):
        return ring(part, at_z) <= ring(home, at_z)

    lm_base = pl.multiple_of(cube // 8 * 8, 8)
    pm_base = pl.multiple_of(parent // 8 * 8, 8)
    loads = [
        pltpu.make_async_copy(lm_hbm.at[pl.ds(lm_base, 8)], lm_v, in_sem.at[0]),
        pltpu.make_async_copy(ll_hbm, ll_s, in_sem.at[1]),
        pltpu.make_async_copy(x_hbm.at[0], x_v, in_sem.at[2]),
        pltpu.make_async_copy(l1_hbm, l1_v, in_sem.at[3]),
        pltpu.make_async_copy(pm_hbm.at[pl.ds(pm_base, 8)], pm_v, in_sem.at[4]),
        pltpu.make_async_copy(pv_hbm, pv_s, in_sem.at[5]),
        pltpu.make_async_copy(l2_hbm, l2_v, in_sem.at[6]),
    ]
    for load in loads:
        load.start()

    barrier = pltpu.get_barrier_semaphore()

    def greet(c, w):
        pl.semaphore_signal(barrier, inc=1, device_id=(c, w), device_id_type=MESH)

    @pl.loop(0, 15)
    def _(n):
        greet(cube, (wide + 8 + n + n // 8) % 16)

    for part in range(4):

        @pl.when(jnp.logical_not(by_rows(part, quarter, z_hi)))
        def _():
            for k in range(4):
                greet(group + part, 4 * quarter + k)

    greet(cube ^ 2, 4 * z_hi)
    for d in (2, 3, 1):
        greet(cube ^ d, wide)
    apart = ring(z_hi, quarter)
    greetings = 18 + 4 * (apart % 2 * 2 + apart // 2) + 4 * (1 - (y + 3) // 4)

    def one_hot(map_ref, live_ref, live_row, block):
        lanes = pl.multiple_of(block * B, B)
        entry = map_ref[:1, pl.ds(lanes, B)] - lanes
        live = live_ref[block, live_row] if live_ref is ll_s else live_ref[live_row, block]
        hit = (entry == iota((B, B), 0)) & (iota((B, B), 1) < live)
        return jnp.where(hit, 1.0, 0.0).astype(BF16)

    def map_quarter(values, row_hot, hots):
        top = values.astype(BF16)
        rest = (values - top.astype(F32)).astype(BF16)
        top = jnp.dot(row_hot, top, preferred_element_type=F32).astype(BF16)
        rest = jnp.dot(row_hot, rest, preferred_element_type=F32).astype(BF16)
        parts = []
        for i in range(4):
            both = jnp.concatenate((top[:, i * B : (i + 1) * B], rest[:, i * B : (i + 1) * B]), axis=0)
            got = lax.dot_general(both, hots[i], (((1,), (1,)), ((), ())), preferred_element_type=F32)
            parts.append(got[:B] + got[B:])
        return jnp.concatenate(parts, axis=1)

    loads[0].wait()
    loads[1].wait()
    lm_v[:1, :] = lm_v[pl.ds(cube - lm_base, 1), :]
    row_hot = one_hot(lm_v, ll_s, cube, wide)
    loads[2].wait()

    def leaf_quarter(at_quarter):
        hots = [one_hot(lm_v, ll_s, cube, at_quarter * 4 + i) for i in range(4)]
        values = x_v[:, pl.ds(pl.multiple_of(at_quarter * Q, Q), Q)]
        return map_quarter(values, row_hot, hots)

    def exchange1(n):
        return pltpu.make_async_remote_copy(
            src_ref=zs.at[n], dst_ref=zr.at[n], send_sem=e1_send.at[n], recv_sem=e1_recv.at[n],
            device_id=(cube ^ 1, wide), device_id_type=MESH,
        )

    for n in range(2):
        half = 1 - high if n == 0 else high
        zs[n] = leaf_quarter(2 * half + 1 - low)
        if n == 0:
            pl.semaphore_wait(barrier, greetings)
        exchange1(n).start()
    for n in range(2):
        half = 1 - high if n == 0 else high
        zo[n] = leaf_quarter(2 * half + low)

    for n in range(3, 7):
        loads[n].wait()
    pm_v[:1, :] = pm_v[pl.ds(parent - pm_base, 1), :]
    up_row_hot = one_hot(pm_v, pv_s, parent, wide)

    def upper_quarter(n):
        half = 1 - high if n == 0 else high
        first = jnp.where(half == 0, l1_v[:, 0, 0, :], l1_v[:, 0, 1, :])
        values = first + zo[n] + zr[n]
        hots = [one_hot(pm_v, pv_s, parent, (2 * half + low) * 4 + i) for i in range(4)]
        return map_quarter(values, up_row_hot, hots)

    def exchange2(i):
        rows = pl.ds(pl.multiple_of(i * 32, 32), 32)
        return pltpu.make_async_remote_copy(
            src_ref=us.at[rows], dst_ref=ur.at[rows], send_sem=e2_send.at[i], recv_sem=e2_recv.at[i],
            device_id=(cube ^ 2, wide), device_id_type=MESH,
        )

    exchange1(0).wait_recv()
    us[...] = upper_quarter(0)
    def rows_of(w):
        return pl.ds(pl.multiple_of(w * CYC, CYC), CYC)

    def corner_term():
        return pltpu.make_async_remote_copy(
            src_ref=us.at[pl.ds(0, PIV), pl.ds(0, B)], dst_ref=cr, send_sem=cr_send, recv_sem=cr_recv,
            device_id=(cube ^ 2, wide), device_id_type=MESH,
        )

    def pivot_term(j):
        return pltpu.make_async_remote_copy(
            src_ref=us.at[pl.ds(j * CYC, CYC)], dst_ref=terms.at[0], send_sem=pa_send.at[j], recv_sem=pa_recv.at[0],
            device_id=(cube ^ 2, 4 * z_hi + j), device_id_type=MESH,
        )

    def own_term(j):
        return pltpu.make_async_remote_copy(
            src_ref=uk.at[pl.ds(j * CYC, CYC)], dst_ref=terms.at[1], send_sem=pb_send.at[j], recv_sem=pa_recv.at[1],
            device_id=(cube, 4 * z_hi + j), device_id_type=MESH,
        )

    @pl.when(y == 0)
    def _():
        corner_term().start()
        for j in (2, 1, 3, 0):
            pivot_term(j).start()

    order = (2, 1, 3, 0)
    exchange2((z_hi + 2) % 4).start()

    @pl.when(y != 0)
    def _():
        exchange2((z_hi + 1) % 4).start()

    exchange1(1).wait_recv()
    uk[...] = upper_quarter(1) + l2_v[:, 0, :]

    def corner_to(w):
        return pltpu.make_async_remote_copy(
            src_ref=tiles.at[quarter, z_hi], dst_ref=tiles.at[quarter, z_hi],
            send_sem=co_send.at[w], recv_sem=co_recv.at[z_hi],
            device_id=(cube, w), device_id_type=MESH,
        )

    def along_z(d):
        return pltpu.make_async_remote_copy(
            src_ref=at.at[rows_of(wide)], dst_ref=at.at[rows_of(wide)],
            send_sem=zg_send.at[d], recv_sem=pg_recv.at[wide],
            device_id=(cube, (wide + 4 * d) % 16), device_id_type=MESH,
        )

    def along_y(piece_z, d):
        piece = 4 * piece_z + y
        return pltpu.make_async_remote_copy(
            src_ref=at.at[rows_of(piece)], dst_ref=at.at[rows_of(piece)],
            send_sem=yg_send.at[piece_z, d], recv_sem=pg_recv.at[piece],
            device_id=(cube, 4 * z_hi + (y + d) % 4), device_id_type=MESH,
        )

    def piece_from(piece):
        return pltpu.make_async_remote_copy(
            src_ref=at.at[rows_of(piece)], dst_ref=at.at[rows_of(piece)],
            send_sem=zg_send.at[0], recv_sem=pg_recv.at[piece],
            device_id=(cube, piece), device_id_type=MESH,
        )

    def term_from(n):
        return pltpu.make_async_remote_copy(
            src_ref=us.at[pl.ds(0, CYC)], dst_ref=terms.at[n], send_sem=pa_send.at[0], recv_sem=pa_recv.at[n],
            device_id=(cube ^ 2, 4 * z_hi), device_id_type=MESH,
        )

    @pl.when(y == 0)
    def _():
        for j in (2, 1, 3):
            own_term(j).start()
        corner_term().wait_recv()
        block = uk[:PIV, :B] + cr[...]
        tile = block[:CYC]
        for r in range(1, 4):
            moved = pltpu.roll(block[CYC * r : CYC * (r + 1)], PIV * r, 1)
            tile = jnp.where(lane[:CYC] >= PIV * r, moved, tile)
        tiles[quarter, z_hi] = tile

        @pl.loop(0, 15)
        def _(n):
            corner_to((wide + 8 + n + n // 8) % 16).start()

        term_from(0).wait_recv()
        at[rows_of(wide), :] = terms[0] + uk[:CYC, :]

    @pl.when(y != 0)
    def _():
        term_from(0).wait_recv()
        term_from(1).wait_recv()
        at[rows_of(wide), :] = terms[0] + terms[1]

    for d in (2, 1, 3):
        along_z(d).start()
    for d in (2, 1, 3):
        along_y(z_hi, d).start()

    @pl.when(y == 0)
    def _():
        exchange2((z_hi + 1) % 4).start()

    for o in order[2:]:
        exchange2((z_hi + o) % 4).start()

    def share_corner(d):
        return pltpu.make_async_remote_copy(
            src_ref=tiles.at[quarter], dst_ref=tiles.at[quarter],
            send_sem=cs_send.at[d], recv_sem=cs_recv.at[quarter],
            device_id=(cube ^ d, wide), device_id_type=MESH,
        )

    def corner_from(q):
        return pltpu.make_async_remote_copy(
            src_ref=tiles.at[quarter, q], dst_ref=tiles.at[quarter, q],
            send_sem=co_send.at[0], recv_sem=co_recv.at[q],
            device_id=(cube, 4 * q), device_id_type=MESH,
        )

    def spread_rows(w):
        return pltpu.make_async_remote_copy(
            src_ref=f2.at[rows_of(w)], dst_ref=f2r.at[z_hi, y],
            send_sem=aa_send.at[w], recv_sem=aa_recv.at[wide],
            device_id=(cube, w), device_id_type=MESH,
        )

    def spread_columns(w):
        return pltpu.make_async_remote_copy(
            src_ref=tt.at[:, w], dst_ref=f2r.at[quarter, :, :, pl.ds(pl.multiple_of(y * B, B), B)],
            send_sem=ac_send.at[w], recv_sem=aa_recv.at[4 * quarter + y],
            device_id=(group + z_hi, w), device_id_type=MESH,
        )

    def rows_from(part, k):
        return pltpu.make_async_remote_copy(
            src_ref=f2.at[rows_of(0)], dst_ref=f2r.at[part, k],
            send_sem=aa_send.at[0], recv_sem=aa_recv.at[4 * part + k],
            device_id=(cube, 4 * part + k), device_id_type=MESH,
        )

    def columns_from(part, k):
        return pltpu.make_async_remote_copy(
            src_ref=tt.at[:, 0], dst_ref=f2r.at[part, :, :, pl.ds(k * B, B)],
            send_sem=ac_send.at[0], recv_sem=aa_recv.at[4 * part + k],
            device_id=(group + part, 4 * quarter + k), device_id_type=MESH,
        )

    for o in order:
        chunk = (z_hi + o) % 4
        exchange2(chunk).wait_recv()
        rows = pl.ds(pl.multiple_of(chunk * 32, 32), 32)
        f2[rows, :] = uk[rows, :] + ur[rows, :]

        @pl.when(by_rows(z_hi, quarter, chunk))
        def _():
            for k in range(4):
                w = 4 * chunk + k

                @pl.when(w != wide)
                def _():
                    spread_rows(w).start()

    f2r[z_hi, y] = f2[rows_of(wide), :]

    @pl.when(z_hi != quarter)
    def _():
        for i in range(4):
            tt[i] = f2[:, i * B : (i + 1) * B].T.reshape(16, CYC, B)

    for q in range(4):

        @pl.when(wide != 4 * q)
        def _():
            corner_from(q).wait_recv()

    for d in (2, 3, 1):
        share_corner(d).start()

    @pl.when(z_hi != quarter)
    def _():
        for o in (1, 3, 0):
            chunk = (z_hi + o) % 4

            @pl.when(ring(z_hi, chunk) < ring(quarter, chunk))
            def _():
                for k in range(4):
                    spread_columns(4 * chunk + k).start()

    for o in (1, 3, 2):
        piece_z = (z_hi + o) % 4
        piece_from(4 * piece_z + y).wait_recv()
        for d in (2, 1, 3):
            along_y(piece_z, d).start()

    for d in range(1, 4):
        other = quarter ^ d
        pltpu.make_async_remote_copy(
            src_ref=tiles.at[other], dst_ref=tiles.at[other],
            send_sem=cs_send.at[d], recv_sem=cs_recv.at[other],
            device_id=(group + other, wide), device_id_type=MESH,
        ).wait_recv()

    def gathered(parts, r):
        got = parts[0]
        if r:
            got = pltpu.roll(got, B - PIV * r, 1)
        for c in range(1, 4):
            moved = parts[c] if c == r else pltpu.roll(parts[c], PIV * (c - r) % B, 1)
            got = jnp.where(lane[:PIV] >= PIV * c, moved, got)
        return got

    corners = [tiles[c].reshape(PIV, B) for c in range(4)]
    for r in range(4):
        got = gathered(corners, r)
        for q in range(4):
            mat[PIV * q + CYC * r : PIV * q + CYC * (r + 1), :B] = got[CYC * q : CYC * (q + 1)]
    mat[:, B:] = jnp.where(iota((B, B), 0) == lane, 1.0, 0.0)

    def share(d):
        return pltpu.make_async_remote_copy(
            src_ref=msgs.at[quarter], dst_ref=msgs.at[quarter],
            send_sem=cb_send.at[d], recv_sem=cb_recv.at[quarter],
            device_id=(cube ^ d, wide), device_id_type=MESH,
        )

    @pl.loop(0, 4)
    def _(step):
        @pl.when(step == 2)
        def _():
            @pl.loop(0, 16)
            def _(piece):
                @pl.when(piece % 4 != y)
                def _():
                    piece_from(piece).wait_recv()

            packed = jnp.zeros((PIV, B), F32)
            for r in range(4):
                for i in range(4):
                    first = PIV * r + CYC * i
                    part = at[PIV * r : PIV * (r + 1), B * i : B * (i + 1)]
                    moved = pltpu.roll(part, (first + B - CYC * wide) % B, 1)
                    packed = jnp.where(lane[:PIV] >= first, moved, packed)
            msgs[quarter] = packed
            for d in (2, 3, 1):
                share(d).start()

        left = mat[:PIV, :B]
        right = mat[:PIV, B:]
        row_id = iota((PIV, B), 0)
        diag = jnp.ones((PIV, B), F32)
        for first in range(0, PIV, CYC):
            columns = [jnp.broadcast_to(left[:, first + n : first + n + 1], (PIV, B)) for n in range(CYC)]
            for n in range(CYC):
                j = first + n
                pivot = columns[n][j : j + 1, :]
                diag = jnp.where(row_id == j, pivot, diag)
                factor = jnp.where(row_id > j, columns[n] * (1.0 / pivot), 0.0)
                for m in range(n + 1, CYC):
                    columns[m] = columns[m] - factor * columns[m][j : j + 1, :]
                left = left - factor * left[j : j + 1, :]
                right = right - factor * right[j : j + 1, :]
        scale = lax.rsqrt(diag)
        right = right * scale
        linv[pl.ds(pl.multiple_of(step * PIV, PIV), PIV), :] = right

        @pl.when(step < 3)
        def _():
            moved = pltpu.roll(left * scale, B - PIV, 1)
            moved = jnp.where(lane[:PIV] < B - PIV, moved, 0.0)
            both = jnp.concatenate((moved, right), axis=1)
            change = lax.dot_general(
                moved, both, (((0,), (0,)), ((), ())), precision=HIGHEST, preferred_element_type=F32
            )
            trail_left = pltpu.roll(mat[PIV:, :B], B - PIV, 1)
            trail_right = mat[PIV:, B:]
            mat[: B - PIV, :B] = trail_left - change[: B - PIV, :B]
            mat[: B - PIV, B:] = trail_right - change[: B - PIV, B:]

    lower = linv[...]
    lt[...] = jnp.dot(lower, at[...], precision=HIGHEST, preferred_element_type=F32)
    tr_v[...] = lt[:, pl.ds(pl.multiple_of(wide // 4 * B, B), B)].T
    panel_hbm[0] = tr_v[pl.ds(pl.multiple_of(wide % 4 * PIV, PIV), PIV), :]
    for d in range(1, 4):
        other = quarter ^ d
        pltpu.make_async_remote_copy(
            src_ref=msgs.at[other], dst_ref=msgs.at[other],
            send_sem=cb_send.at[d], recv_sem=cb_recv.at[other],
            device_id=(group + other, wide), device_id_type=MESH,
        ).wait_recv()

    shared = [msgs[c] for c in range(4)]
    rows_t = jnp.concatenate([gathered(shared, r) for r in range(4)], axis=0)
    own_t = jnp.dot(lower, rows_t, precision=HIGHEST, preferred_element_type=F32)
    update = lax.dot_general(
        own_t, lt[...], (((0,), (0,)), ((), ())), precision=HIGHEST, preferred_element_type=F32
    )

    for part in range(4):
        as_rows = by_rows(part, quarter, z_hi)
        for k in range(4):

            @pl.when(as_rows & (wide != 4 * part + k))
            def _():
                rows_from(part, k).wait_recv()

            @pl.when(jnp.logical_not(as_rows))
            def _():
                columns_from(part, k).wait_recv()

    row = iota((B, Q), 0)
    inside = (row // CYC % 4 == 0) & (wide * CYC + row % CYC < PIV)
    dropped = inside | (iota((B, Q), 1) < PIV)
    schur_hbm[:, 0, :] = jnp.where(dropped, 0.0, f2r[...].reshape(B, Q) - update)

    for n in range(2):
        exchange1(n).wait_send()
    for i in range(4):
        exchange2(i).wait_send()

    @pl.when(y == 0)
    def _():
        corner_term().wait_send()
        for j in range(4):
            pivot_term(j).wait_send()
        for j in range(1, 4):
            own_term(j).wait_send()

        @pl.loop(1, 16)
        def _(d):
            corner_to((wide + d) % 16).wait_send()

    for d in range(1, 4):
        along_z(d).wait_send()
        share(d).wait_send()
        share_corner(d).wait_send()
        for piece_z in range(4):
            along_y(piece_z, d).wait_send()

    for o in range(4):
        chunk = (z_hi + o) % 4

        @pl.when(by_rows(z_hi, quarter, chunk))
        def _():
            for k in range(4):
                w = 4 * chunk + k

                @pl.when(w != wide)
                def _():
                    spread_rows(w).wait_send()

        @pl.when(ring(z_hi, chunk) < ring(quarter, chunk))
        def _():
            for k in range(4):
                spread_columns(4 * chunk + k).wait_send()


def on_device(updates, entries1, entries2, leaf_maps, leaf_live, parent_maps, parent_live):
    operands = (updates, entries1, entries2, leaf_maps, leaf_live.T, parent_maps, parent_live)
    operands = tuple(pltpu.with_memory_space_constraint(o, pltpu.HBM) for o in operands)
    dma = pltpu.SemaphoreType.DMA
    vmem = pltpu.VMEM
    return pl.pallas_call(
        kernel,
        out_shape=(
            jax.ShapeDtypeStruct((1, PIV, B), F32),
            jax.ShapeDtypeStruct((B, 1, Q), F32),
        ),
        in_specs=[pl.BlockSpec(memory_space=pltpu.HBM)] * 7,
        out_specs=(pl.BlockSpec(memory_space=pltpu.VMEM),) * 2,
        scratch_shapes=[
            vmem((B, 4 * Q), F32), vmem((B, 1, 2, Q), F32), vmem((B, 1, Q), F32),
            vmem((8, 4 * Q), jnp.int32), vmem((8, 4 * Q), jnp.int32),
            pltpu.SMEM((16, 32), jnp.int32), pltpu.SMEM((16, 16), jnp.int32),
            vmem((2, B, Q), F32), vmem((2, B, Q), F32), vmem((2, B, Q), F32),
            vmem((B, Q), F32), vmem((B, Q), F32), vmem((B, Q), F32), vmem((B, Q), F32),
            vmem((4, 4, CYC, Q), F32), vmem((4, 16, CYC, B), F32), vmem((B, Q), F32), vmem((B, Q), F32),
            vmem((PIV, B), F32), vmem((2, CYC, Q), F32),
            vmem((4, 4, CYC, B), F32), vmem((4, PIV, B), F32), vmem((B, 2 * B), F32), vmem((B, B), F32),
            vmem((B, B), F32),
            dma((7,)), dma((2,)), dma((2,)), dma((4,)), dma((4,)), dma((16,)), dma((16,)), dma((16,)),
            dma, dma, dma((4,)), dma((4,)), dma((2,)), dma((4,)), dma((4, 4)), dma((16,)), dma((4,)), dma((4,)),
            dma((16,)), dma((4,)), dma((4,)), dma((4,)),
        ],
        compiler_params=pltpu.CompilerParams(
            collective_id=0, has_side_effects=True, vmem_limit_bytes=16 * 1024 * 1024
        ),
        cost_estimate=pl.CostEstimate(flops=600_000_000, bytes_accessed=3_000_000, transcendentals=0),
    )(*operands)


def solution(mesh):
    placed = (
        P("cube", "wide", None),
        P("wide", "cube", None, None),
        P("wide", "cube", None),
        P(),
        P(),
        P(),
        P(),
    )
    return jax.shard_map(
        on_device,
        mesh=mesh,
        in_specs=placed,
        out_specs=(P("cube", "wide", None), P("wide", "cube", None)),
        check_vma=False,
    )
```

```python
import jax
import jax.numpy as jnp
from jax import lax
from jax.experimental import pallas as pl
from jax.experimental.pallas import tpu as pltpu
from jax.sharding import PartitionSpec as P

F32 = jnp.float32
BF16 = jnp.bfloat16
MESH = pl.DeviceIdType.MESH
HIGHEST = lax.Precision.HIGHEST
B = 128
Q = 512
PIV = 32
CYC = 8


def iota(shape, dim):
    return lax.broadcasted_iota(jnp.int32, shape, dim)


def kernel(
    x_hbm, l1_hbm, l2_hbm, lm_hbm, ll_hbm, pm_hbm, pv_hbm,
    panel_hbm, schur_hbm,
    x_v, l1_v, l2_v, lm_v, pm_v, ll_s, pv_s,
    zs, zo, zr, us, uk, ur, f2, f2r, tt, at, lt, cr, terms, tiles, msgs, mat, linv, tr_v,
    in_sem, e1_send, e1_recv, e2_send, e2_recv, aa_send, aa_recv, ac_send,
    cr_send, cr_recv, pa_send, pb_send, pa_recv, zg_send, yg_send, pg_recv, cb_send, cb_recv,
    co_send, co_recv, cs_send, cs_recv,
):
    cube = lax.axis_index("cube")
    wide = lax.axis_index("wide")
    low = cube % 2
    high = cube // 2 % 2
    quarter = cube % 4
    group = cube - quarter
    z_hi = wide // 4
    y = wide % 4
    parent = cube // 2
    lane = iota((B, B), 1)

    def ring(a, b):
        m = (a - b + 4) % 4
        return m - m // 3 * 2

    def by_rows(part, home, at_z):
        return ring(part, at_z) <= ring(home, at_z)

    lm_base = pl.multiple_of(cube // 8 * 8, 8)
    pm_base = pl.multiple_of(parent // 8 * 8, 8)
    loads = [
        pltpu.make_async_copy(lm_hbm.at[pl.ds(lm_base, 8)], lm_v, in_sem.at[0]),
        pltpu.make_async_copy(ll_hbm, ll_s, in_sem.at[1]),
        pltpu.make_async_copy(x_hbm.at[0], x_v, in_sem.at[2]),
        pltpu.make_async_copy(l1_hbm, l1_v, in_sem.at[3]),
        pltpu.make_async_copy(pm_hbm.at[pl.ds(pm_base, 8)], pm_v, in_sem.at[4]),
        pltpu.make_async_copy(pv_hbm, pv_s, in_sem.at[5]),
        pltpu.make_async_copy(l2_hbm, l2_v, in_sem.at[6]),
    ]
    for load in loads:
        load.start()

    barrier = pltpu.get_barrier_semaphore()

    def greet(c, w):
        pl.semaphore_signal(barrier, inc=1, device_id=(c, w), device_id_type=MESH)

    @pl.loop(0, 15)
    def _(n):
        greet(cube, (wide + 8 + n + n // 8) % 16)

    for part in range(4):

        @pl.when(jnp.logical_not(by_rows(part, quarter, z_hi)))
        def _():
            for k in range(4):
                greet(group + part, 4 * quarter + k)

    greet(cube ^ 2, 4 * z_hi)
    for d in (2, 3, 1):
        greet(cube ^ d, wide)
    apart = ring(z_hi, quarter)
    greetings = 18 + 4 * (apart % 2 * 2 + apart // 2) + 4 * (1 - (y + 3) // 4)

    def one_hot(map_ref, live_ref, live_row, block):
        lanes = pl.multiple_of(block * B, B)
        entry = map_ref[:1, pl.ds(lanes, B)] - lanes
        live = live_ref[block, live_row] if live_ref is ll_s else live_ref[live_row, block]
        hit = (entry == iota((B, B), 0)) & (iota((B, B), 1) < live)
        return jnp.where(hit, 1.0, 0.0).astype(BF16)

    def map_quarter(values, row_hot, hots):
        top = values.astype(BF16)
        rest = (values - top.astype(F32)).astype(BF16)
        top = jnp.dot(row_hot, top, preferred_element_type=F32).astype(BF16)
        rest = jnp.dot(row_hot, rest, preferred_element_type=F32).astype(BF16)
        parts = []
        for i in range(4):
            both = jnp.concatenate((top[:, i * B : (i + 1) * B], rest[:, i * B : (i + 1) * B]), axis=0)
            got = lax.dot_general(both, hots[i], (((1,), (1,)), ((), ())), preferred_element_type=F32)
            parts.append(got[:B] + got[B:])
        return jnp.concatenate(parts, axis=1)

    loads[0].wait()
    loads[1].wait()
    lm_v[:1, :] = lm_v[pl.ds(cube - lm_base, 1), :]
    row_hot = one_hot(lm_v, ll_s, cube, wide)
    loads[2].wait()

    def leaf_quarter(at_quarter):
        hots = [one_hot(lm_v, ll_s, cube, at_quarter * 4 + i) for i in range(4)]
        values = x_v[:, pl.ds(pl.multiple_of(at_quarter * Q, Q), Q)]
        return map_quarter(values, row_hot, hots)

    def exchange1(n):
        return pltpu.make_async_remote_copy(
            src_ref=zs.at[n], dst_ref=zr.at[n], send_sem=e1_send.at[n], recv_sem=e1_recv.at[n],
            device_id=(cube ^ 1, wide), device_id_type=MESH,
        )

    for n in range(2):
        half = 1 - high if n == 0 else high
        zs[n] = leaf_quarter(2 * half + 1 - low)
        if n == 0:
            pl.semaphore_wait(barrier, greetings)
        exchange1(n).start()
    for n in range(2):
        half = 1 - high if n == 0 else high
        zo[n] = leaf_quarter(2 * half + low)

    for n in range(3, 7):
        loads[n].wait()
    pm_v[:1, :] = pm_v[pl.ds(parent - pm_base, 1), :]
    up_row_hot = one_hot(pm_v, pv_s, parent, wide)

    def upper_quarter(n):
        half = 1 - high if n == 0 else high
        first = jnp.where(half == 0, l1_v[:, 0, 0, :], l1_v[:, 0, 1, :])
        values = first + zo[n] + zr[n]
        hots = [one_hot(pm_v, pv_s, parent, (2 * half + low) * 4 + i) for i in range(4)]
        return map_quarter(values, up_row_hot, hots)

    def exchange2(i):
        rows = pl.ds(pl.multiple_of(i * 32, 32), 32)
        return pltpu.make_async_remote_copy(
            src_ref=us.at[rows], dst_ref=ur.at[rows], send_sem=e2_send.at[i], recv_sem=e2_recv.at[i],
            device_id=(cube ^ 2, wide), device_id_type=MESH,
        )

    exchange1(0).wait_recv()
    us[...] = upper_quarter(0)
    def rows_of(w):
        return pl.ds(pl.multiple_of(w * CYC, CYC), CYC)

    def corner_term():
        return pltpu.make_async_remote_copy(
            src_ref=us.at[pl.ds(0, PIV), pl.ds(0, B)], dst_ref=cr, send_sem=cr_send, recv_sem=cr_recv,
            device_id=(cube ^ 2, wide), device_id_type=MESH,
        )

    def pivot_term(j):
        return pltpu.make_async_remote_copy(
            src_ref=us.at[pl.ds(j * CYC, CYC)], dst_ref=terms.at[0], send_sem=pa_send.at[j], recv_sem=pa_recv.at[0],
            device_id=(cube ^ 2, 4 * z_hi + j), device_id_type=MESH,
        )

    def own_term(j):
        return pltpu.make_async_remote_copy(
            src_ref=uk.at[pl.ds(j * CYC, CYC)], dst_ref=terms.at[1], send_sem=pb_send.at[j], recv_sem=pa_recv.at[1],
            device_id=(cube, 4 * z_hi + j), device_id_type=MESH,
        )

    @pl.when(y == 0)
    def _():
        corner_term().start()
        for j in (2, 1, 3, 0):
            pivot_term(j).start()

    order = (2, 1, 3, 0)
    exchange2((z_hi + 2) % 4).start()

    @pl.when(y != 0)
    def _():
        exchange2((z_hi + 1) % 4).start()

    exchange1(1).wait_recv()
    uk[...] = upper_quarter(1) + l2_v[:, 0, :]

    def corner_to(w):
        return pltpu.make_async_remote_copy(
            src_ref=tiles.at[quarter, z_hi], dst_ref=tiles.at[quarter, z_hi],
            send_sem=co_send.at[w], recv_sem=co_recv.at[z_hi],
            device_id=(cube, w), device_id_type=MESH,
        )

    def along_z(d):
        return pltpu.make_async_remote_copy(
            src_ref=at.at[rows_of(wide)], dst_ref=at.at[rows_of(wide)],
            send_sem=zg_send.at[d], recv_sem=pg_recv.at[wide],
            device_id=(cube, (wide + 4 * d) % 16), device_id_type=MESH,
        )

    def along_y(piece_z, d):
        piece = 4 * piece_z + y
        return pltpu.make_async_remote_copy(
            src_ref=at.at[rows_of(piece)], dst_ref=at.at[rows_of(piece)],
            send_sem=yg_send.at[piece_z, d], recv_sem=pg_recv.at[piece],
            device_id=(cube, 4 * z_hi + (y + d) % 4), device_id_type=MESH,
        )

    def piece_from(piece):
        return pltpu.make_async_remote_copy(
            src_ref=at.at[rows_of(piece)], dst_ref=at.at[rows_of(piece)],
            send_sem=zg_send.at[0], recv_sem=pg_recv.at[piece],
            device_id=(cube, piece), device_id_type=MESH,
        )

    def term_from(n):
        return pltpu.make_async_remote_copy(
            src_ref=us.at[pl.ds(0, CYC)], dst_ref=terms.at[n], send_sem=pa_send.at[0], recv_sem=pa_recv.at[n],
            device_id=(cube ^ 2, 4 * z_hi), device_id_type=MESH,
        )

    @pl.when(y == 0)
    def _():
        for j in (2, 1, 3):
            own_term(j).start()
        corner_term().wait_recv()
        block = uk[:PIV, :B] + cr[...]
        tile = block[:CYC]
        for r in range(1, 4):
            moved = pltpu.roll(block[CYC * r : CYC * (r + 1)], PIV * r, 1)
            tile = jnp.where(lane[:CYC] >= PIV * r, moved, tile)
        tiles[quarter, z_hi] = tile

        @pl.loop(0, 15)
        def _(n):
            corner_to((wide + 8 + n + n // 8) % 16).start()

        term_from(0).wait_recv()
        at[rows_of(wide), :] = terms[0] + uk[:CYC, :]

    @pl.when(y != 0)
    def _():
        term_from(0).wait_recv()
        term_from(1).wait_recv()
        at[rows_of(wide), :] = terms[0] + terms[1]

    for d in (2, 1, 3):
        along_z(d).start()
    for d in (2, 1, 3):
        along_y(z_hi, d).start()

    @pl.when(y == 0)
    def _():
        exchange2((z_hi + 1) % 4).start()

    for o in order[2:]:
        exchange2((z_hi + o) % 4).start()

    def share_corner(d):
        return pltpu.make_async_remote_copy(
            src_ref=tiles.at[quarter], dst_ref=tiles.at[quarter],
            send_sem=cs_send.at[d], recv_sem=cs_recv.at[quarter],
            device_id=(cube ^ d, wide), device_id_type=MESH,
        )

    def corner_from(q):
        return pltpu.make_async_remote_copy(
            src_ref=tiles.at[quarter, q], dst_ref=tiles.at[quarter, q],
            send_sem=co_send.at[0], recv_sem=co_recv.at[q],
            device_id=(cube, 4 * q), device_id_type=MESH,
        )

    def spread_rows(w):
        return pltpu.make_async_remote_copy(
            src_ref=f2.at[rows_of(w)], dst_ref=f2r.at[z_hi, y],
            send_sem=aa_send.at[w], recv_sem=aa_recv.at[wide],
            device_id=(cube, w), device_id_type=MESH,
        )

    def spread_columns(w):
        return pltpu.make_async_remote_copy(
            src_ref=tt.at[:, w], dst_ref=f2r.at[quarter, :, :, pl.ds(pl.multiple_of(y * B, B), B)],
            send_sem=ac_send.at[w], recv_sem=aa_recv.at[4 * quarter + y],
            device_id=(group + z_hi, w), device_id_type=MESH,
        )

    def rows_from(part, k):
        return pltpu.make_async_remote_copy(
            src_ref=f2.at[rows_of(0)], dst_ref=f2r.at[part, k],
            send_sem=aa_send.at[0], recv_sem=aa_recv.at[4 * part + k],
            device_id=(cube, 4 * part + k), device_id_type=MESH,
        )

    def columns_from(part, k):
        return pltpu.make_async_remote_copy(
            src_ref=tt.at[:, 0], dst_ref=f2r.at[part, :, :, pl.ds(k * B, B)],
            send_sem=ac_send.at[0], recv_sem=aa_recv.at[4 * part + k],
            device_id=(group + part, 4 * quarter + k), device_id_type=MESH,
        )

    def start_rows(chunk):
        @pl.when(by_rows(z_hi, quarter, chunk))
        def _():
            for k in range(4):
                w = 4 * chunk + k

                @pl.when(w != wide)
                def _():
                    spread_rows(w).start()

    for o in order:
        chunk = (z_hi + o) % 4
        exchange2(chunk).wait_recv()
        rows = pl.ds(pl.multiple_of(chunk * 32, 32), 32)
        f2[rows, :] = uk[rows, :] + ur[rows, :]

        if o in order[:2]:
            start_rows(chunk)

    f2r[z_hi, y] = f2[rows_of(wide), :]

    @pl.when(z_hi != quarter)
    def _():
        for i in range(4):
            tt[i] = f2[:, i * B : (i + 1) * B].T.reshape(16, CYC, B)

    for q in range(4):

        @pl.when(wide != 4 * q)
        def _():
            corner_from(q).wait_recv()

    for d in (2, 3, 1):
        share_corner(d).start()

    for o in (1, 3, 2):
        piece_z = (z_hi + o) % 4
        piece_from(4 * piece_z + y).wait_recv()
        for d in (2, 1, 3):
            along_y(piece_z, d).start()

    for o in order[2:]:
        start_rows((z_hi + o) % 4)

    @pl.when(z_hi != quarter)
    def _():
        for o in (1, 3, 0):
            chunk = (z_hi + o) % 4

            @pl.when(ring(z_hi, chunk) < ring(quarter, chunk))
            def _():
                for k in range(4):
                    spread_columns(4 * chunk + k).start()

    for d in range(1, 4):
        other = quarter ^ d
        pltpu.make_async_remote_copy(
            src_ref=tiles.at[other], dst_ref=tiles.at[other],
            send_sem=cs_send.at[d], recv_sem=cs_recv.at[other],
            device_id=(group + other, wide), device_id_type=MESH,
        ).wait_recv()

    def gathered(parts, r):
        got = parts[0]
        if r:
            got = pltpu.roll(got, B - PIV * r, 1)
        for c in range(1, 4):
            moved = parts[c] if c == r else pltpu.roll(parts[c], PIV * (c - r) % B, 1)
            got = jnp.where(lane[:PIV] >= PIV * c, moved, got)
        return got

    corners = [tiles[c].reshape(PIV, B) for c in range(4)]
    for r in range(4):
        got = gathered(corners, r)
        for q in range(4):
            mat[PIV * q + CYC * r : PIV * q + CYC * (r + 1), :B] = got[CYC * q : CYC * (q + 1)]
    mat[:, B:] = jnp.where(iota((B, B), 0) == lane, 1.0, 0.0)

    def share(d):
        return pltpu.make_async_remote_copy(
            src_ref=msgs.at[quarter], dst_ref=msgs.at[quarter],
            send_sem=cb_send.at[d], recv_sem=cb_recv.at[quarter],
            device_id=(cube ^ d, wide), device_id_type=MESH,
        )

    @pl.loop(0, 4)
    def _(step):
        @pl.when(step == 2)
        def _():
            @pl.loop(0, 16)
            def _(piece):
                @pl.when(piece % 4 != y)
                def _():
                    piece_from(piece).wait_recv()

            packed = jnp.zeros((PIV, B), F32)
            for r in range(4):
                for i in range(4):
                    first = PIV * r + CYC * i
                    part = at[PIV * r : PIV * (r + 1), B * i : B * (i + 1)]
                    moved = pltpu.roll(part, (first + B - CYC * wide) % B, 1)
                    packed = jnp.where(lane[:PIV] >= first, moved, packed)
            msgs[quarter] = packed
            for d in (2, 3, 1):
                share(d).start()

        left = mat[:PIV, :B]
        right = mat[:PIV, B:]
        row_id = iota((PIV, B), 0)
        diag = jnp.ones((PIV, B), F32)
        for first in range(0, PIV, CYC):
            columns = [jnp.broadcast_to(left[:, first + n : first + n + 1], (PIV, B)) for n in range(CYC)]
            for n in range(CYC):
                j = first + n
                pivot = columns[n][j : j + 1, :]
                diag = jnp.where(row_id == j, pivot, diag)
                factor = jnp.where(row_id > j, columns[n] * (1.0 / pivot), 0.0)
                for m in range(n + 1, CYC):
                    columns[m] = columns[m] - factor * columns[m][j : j + 1, :]
                left = left - factor * left[j : j + 1, :]
                right = right - factor * right[j : j + 1, :]
        scale = lax.rsqrt(diag)
        right = right * scale
        linv[pl.ds(pl.multiple_of(step * PIV, PIV), PIV), :] = right

        @pl.when(step < 3)
        def _():
            moved = pltpu.roll(left * scale, B - PIV, 1)
            moved = jnp.where(lane[:PIV] < B - PIV, moved, 0.0)
            both = jnp.concatenate((moved, right), axis=1)
            change = lax.dot_general(
                moved, both, (((0,), (0,)), ((), ())), precision=HIGHEST, preferred_element_type=F32
            )
            trail_left = pltpu.roll(mat[PIV:, :B], B - PIV, 1)
            trail_right = mat[PIV:, B:]
            mat[: B - PIV, :B] = trail_left - change[: B - PIV, :B]
            mat[: B - PIV, B:] = trail_right - change[: B - PIV, B:]

    lower = linv[...]
    lt[...] = jnp.dot(lower, at[...], precision=HIGHEST, preferred_element_type=F32)
    tr_v[...] = lt[:, pl.ds(pl.multiple_of(wide // 4 * B, B), B)].T
    panel_hbm[0] = tr_v[pl.ds(pl.multiple_of(wide % 4 * PIV, PIV), PIV), :]
    for d in range(1, 4):
        other = quarter ^ d
        pltpu.make_async_remote_copy(
            src_ref=msgs.at[other], dst_ref=msgs.at[other],
            send_sem=cb_send.at[d], recv_sem=cb_recv.at[other],
            device_id=(group + other, wide), device_id_type=MESH,
        ).wait_recv()

    shared = [msgs[c] for c in range(4)]
    rows_t = jnp.concatenate([gathered(shared, r) for r in range(4)], axis=0)
    own_t = jnp.dot(lower, rows_t, precision=HIGHEST, preferred_element_type=F32)
    update = lax.dot_general(
        own_t, lt[...], (((0,), (0,)), ((), ())), precision=HIGHEST, preferred_element_type=F32
    )

    for part in range(4):
        as_rows = by_rows(part, quarter, z_hi)
        for k in range(4):

            @pl.when(as_rows & (wide != 4 * part + k))
            def _():
                rows_from(part, k).wait_recv()

            @pl.when(jnp.logical_not(as_rows))
            def _():
                columns_from(part, k).wait_recv()

    row = iota((B, Q), 0)
    inside = (row // CYC % 4 == 0) & (wide * CYC + row % CYC < PIV)
    dropped = inside | (iota((B, Q), 1) < PIV)
    schur_hbm[:, 0, :] = jnp.where(dropped, 0.0, f2r[...].reshape(B, Q) - update)

    for n in range(2):
        exchange1(n).wait_send()
    for i in range(4):
        exchange2(i).wait_send()

    @pl.when(y == 0)
    def _():
        corner_term().wait_send()
        for j in range(4):
            pivot_term(j).wait_send()
        for j in range(1, 4):
            own_term(j).wait_send()

        @pl.loop(1, 16)
        def _(d):
            corner_to((wide + d) % 16).wait_send()

    for d in range(1, 4):
        along_z(d).wait_send()
        share(d).wait_send()
        share_corner(d).wait_send()
        for piece_z in range(4):
            along_y(piece_z, d).wait_send()

    for o in range(4):
        chunk = (z_hi + o) % 4

        @pl.when(by_rows(z_hi, quarter, chunk))
        def _():
            for k in range(4):
                w = 4 * chunk + k

                @pl.when(w != wide)
                def _():
                    spread_rows(w).wait_send()

        @pl.when(ring(z_hi, chunk) < ring(quarter, chunk))
        def _():
            for k in range(4):
                spread_columns(4 * chunk + k).wait_send()


def on_device(updates, entries1, entries2, leaf_maps, leaf_live, parent_maps, parent_live):
    operands = (updates, entries1, entries2, leaf_maps, leaf_live.T, parent_maps, parent_live)
    operands = tuple(pltpu.with_memory_space_constraint(o, pltpu.HBM) for o in operands)
    dma = pltpu.SemaphoreType.DMA
    vmem = pltpu.VMEM
    return pl.pallas_call(
        kernel,
        out_shape=(
            jax.ShapeDtypeStruct((1, PIV, B), F32),
            jax.ShapeDtypeStruct((B, 1, Q), F32),
        ),
        in_specs=[pl.BlockSpec(memory_space=pltpu.HBM)] * 7,
        out_specs=(pl.BlockSpec(memory_space=pltpu.VMEM),) * 2,
        scratch_shapes=[
            vmem((B, 4 * Q), F32), vmem((B, 1, 2, Q), F32), vmem((B, 1, Q), F32),
            vmem((8, 4 * Q), jnp.int32), vmem((8, 4 * Q), jnp.int32),
            pltpu.SMEM((16, 32), jnp.int32), pltpu.SMEM((16, 16), jnp.int32),
            vmem((2, B, Q), F32), vmem((2, B, Q), F32), vmem((2, B, Q), F32),
            vmem((B, Q), F32), vmem((B, Q), F32), vmem((B, Q), F32), vmem((B, Q), F32),
            vmem((4, 4, CYC, Q), F32), vmem((4, 16, CYC, B), F32), vmem((B, Q), F32), vmem((B, Q), F32),
            vmem((PIV, B), F32), vmem((2, CYC, Q), F32),
            vmem((4, 4, CYC, B), F32), vmem((4, PIV, B), F32), vmem((B, 2 * B), F32), vmem((B, B), F32),
            vmem((B, B), F32),
            dma((7,)), dma((2,)), dma((2,)), dma((4,)), dma((4,)), dma((16,)), dma((16,)), dma((16,)),
            dma, dma, dma((4,)), dma((4,)), dma((2,)), dma((4,)), dma((4, 4)), dma((16,)), dma((4,)), dma((4,)),
            dma((16,)), dma((4,)), dma((4,)), dma((4,)),
        ],
        compiler_params=pltpu.CompilerParams(
            collective_id=0, has_side_effects=True, vmem_limit_bytes=16 * 1024 * 1024
        ),
        cost_estimate=pl.CostEstimate(flops=600_000_000, bytes_accessed=3_000_000, transcendentals=0),
    )(*operands)


def solution(mesh):
    placed = (
        P("cube", "wide", None),
        P("wide", "cube", None, None),
        P("wide", "cube", None),
        P(),
        P(),
        P(),
        P(),
    )
    return jax.shard_map(
        on_device,
        mesh=mesh,
        in_specs=placed,
        out_specs=(P("cube", "wide", None), P("wide", "cube", None)),
        check_vma=False,
    )
```

```python
import jax
import jax.numpy as jnp
from jax import lax
from jax.experimental import pallas as pl
from jax.experimental.pallas import tpu as pltpu
from jax.sharding import PartitionSpec as P

F32 = jnp.float32
BF16 = jnp.bfloat16
MESH = pl.DeviceIdType.MESH
HIGHEST = lax.Precision.HIGHEST
B = 128
Q = 512
PIV = 32
CYC = 8


def iota(shape, dim):
    return lax.broadcasted_iota(jnp.int32, shape, dim)


def kernel(
    x_hbm, l1_hbm, l2_hbm, lm_hbm, ll_hbm, pm_hbm, pv_hbm,
    panel_hbm, schur_hbm,
    x_v, l1_v, l2_v, lm_v, pm_v, ll_s, pv_s,
    zs, zo, zr, us, uk, ur, f2, f2r, tt, at, lt, cr, terms, tiles, msgs, packs, mat, linv, tr_v,
    in_sem, e1_send, e1_recv, e2_send, e2_recv, aa_send, aa_recv, ac_send,
    cr_send, cr_recv, pa_send, pb_send, pa_recv, zg_send, yg_send, pg_recv, cb_send, cb_recv,
    co_send, co_recv, cs_send, cs_recv,
):
    cube = lax.axis_index("cube")
    wide = lax.axis_index("wide")
    low = cube % 2
    high = cube // 2 % 2
    quarter = cube % 4
    group = cube - quarter
    z_hi = wide // 4
    y = wide % 4
    parent = cube // 2
    lane = iota((B, B), 1)

    def ring(a, b):
        m = (a - b + 4) % 4
        return m - m // 3 * 2

    def by_rows(part, home, at_z):
        return ring(part, at_z) <= ring(home, at_z)

    lm_base = pl.multiple_of(cube // 8 * 8, 8)
    pm_base = pl.multiple_of(parent // 8 * 8, 8)
    loads = [
        pltpu.make_async_copy(lm_hbm.at[pl.ds(lm_base, 8)], lm_v, in_sem.at[0]),
        pltpu.make_async_copy(ll_hbm, ll_s, in_sem.at[1]),
        pltpu.make_async_copy(x_hbm.at[0], x_v, in_sem.at[2]),
        pltpu.make_async_copy(l1_hbm, l1_v, in_sem.at[3]),
        pltpu.make_async_copy(pm_hbm.at[pl.ds(pm_base, 8)], pm_v, in_sem.at[4]),
        pltpu.make_async_copy(pv_hbm, pv_s, in_sem.at[5]),
        pltpu.make_async_copy(l2_hbm, l2_v, in_sem.at[6]),
    ]
    for load in loads:
        load.start()

    barrier = pltpu.get_barrier_semaphore()

    def greet(c, w):
        pl.semaphore_signal(barrier, inc=1, device_id=(c, w), device_id_type=MESH)

    @pl.loop(0, 15)
    def _(n):
        greet(cube, (wide + 8 + n + n // 8) % 16)

    for part in range(4):

        @pl.when(jnp.logical_not(by_rows(part, quarter, z_hi)))
        def _():
            for k in range(4):
                greet(group + part, 4 * quarter + k)

    greet(cube ^ 2, 4 * z_hi)
    for d in (2, 3, 1):
        for e in range(4):
            greet(cube ^ d, 4 * z_hi + (y + e) % 4)
    apart = ring(z_hi, quarter)
    greetings = 27 + 4 * (apart % 2 * 2 + apart // 2) + 4 * (1 - (y + 3) // 4)

    def one_hot(map_ref, live_ref, live_row, block):
        lanes = pl.multiple_of(block * B, B)
        entry = map_ref[:1, pl.ds(lanes, B)] - lanes
        live = live_ref[block, live_row] if live_ref is ll_s else live_ref[live_row, block]
        hit = (entry == iota((B, B), 0)) & (iota((B, B), 1) < live)
        return jnp.where(hit, 1.0, 0.0).astype(BF16)

    def map_quarter(values, row_hot, hots):
        top = values.astype(BF16)
        rest = (values - top.astype(F32)).astype(BF16)
        top = jnp.dot(row_hot, top, preferred_element_type=F32).astype(BF16)
        rest = jnp.dot(row_hot, rest, preferred_element_type=F32).astype(BF16)
        parts = []
        for i in range(4):
            both = jnp.concatenate((top[:, i * B : (i + 1) * B], rest[:, i * B : (i + 1) * B]), axis=0)
            got = lax.dot_general(both, hots[i], (((1,), (1,)), ((), ())), preferred_element_type=F32)
            parts.append(got[:B] + got[B:])
        return jnp.concatenate(parts, axis=1)

    loads[0].wait()
    loads[1].wait()
    lm_v[:1, :] = lm_v[pl.ds(cube - lm_base, 1), :]
    row_hot = one_hot(lm_v, ll_s, cube, wide)
    loads[2].wait()

    def leaf_quarter(at_quarter):
        hots = [one_hot(lm_v, ll_s, cube, at_quarter * 4 + i) for i in range(4)]
        values = x_v[:, pl.ds(pl.multiple_of(at_quarter * Q, Q), Q)]
        return map_quarter(values, row_hot, hots)

    def exchange1(n):
        return pltpu.make_async_remote_copy(
            src_ref=zs.at[n], dst_ref=zr.at[n], send_sem=e1_send.at[n], recv_sem=e1_recv.at[n],
            device_id=(cube ^ 1, wide), device_id_type=MESH,
        )

    for n in range(2):
        half = 1 - high if n == 0 else high
        zs[n] = leaf_quarter(2 * half + 1 - low)
        if n == 0:
            pl.semaphore_wait(barrier, greetings)
        exchange1(n).start()
    for n in range(2):
        half = 1 - high if n == 0 else high
        zo[n] = leaf_quarter(2 * half + low)

    for n in range(3, 7):
        loads[n].wait()
    pm_v[:1, :] = pm_v[pl.ds(parent - pm_base, 1), :]
    up_row_hot = one_hot(pm_v, pv_s, parent, wide)

    def upper_quarter(n):
        half = 1 - high if n == 0 else high
        first = jnp.where(half == 0, l1_v[:, 0, 0, :], l1_v[:, 0, 1, :])
        values = first + zo[n] + zr[n]
        hots = [one_hot(pm_v, pv_s, parent, (2 * half + low) * 4 + i) for i in range(4)]
        return map_quarter(values, up_row_hot, hots)

    def exchange2(i):
        rows = pl.ds(pl.multiple_of(i * 32, 32), 32)
        return pltpu.make_async_remote_copy(
            src_ref=us.at[rows], dst_ref=ur.at[rows], send_sem=e2_send.at[i], recv_sem=e2_recv.at[i],
            device_id=(cube ^ 2, wide), device_id_type=MESH,
        )

    exchange1(0).wait_recv()
    us[...] = upper_quarter(0)
    def rows_of(w):
        return pl.ds(pl.multiple_of(w * CYC, CYC), CYC)

    def corner_term():
        return pltpu.make_async_remote_copy(
            src_ref=us.at[pl.ds(0, PIV), pl.ds(0, B)], dst_ref=cr, send_sem=cr_send, recv_sem=cr_recv,
            device_id=(cube ^ 2, wide), device_id_type=MESH,
        )

    def pivot_term(j):
        return pltpu.make_async_remote_copy(
            src_ref=us.at[pl.ds(j * CYC, CYC)], dst_ref=terms.at[0], send_sem=pa_send.at[j], recv_sem=pa_recv.at[0],
            device_id=(cube ^ 2, 4 * z_hi + j), device_id_type=MESH,
        )

    def own_term(j):
        return pltpu.make_async_remote_copy(
            src_ref=uk.at[pl.ds(j * CYC, CYC)], dst_ref=terms.at[1], send_sem=pb_send.at[j], recv_sem=pa_recv.at[1],
            device_id=(cube, 4 * z_hi + j), device_id_type=MESH,
        )

    @pl.when(y == 0)
    def _():
        corner_term().start()
        for j in (2, 1, 3, 0):
            pivot_term(j).start()

    order = (2, 1, 3, 0)
    exchange2((z_hi + 2) % 4).start()

    @pl.when(y != 0)
    def _():
        exchange2((z_hi + 1) % 4).start()

    exchange1(1).wait_recv()
    uk[...] = upper_quarter(1) + l2_v[:, 0, :]

    def corner_to(w):
        return pltpu.make_async_remote_copy(
            src_ref=tiles.at[quarter, z_hi], dst_ref=tiles.at[quarter, z_hi],
            send_sem=co_send.at[w], recv_sem=co_recv.at[z_hi],
            device_id=(cube, w), device_id_type=MESH,
        )

    def along_z(d):
        return pltpu.make_async_remote_copy(
            src_ref=at.at[rows_of(wide)], dst_ref=at.at[rows_of(wide)],
            send_sem=zg_send.at[d], recv_sem=pg_recv.at[wide],
            device_id=(cube, (wide + 4 * d) % 16), device_id_type=MESH,
        )

    def along_y(piece_z, d):
        piece = 4 * piece_z + y
        return pltpu.make_async_remote_copy(
            src_ref=at.at[rows_of(piece)], dst_ref=at.at[rows_of(piece)],
            send_sem=yg_send.at[piece_z, d], recv_sem=pg_recv.at[piece],
            device_id=(cube, 4 * z_hi + (y + d) % 4), device_id_type=MESH,
        )

    def piece_from(piece):
        return pltpu.make_async_remote_copy(
            src_ref=at.at[rows_of(piece)], dst_ref=at.at[rows_of(piece)],
            send_sem=zg_send.at[0], recv_sem=pg_recv.at[piece],
            device_id=(cube, piece), device_id_type=MESH,
        )

    def term_from(n):
        return pltpu.make_async_remote_copy(
            src_ref=us.at[pl.ds(0, CYC)], dst_ref=terms.at[n], send_sem=pa_send.at[0], recv_sem=pa_recv.at[n],
            device_id=(cube ^ 2, 4 * z_hi), device_id_type=MESH,
        )

    @pl.when(y == 0)
    def _():
        for j in (2, 1, 3):
            own_term(j).start()
        corner_term().wait_recv()
        block = uk[:PIV, :B] + cr[...]
        tile = block[:CYC]
        for r in range(1, 4):
            moved = pltpu.roll(block[CYC * r : CYC * (r + 1)], PIV * r, 1)
            tile = jnp.where(lane[:CYC] >= PIV * r, moved, tile)
        tiles[quarter, z_hi] = tile

        @pl.loop(0, 15)
        def _(n):
            corner_to((wide + 8 + n + n // 8) % 16).start()

        term_from(0).wait_recv()
        at[rows_of(wide), :] = terms[0] + uk[:CYC, :]

    @pl.when(y != 0)
    def _():
        term_from(0).wait_recv()
        term_from(1).wait_recv()
        at[rows_of(wide), :] = terms[0] + terms[1]

    for d in (2, 1, 3):
        along_z(d).start()
    for d in (2, 1, 3):
        along_y(z_hi, d).start()

    @pl.when(y == 0)
    def _():
        exchange2((z_hi + 1) % 4).start()

    for o in order[2:]:
        exchange2((z_hi + o) % 4).start()

    def share_corner(d):
        return pltpu.make_async_remote_copy(
            src_ref=tiles.at[quarter], dst_ref=tiles.at[quarter],
            send_sem=cs_send.at[d], recv_sem=cs_recv.at[quarter],
            device_id=(cube ^ d, wide), device_id_type=MESH,
        )

    def corner_from(q):
        return pltpu.make_async_remote_copy(
            src_ref=tiles.at[quarter, q], dst_ref=tiles.at[quarter, q],
            send_sem=co_send.at[0], recv_sem=co_recv.at[q],
            device_id=(cube, 4 * q), device_id_type=MESH,
        )

    def spread_rows(w):
        return pltpu.make_async_remote_copy(
            src_ref=f2.at[rows_of(w)], dst_ref=f2r.at[z_hi, y],
            send_sem=aa_send.at[w], recv_sem=aa_recv.at[wide],
            device_id=(cube, w), device_id_type=MESH,
        )

    def spread_columns(w):
        return pltpu.make_async_remote_copy(
            src_ref=tt.at[:, w], dst_ref=f2r.at[quarter, :, :, pl.ds(pl.multiple_of(y * B, B), B)],
            send_sem=ac_send.at[w], recv_sem=aa_recv.at[4 * quarter + y],
            device_id=(group + z_hi, w), device_id_type=MESH,
        )

    def rows_from(part, k):
        return pltpu.make_async_remote_copy(
            src_ref=f2.at[rows_of(0)], dst_ref=f2r.at[part, k],
            send_sem=aa_send.at[0], recv_sem=aa_recv.at[4 * part + k],
            device_id=(cube, 4 * part + k), device_id_type=MESH,
        )

    def columns_from(part, k):
        return pltpu.make_async_remote_copy(
            src_ref=tt.at[:, 0], dst_ref=f2r.at[part, :, :, pl.ds(k * B, B)],
            send_sem=ac_send.at[0], recv_sem=aa_recv.at[4 * part + k],
            device_id=(group + part, 4 * quarter + k), device_id_type=MESH,
        )

    def start_rows(chunk):
        @pl.when(by_rows(z_hi, quarter, chunk))
        def _():
            for k in range(4):
                w = 4 * chunk + k

                @pl.when(w != wide)
                def _():
                    spread_rows(w).start()

    for o in order:
        chunk = (z_hi + o) % 4
        exchange2(chunk).wait_recv()
        rows = pl.ds(pl.multiple_of(chunk * 32, 32), 32)
        f2[rows, :] = uk[rows, :] + ur[rows, :]

        if o in order[:2]:
            start_rows(chunk)

    f2r[z_hi, y] = f2[rows_of(wide), :]

    @pl.when(z_hi != quarter)
    def _():
        for i in range(4):
            tt[i] = f2[:, i * B : (i + 1) * B].T.reshape(16, CYC, B)

    for q in range(4):

        @pl.when(wide != 4 * q)
        def _():
            corner_from(q).wait_recv()

    for d in (2, 3, 1):
        share_corner(d).start()

    for o in (1, 3, 2):
        piece_z = (z_hi + o) % 4
        piece_from(4 * piece_z + y).wait_recv()
        for d in (2, 1, 3):
            along_y(piece_z, d).start()

    for e in range(4):
        to_y = (y + e) % 4
        packed = jnp.zeros((CYC, B), F32)
        for r in range(4):
            rows = at[rows_of(4 * r + y), :]
            for i in range(4):
                first = PIV * r + CYC * i
                moved = pltpu.roll(rows[:, B * i : B * (i + 1)], (first + B - CYC * (4 * z_hi + to_y)) % B, 1)
                packed = jnp.where(lane[:CYC] >= first, moved, packed)
        packs[e] = packed

    def share(d, e):
        return pltpu.make_async_remote_copy(
            src_ref=packs.at[e], dst_ref=msgs.at[quarter, y], send_sem=cb_send.at[d, e], recv_sem=cb_recv.at[quarter, y],
            device_id=(cube ^ d, 4 * z_hi + (y + e) % 4), device_id_type=MESH,
        )

    def shared_from(d, e):
        other, other_y = quarter ^ d, (y + e) % 4
        return pltpu.make_async_remote_copy(
            src_ref=packs.at[0], dst_ref=msgs.at[other, other_y], send_sem=cb_send.at[d, e], recv_sem=cb_recv.at[other, other_y],
            device_id=(group + other, 4 * z_hi + other_y), device_id_type=MESH,
        )

    others = [(d, e) for d in (2, 3, 1, 0) for e in (2, 1, 3, 0) if d or e]
    for d, e in others:
        share(d, e).start()
    msgs[quarter, y] = packs[0]

    for o in order[2:]:
        start_rows((z_hi + o) % 4)

    @pl.when(z_hi != quarter)
    def _():
        for o in (1, 3, 0):
            chunk = (z_hi + o) % 4

            @pl.when(ring(z_hi, chunk) < ring(quarter, chunk))
            def _():
                for k in range(4):
                    spread_columns(4 * chunk + k).start()

    for d in range(1, 4):
        other = quarter ^ d
        pltpu.make_async_remote_copy(
            src_ref=tiles.at[other], dst_ref=tiles.at[other],
            send_sem=cs_send.at[d], recv_sem=cs_recv.at[other],
            device_id=(group + other, wide), device_id_type=MESH,
        ).wait_recv()

    def gathered(parts, r):
        got = parts[0]
        if r:
            got = pltpu.roll(got, B - PIV * r, 1)
        for c in range(1, 4):
            moved = parts[c] if c == r else pltpu.roll(parts[c], PIV * (c - r) % B, 1)
            got = jnp.where(lane[:PIV] >= PIV * c, moved, got)
        return got

    corners = [tiles[c].reshape(PIV, B) for c in range(4)]
    for r in range(4):
        got = gathered(corners, r)
        for q in range(4):
            mat[PIV * q + CYC * r : PIV * q + CYC * (r + 1), :B] = got[CYC * q : CYC * (q + 1)]
    mat[:, B:] = jnp.where(iota((B, B), 0) == lane, 1.0, 0.0)

    @pl.loop(0, 4)
    def _(step):
        left = mat[:PIV, :B]
        right = mat[:PIV, B:]
        row_id = iota((PIV, B), 0)
        diag = jnp.ones((PIV, B), F32)
        for first in range(0, PIV, CYC):
            columns = [jnp.broadcast_to(left[:, first + n : first + n + 1], (PIV, B)) for n in range(CYC)]
            for n in range(CYC):
                j = first + n
                pivot = columns[n][j : j + 1, :]
                diag = jnp.where(row_id == j, pivot, diag)
                factor = jnp.where(row_id > j, columns[n] * (1.0 / pivot), 0.0)
                for m in range(n + 1, CYC):
                    columns[m] = columns[m] - factor * columns[m][j : j + 1, :]
                left = left - factor * left[j : j + 1, :]
                right = right - factor * right[j : j + 1, :]
        scale = lax.rsqrt(diag)
        right = right * scale
        linv[pl.ds(pl.multiple_of(step * PIV, PIV), PIV), :] = right

        @pl.when(step < 3)
        def _():
            moved = pltpu.roll(left * scale, B - PIV, 1)
            moved = jnp.where(lane[:PIV] < B - PIV, moved, 0.0)
            both = jnp.concatenate((moved, right), axis=1)
            change = lax.dot_general(
                moved, both, (((0,), (0,)), ((), ())), precision=HIGHEST, preferred_element_type=F32
            )
            trail_left = pltpu.roll(mat[PIV:, :B], B - PIV, 1)
            trail_right = mat[PIV:, B:]
            mat[: B - PIV, :B] = trail_left - change[: B - PIV, :B]
            mat[: B - PIV, B:] = trail_right - change[: B - PIV, B:]

    @pl.loop(0, 16)
    def _(piece):
        @pl.when(piece % 4 != y)
        def _():
            piece_from(piece).wait_recv()

    lower = linv[...]
    lt[...] = jnp.dot(lower, at[...], precision=HIGHEST, preferred_element_type=F32)
    tr_v[...] = lt[:, pl.ds(pl.multiple_of(wide // 4 * B, B), B)].T
    panel_hbm[0] = tr_v[pl.ds(pl.multiple_of(wide % 4 * PIV, PIV), PIV), :]
    for d, e in others:
        shared_from(d, e).wait_recv()

    shared = [msgs[c].reshape(PIV, B) for c in range(4)]
    rows_t = jnp.concatenate([gathered(shared, r) for r in range(4)], axis=0)
    own_t = jnp.dot(lower, rows_t, precision=HIGHEST, preferred_element_type=F32)
    update = lax.dot_general(
        own_t, lt[...], (((0,), (0,)), ((), ())), precision=HIGHEST, preferred_element_type=F32
    )

    for part in range(4):
        as_rows = by_rows(part, quarter, z_hi)
        for k in range(4):

            @pl.when(as_rows & (wide != 4 * part + k))
            def _():
                rows_from(part, k).wait_recv()

            @pl.when(jnp.logical_not(as_rows))
            def _():
                columns_from(part, k).wait_recv()

    row = iota((B, Q), 0)
    inside = (row // CYC % 4 == 0) & (wide * CYC + row % CYC < PIV)
    dropped = inside | (iota((B, Q), 1) < PIV)
    schur_hbm[:, 0, :] = jnp.where(dropped, 0.0, f2r[...].reshape(B, Q) - update)

    for n in range(2):
        exchange1(n).wait_send()
    for i in range(4):
        exchange2(i).wait_send()

    @pl.when(y == 0)
    def _():
        corner_term().wait_send()
        for j in range(4):
            pivot_term(j).wait_send()
        for j in range(1, 4):
            own_term(j).wait_send()

        @pl.loop(1, 16)
        def _(d):
            corner_to((wide + d) % 16).wait_send()

    for d in range(1, 4):
        along_z(d).wait_send()
        share_corner(d).wait_send()
        for piece_z in range(4):
            along_y(piece_z, d).wait_send()

    for d, e in others:
        share(d, e).wait_send()

    for o in range(4):
        chunk = (z_hi + o) % 4

        @pl.when(by_rows(z_hi, quarter, chunk))
        def _():
            for k in range(4):
                w = 4 * chunk + k

                @pl.when(w != wide)
                def _():
                    spread_rows(w).wait_send()

        @pl.when(ring(z_hi, chunk) < ring(quarter, chunk))
        def _():
            for k in range(4):
                spread_columns(4 * chunk + k).wait_send()


def on_device(updates, entries1, entries2, leaf_maps, leaf_live, parent_maps, parent_live):
    operands = (updates, entries1, entries2, leaf_maps, leaf_live.T, parent_maps, parent_live)
    operands = tuple(pltpu.with_memory_space_constraint(o, pltpu.HBM) for o in operands)
    dma = pltpu.SemaphoreType.DMA
    vmem = pltpu.VMEM
    return pl.pallas_call(
        kernel,
        out_shape=(
            jax.ShapeDtypeStruct((1, PIV, B), F32),
            jax.ShapeDtypeStruct((B, 1, Q), F32),
        ),
        in_specs=[pl.BlockSpec(memory_space=pltpu.HBM)] * 7,
        out_specs=(pl.BlockSpec(memory_space=pltpu.VMEM),) * 2,
        scratch_shapes=[
            vmem((B, 4 * Q), F32), vmem((B, 1, 2, Q), F32), vmem((B, 1, Q), F32),
            vmem((8, 4 * Q), jnp.int32), vmem((8, 4 * Q), jnp.int32),
            pltpu.SMEM((16, 32), jnp.int32), pltpu.SMEM((16, 16), jnp.int32),
            vmem((2, B, Q), F32), vmem((2, B, Q), F32), vmem((2, B, Q), F32),
            vmem((B, Q), F32), vmem((B, Q), F32), vmem((B, Q), F32), vmem((B, Q), F32),
            vmem((4, 4, CYC, Q), F32), vmem((4, 16, CYC, B), F32), vmem((B, Q), F32), vmem((B, Q), F32),
            vmem((PIV, B), F32), vmem((2, CYC, Q), F32),
            vmem((4, 4, CYC, B), F32), vmem((4, 4, CYC, B), F32), vmem((4, CYC, B), F32), vmem((B, 2 * B), F32), vmem((B, B), F32),
            vmem((B, B), F32),
            dma((7,)), dma((2,)), dma((2,)), dma((4,)), dma((4,)), dma((16,)), dma((16,)), dma((16,)),
            dma, dma, dma((4,)), dma((4,)), dma((2,)), dma((4,)), dma((4, 4)), dma((16,)), dma((4, 4)), dma((4, 4)),
            dma((16,)), dma((4,)), dma((4,)), dma((4,)),
        ],
        compiler_params=pltpu.CompilerParams(
            collective_id=0, has_side_effects=True, vmem_limit_bytes=16 * 1024 * 1024
        ),
        cost_estimate=pl.CostEstimate(flops=600_000_000, bytes_accessed=3_000_000, transcendentals=0),
    )(*operands)


def solution(mesh):
    placed = (
        P("cube", "wide", None),
        P("wide", "cube", None, None),
        P("wide", "cube", None),
        P(),
        P(),
        P(),
        P(),
    )
    return jax.shard_map(
        on_device,
        mesh=mesh,
        in_specs=placed,
        out_specs=(P("cube", "wide", None), P("wide", "cube", None)),
        check_vma=False,
    )
```

```python
import jax
import jax.numpy as jnp
from jax import lax
from jax.experimental import pallas as pl
from jax.experimental.pallas import tpu as pltpu
from jax.sharding import PartitionSpec as P

F32 = jnp.float32
BF16 = jnp.bfloat16
MESH = pl.DeviceIdType.MESH
HIGHEST = lax.Precision.HIGHEST
B = 128
Q = 512
PIV = 32
CYC = 8


def iota(shape, dim):
    return lax.broadcasted_iota(jnp.int32, shape, dim)


def kernel(
    x_hbm, l1_hbm, l2_hbm, lm_hbm, ll_hbm, pm_hbm, pv_hbm,
    panel_hbm, schur_hbm,
    x_v, l1_v, l2_v, lm_v, pm_v, ll_s, pv_s,
    zs, zo, zr, us, uk, ur, f2, f2r, tt, at, lt, cr, terms, tiles, msgs, packs, mat, linv, tr_v,
    in_sem, e1_send, e1_recv, e2_send, e2_recv, aa_send, aa_recv, ac_send,
    cr_send, cr_recv, pa_send, pb_send, pa_recv, zg_send, yg_send, pg_recv, cb_send, cb_recv,
    co_send, co_recv, cs_send, cs_recv,
):
    cube = lax.axis_index("cube")
    wide = lax.axis_index("wide")
    low = cube % 2
    high = cube // 2 % 2
    quarter = cube % 4
    group = cube - quarter
    z_hi = wide // 4
    y = wide % 4
    parent = cube // 2
    lane = iota((B, B), 1)

    def ring(a, b):
        m = (a - b + 4) % 4
        return m - m // 3 * 2

    def by_rows(part, home, at_z):
        return ring(part, at_z) <= ring(home, at_z)

    lm_base = pl.multiple_of(cube // 8 * 8, 8)
    pm_base = pl.multiple_of(parent // 8 * 8, 8)
    loads = [
        pltpu.make_async_copy(lm_hbm.at[pl.ds(lm_base, 8)], lm_v, in_sem.at[0]),
        pltpu.make_async_copy(ll_hbm, ll_s, in_sem.at[1]),
        pltpu.make_async_copy(x_hbm.at[0], x_v, in_sem.at[2]),
        pltpu.make_async_copy(l1_hbm, l1_v, in_sem.at[3]),
        pltpu.make_async_copy(pm_hbm.at[pl.ds(pm_base, 8)], pm_v, in_sem.at[4]),
        pltpu.make_async_copy(pv_hbm, pv_s, in_sem.at[5]),
        pltpu.make_async_copy(l2_hbm, l2_v, in_sem.at[6]),
    ]
    for load in loads:
        load.start()

    barrier = pltpu.get_barrier_semaphore()

    def greet(c, w):
        pl.semaphore_signal(barrier, inc=1, device_id=(c, w), device_id_type=MESH)

    @pl.loop(0, 15)
    def _(n):
        greet(cube, (wide + 8 + n + n // 8) % 16)

    for part in range(4):

        @pl.when(jnp.logical_not(by_rows(part, quarter, z_hi)))
        def _():
            for k in range(4):
                greet(group + part, 4 * quarter + k)

    greet(cube ^ 2, 4 * z_hi)
    for d in (2, 3, 1):
        for e in range(4):
            greet(cube ^ d, 4 * z_hi + (y + e) % 4)
    apart = ring(z_hi, quarter)
    greetings = 27 + 4 * (apart % 2 * 2 + apart // 2) + 4 * (1 - (y + 3) // 4)

    def one_hot(map_ref, live_ref, live_row, block):
        lanes = pl.multiple_of(block * B, B)
        entry = map_ref[:1, pl.ds(lanes, B)] - lanes
        live = live_ref[block, live_row] if live_ref is ll_s else live_ref[live_row, block]
        hit = (entry == iota((B, B), 0)) & (iota((B, B), 1) < live)
        return jnp.where(hit, 1.0, 0.0).astype(BF16)

    def map_quarter(values, row_hot, hots):
        top = values.astype(BF16)
        rest = (values - top.astype(F32)).astype(BF16)
        top = jnp.dot(row_hot, top, preferred_element_type=F32).astype(BF16)
        rest = jnp.dot(row_hot, rest, preferred_element_type=F32).astype(BF16)
        parts = []
        for i in range(4):
            both = jnp.concatenate((top[:, i * B : (i + 1) * B], rest[:, i * B : (i + 1) * B]), axis=0)
            got = lax.dot_general(both, hots[i], (((1,), (1,)), ((), ())), preferred_element_type=F32)
            parts.append(got[:B] + got[B:])
        return jnp.concatenate(parts, axis=1)

    loads[0].wait()
    loads[1].wait()
    lm_v[:1, :] = lm_v[pl.ds(cube - lm_base, 1), :]
    row_hot = one_hot(lm_v, ll_s, cube, wide)
    loads[2].wait()

    def leaf_quarter(at_quarter):
        hots = [one_hot(lm_v, ll_s, cube, at_quarter * 4 + i) for i in range(4)]
        values = x_v[:, pl.ds(pl.multiple_of(at_quarter * Q, Q), Q)]
        return map_quarter(values, row_hot, hots)

    def exchange1(n):
        return pltpu.make_async_remote_copy(
            src_ref=zs.at[n], dst_ref=zr.at[n], send_sem=e1_send.at[n], recv_sem=e1_recv.at[n],
            device_id=(cube ^ 1, wide), device_id_type=MESH,
        )

    for n in range(2):
        half = 1 - high if n == 0 else high
        zs[n] = leaf_quarter(2 * half + 1 - low)
        if n == 0:
            pl.semaphore_wait(barrier, greetings)
        exchange1(n).start()
    for n in range(2):
        half = 1 - high if n == 0 else high
        zo[n] = leaf_quarter(2 * half + low)

    for n in range(3, 7):
        loads[n].wait()
    pm_v[:1, :] = pm_v[pl.ds(parent - pm_base, 1), :]
    up_row_hot = one_hot(pm_v, pv_s, parent, wide)

    def upper_quarter(n):
        half = 1 - high if n == 0 else high
        first = jnp.where(half == 0, l1_v[:, 0, 0, :], l1_v[:, 0, 1, :])
        values = first + zo[n] + zr[n]
        hots = [one_hot(pm_v, pv_s, parent, (2 * half + low) * 4 + i) for i in range(4)]
        return map_quarter(values, up_row_hot, hots)

    def exchange2(i):
        rows = pl.ds(pl.multiple_of(i * 32, 32), 32)
        return pltpu.make_async_remote_copy(
            src_ref=us.at[rows], dst_ref=ur.at[rows], send_sem=e2_send.at[i], recv_sem=e2_recv.at[i],
            device_id=(cube ^ 2, wide), device_id_type=MESH,
        )

    exchange1(0).wait_recv()
    us[...] = upper_quarter(0)
    def rows_of(w):
        return pl.ds(pl.multiple_of(w * CYC, CYC), CYC)

    def corner_term():
        return pltpu.make_async_remote_copy(
            src_ref=us.at[pl.ds(0, PIV), pl.ds(0, B)], dst_ref=cr, send_sem=cr_send, recv_sem=cr_recv,
            device_id=(cube ^ 2, wide), device_id_type=MESH,
        )

    def pivot_term(j):
        return pltpu.make_async_remote_copy(
            src_ref=us.at[pl.ds(j * CYC, CYC)], dst_ref=terms.at[0], send_sem=pa_send.at[j], recv_sem=pa_recv.at[0],
            device_id=(cube ^ 2, 4 * z_hi + j), device_id_type=MESH,
        )

    def own_term(j):
        return pltpu.make_async_remote_copy(
            src_ref=uk.at[pl.ds(j * CYC, CYC)], dst_ref=terms.at[1], send_sem=pb_send.at[j], recv_sem=pa_recv.at[1],
            device_id=(cube, 4 * z_hi + j), device_id_type=MESH,
        )

    @pl.when(y == 0)
    def _():
        corner_term().start()
        for j in (2, 1, 3, 0):
            pivot_term(j).start()

    order = (2, 1, 3, 0)
    exchange2((z_hi + 2) % 4).start()

    @pl.when(y != 0)
    def _():
        exchange2((z_hi + 1) % 4).start()

    exchange1(1).wait_recv()
    uk[...] = upper_quarter(1) + l2_v[:, 0, :]

    def corner_to(w):
        return pltpu.make_async_remote_copy(
            src_ref=tiles.at[quarter, z_hi], dst_ref=tiles.at[quarter, z_hi],
            send_sem=co_send.at[w], recv_sem=co_recv.at[z_hi],
            device_id=(cube, w), device_id_type=MESH,
        )

    def along_z(d):
        return pltpu.make_async_remote_copy(
            src_ref=at.at[rows_of(wide)], dst_ref=at.at[rows_of(wide)],
            send_sem=zg_send.at[d], recv_sem=pg_recv.at[wide],
            device_id=(cube, (wide + 4 * d) % 16), device_id_type=MESH,
        )

    def along_y(piece_z, d):
        piece = 4 * piece_z + y
        return pltpu.make_async_remote_copy(
            src_ref=at.at[rows_of(piece)], dst_ref=at.at[rows_of(piece)],
            send_sem=yg_send.at[piece_z, d], recv_sem=pg_recv.at[piece],
            device_id=(cube, 4 * z_hi + (y + d) % 4), device_id_type=MESH,
        )

    def piece_from(piece):
        return pltpu.make_async_remote_copy(
            src_ref=at.at[rows_of(piece)], dst_ref=at.at[rows_of(piece)],
            send_sem=zg_send.at[0], recv_sem=pg_recv.at[piece],
            device_id=(cube, piece), device_id_type=MESH,
        )

    def term_from(n):
        return pltpu.make_async_remote_copy(
            src_ref=us.at[pl.ds(0, CYC)], dst_ref=terms.at[n], send_sem=pa_send.at[0], recv_sem=pa_recv.at[n],
            device_id=(cube ^ 2, 4 * z_hi), device_id_type=MESH,
        )

    @pl.when(y == 0)
    def _():
        for j in (2, 1, 3):
            own_term(j).start()
        corner_term().wait_recv()
        block = uk[:PIV, :B] + cr[...]
        tile = block[:CYC]
        for r in range(1, 4):
            moved = pltpu.roll(block[CYC * r : CYC * (r + 1)], PIV * r, 1)
            tile = jnp.where(lane[:CYC] >= PIV * r, moved, tile)
        tiles[quarter, z_hi] = tile

        @pl.loop(0, 15)
        def _(n):
            corner_to((wide + 8 + n + n // 8) % 16).start()

        term_from(0).wait_recv()
        at[rows_of(wide), :] = terms[0] + uk[:CYC, :]

    @pl.when(y != 0)
    def _():
        term_from(0).wait_recv()
        term_from(1).wait_recv()
        at[rows_of(wide), :] = terms[0] + terms[1]

    for d in (2, 1, 3):
        along_z(d).start()
    for d in (2, 1, 3):
        along_y(z_hi, d).start()

    @pl.when(y == 0)
    def _():
        exchange2((z_hi + 1) % 4).start()

    for o in order[2:]:
        exchange2((z_hi + o) % 4).start()

    def share_corner(d):
        return pltpu.make_async_remote_copy(
            src_ref=tiles.at[quarter], dst_ref=tiles.at[quarter],
            send_sem=cs_send.at[d], recv_sem=cs_recv.at[quarter],
            device_id=(cube ^ d, wide), device_id_type=MESH,
        )

    def corner_from(q):
        return pltpu.make_async_remote_copy(
            src_ref=tiles.at[quarter, q], dst_ref=tiles.at[quarter, q],
            send_sem=co_send.at[0], recv_sem=co_recv.at[q],
            device_id=(cube, 4 * q), device_id_type=MESH,
        )

    def spread_rows(w):
        return pltpu.make_async_remote_copy(
            src_ref=f2.at[rows_of(w)], dst_ref=f2r.at[z_hi, y],
            send_sem=aa_send.at[w], recv_sem=aa_recv.at[wide],
            device_id=(cube, w), device_id_type=MESH,
        )

    def spread_columns(w):
        return pltpu.make_async_remote_copy(
            src_ref=tt.at[:, w], dst_ref=f2r.at[quarter, :, :, pl.ds(pl.multiple_of(y * B, B), B)],
            send_sem=ac_send.at[w], recv_sem=aa_recv.at[4 * quarter + y],
            device_id=(group + z_hi, w), device_id_type=MESH,
        )

    def rows_from(part, k):
        return pltpu.make_async_remote_copy(
            src_ref=f2.at[rows_of(0)], dst_ref=f2r.at[part, k],
            send_sem=aa_send.at[0], recv_sem=aa_recv.at[4 * part + k],
            device_id=(cube, 4 * part + k), device_id_type=MESH,
        )

    def columns_from(part, k):
        return pltpu.make_async_remote_copy(
            src_ref=tt.at[:, 0], dst_ref=f2r.at[part, :, :, pl.ds(k * B, B)],
            send_sem=ac_send.at[0], recv_sem=aa_recv.at[4 * part + k],
            device_id=(group + part, 4 * quarter + k), device_id_type=MESH,
        )

    def start_rows(chunk):
        @pl.when(by_rows(z_hi, quarter, chunk))
        def _():
            for k in range(4):
                w = 4 * chunk + k

                @pl.when(w != wide)
                def _():
                    spread_rows(w).start()

    for o in order:
        chunk = (z_hi + o) % 4
        exchange2(chunk).wait_recv()
        rows = pl.ds(pl.multiple_of(chunk * 32, 32), 32)
        f2[rows, :] = uk[rows, :] + ur[rows, :]


    f2r[z_hi, y] = f2[rows_of(wide), :]

    @pl.when(z_hi != quarter)
    def _():
        for i in range(4):
            tt[i] = f2[:, i * B : (i + 1) * B].T.reshape(16, CYC, B)

    for q in range(4):

        @pl.when(wide != 4 * q)
        def _():
            corner_from(q).wait_recv()

    for d in (2, 3, 1):
        share_corner(d).start()

    for o in (1, 3, 2):
        piece_z = (z_hi + o) % 4
        piece_from(4 * piece_z + y).wait_recv()
        for d in (2, 1, 3):
            along_y(piece_z, d).start()

    for e in range(4):
        to_y = (y + e) % 4
        packed = jnp.zeros((CYC, B), F32)
        for r in range(4):
            rows = at[rows_of(4 * r + y), :]
            for i in range(4):
                first = PIV * r + CYC * i
                moved = pltpu.roll(rows[:, B * i : B * (i + 1)], (first + B - CYC * (4 * z_hi + to_y)) % B, 1)
                packed = jnp.where(lane[:CYC] >= first, moved, packed)
        packs[e] = packed

    def share(d, e):
        return pltpu.make_async_remote_copy(
            src_ref=packs.at[e], dst_ref=msgs.at[quarter, y], send_sem=cb_send.at[d, e], recv_sem=cb_recv.at[quarter, y],
            device_id=(cube ^ d, 4 * z_hi + (y + e) % 4), device_id_type=MESH,
        )

    def shared_from(d, e):
        other, other_y = quarter ^ d, (y + e) % 4
        return pltpu.make_async_remote_copy(
            src_ref=packs.at[0], dst_ref=msgs.at[other, other_y], send_sem=cb_send.at[d, e], recv_sem=cb_recv.at[other, other_y],
            device_id=(group + other, 4 * z_hi + other_y), device_id_type=MESH,
        )

    others = [(d, e) for d in (2, 3, 1, 0) for e in (2, 1, 3, 0) if d or e]
    for d, e in others:
        share(d, e).start()
    msgs[quarter, y] = packs[0]

    for o in order:
        start_rows((z_hi + o) % 4)

    @pl.when(z_hi != quarter)
    def _():
        for o in (1, 3, 0):
            chunk = (z_hi + o) % 4

            @pl.when(ring(z_hi, chunk) < ring(quarter, chunk))
            def _():
                for k in range(4):
                    spread_columns(4 * chunk + k).start()

    for d in range(1, 4):
        other = quarter ^ d
        pltpu.make_async_remote_copy(
            src_ref=tiles.at[other], dst_ref=tiles.at[other],
            send_sem=cs_send.at[d], recv_sem=cs_recv.at[other],
            device_id=(group + other, wide), device_id_type=MESH,
        ).wait_recv()

    def gathered(parts, r):
        got = parts[0]
        if r:
            got = pltpu.roll(got, B - PIV * r, 1)
        for c in range(1, 4):
            moved = parts[c] if c == r else pltpu.roll(parts[c], PIV * (c - r) % B, 1)
            got = jnp.where(lane[:PIV] >= PIV * c, moved, got)
        return got

    corners = [tiles[c].reshape(PIV, B) for c in range(4)]
    for r in range(4):
        got = gathered(corners, r)
        for q in range(4):
            mat[PIV * q + CYC * r : PIV * q + CYC * (r + 1), :B] = got[CYC * q : CYC * (q + 1)]
    mat[:, B:] = jnp.where(iota((B, B), 0) == lane, 1.0, 0.0)

    @pl.loop(0, 4)
    def _(step):
        left = mat[:PIV, :B]
        right = mat[:PIV, B:]
        row_id = iota((PIV, B), 0)
        diag = jnp.ones((PIV, B), F32)
        for first in range(0, PIV, CYC):
            columns = [jnp.broadcast_to(left[:, first + n : first + n + 1], (PIV, B)) for n in range(CYC)]
            for n in range(CYC):
                j = first + n
                pivot = columns[n][j : j + 1, :]
                diag = jnp.where(row_id == j, pivot, diag)
                factor = jnp.where(row_id > j, columns[n] * (1.0 / pivot), 0.0)
                for m in range(n + 1, CYC):
                    columns[m] = columns[m] - factor * columns[m][j : j + 1, :]
                left = left - factor * left[j : j + 1, :]
                right = right - factor * right[j : j + 1, :]
        scale = lax.rsqrt(diag)
        right = right * scale
        linv[pl.ds(pl.multiple_of(step * PIV, PIV), PIV), :] = right

        @pl.when(step < 3)
        def _():
            moved = pltpu.roll(left * scale, B - PIV, 1)
            moved = jnp.where(lane[:PIV] < B - PIV, moved, 0.0)
            both = jnp.concatenate((moved, right), axis=1)
            change = lax.dot_general(
                moved, both, (((0,), (0,)), ((), ())), precision=HIGHEST, preferred_element_type=F32
            )
            trail_left = pltpu.roll(mat[PIV:, :B], B - PIV, 1)
            trail_right = mat[PIV:, B:]
            mat[: B - PIV, :B] = trail_left - change[: B - PIV, :B]
            mat[: B - PIV, B:] = trail_right - change[: B - PIV, B:]

    @pl.loop(0, 16)
    def _(piece):
        @pl.when(piece % 4 != y)
        def _():
            piece_from(piece).wait_recv()

    lower = linv[...]
    lt[...] = jnp.dot(lower, at[...], precision=HIGHEST, preferred_element_type=F32)
    tr_v[...] = lt[:, pl.ds(pl.multiple_of(wide // 4 * B, B), B)].T
    panel_hbm[0] = tr_v[pl.ds(pl.multiple_of(wide % 4 * PIV, PIV), PIV), :]
    for d, e in others:
        shared_from(d, e).wait_recv()

    shared = [msgs[c].reshape(PIV, B) for c in range(4)]
    rows_t = jnp.concatenate([gathered(shared, r) for r in range(4)], axis=0)
    own_t = jnp.dot(lower, rows_t, precision=HIGHEST, preferred_element_type=F32)
    update = lax.dot_general(
        own_t, lt[...], (((0,), (0,)), ((), ())), precision=HIGHEST, preferred_element_type=F32
    )

    for part in range(4):
        as_rows = by_rows(part, quarter, z_hi)
        for k in range(4):

            @pl.when(as_rows & (wide != 4 * part + k))
            def _():
                rows_from(part, k).wait_recv()

            @pl.when(jnp.logical_not(as_rows))
            def _():
                columns_from(part, k).wait_recv()

    row = iota((B, Q), 0)
    inside = (row // CYC % 4 == 0) & (wide * CYC + row % CYC < PIV)
    dropped = inside | (iota((B, Q), 1) < PIV)
    schur_hbm[:, 0, :] = jnp.where(dropped, 0.0, f2r[...].reshape(B, Q) - update)

    for n in range(2):
        exchange1(n).wait_send()
    for i in range(4):
        exchange2(i).wait_send()

    @pl.when(y == 0)
    def _():
        corner_term().wait_send()
        for j in range(4):
            pivot_term(j).wait_send()
        for j in range(1, 4):
            own_term(j).wait_send()

        @pl.loop(1, 16)
        def _(d):
            corner_to((wide + d) % 16).wait_send()

    for d in range(1, 4):
        along_z(d).wait_send()
        share_corner(d).wait_send()
        for piece_z in range(4):
            along_y(piece_z, d).wait_send()

    for d, e in others:
        share(d, e).wait_send()

    for o in range(4):
        chunk = (z_hi + o) % 4

        @pl.when(by_rows(z_hi, quarter, chunk))
        def _():
            for k in range(4):
                w = 4 * chunk + k

                @pl.when(w != wide)
                def _():
                    spread_rows(w).wait_send()

        @pl.when(ring(z_hi, chunk) < ring(quarter, chunk))
        def _():
            for k in range(4):
                spread_columns(4 * chunk + k).wait_send()


def on_device(updates, entries1, entries2, leaf_maps, leaf_live, parent_maps, parent_live):
    operands = (updates, entries1, entries2, leaf_maps, leaf_live.T, parent_maps, parent_live)
    operands = tuple(pltpu.with_memory_space_constraint(o, pltpu.HBM) for o in operands)
    dma = pltpu.SemaphoreType.DMA
    vmem = pltpu.VMEM
    return pl.pallas_call(
        kernel,
        out_shape=(
            jax.ShapeDtypeStruct((1, PIV, B), F32),
            jax.ShapeDtypeStruct((B, 1, Q), F32),
        ),
        in_specs=[pl.BlockSpec(memory_space=pltpu.HBM)] * 7,
        out_specs=(pl.BlockSpec(memory_space=pltpu.VMEM),) * 2,
        scratch_shapes=[
            vmem((B, 4 * Q), F32), vmem((B, 1, 2, Q), F32), vmem((B, 1, Q), F32),
            vmem((8, 4 * Q), jnp.int32), vmem((8, 4 * Q), jnp.int32),
            pltpu.SMEM((16, 32), jnp.int32), pltpu.SMEM((16, 16), jnp.int32),
            vmem((2, B, Q), F32), vmem((2, B, Q), F32), vmem((2, B, Q), F32),
            vmem((B, Q), F32), vmem((B, Q), F32), vmem((B, Q), F32), vmem((B, Q), F32),
            vmem((4, 4, CYC, Q), F32), vmem((4, 16, CYC, B), F32), vmem((B, Q), F32), vmem((B, Q), F32),
            vmem((PIV, B), F32), vmem((2, CYC, Q), F32),
            vmem((4, 4, CYC, B), F32), vmem((4, 4, CYC, B), F32), vmem((4, CYC, B), F32), vmem((B, 2 * B), F32), vmem((B, B), F32),
            vmem((B, B), F32),
            dma((7,)), dma((2,)), dma((2,)), dma((4,)), dma((4,)), dma((16,)), dma((16,)), dma((16,)),
            dma, dma, dma((4,)), dma((4,)), dma((2,)), dma((4,)), dma((4, 4)), dma((16,)), dma((4, 4)), dma((4, 4)),
            dma((16,)), dma((4,)), dma((4,)), dma((4,)),
        ],
        compiler_params=pltpu.CompilerParams(
            collective_id=0, has_side_effects=True, vmem_limit_bytes=16 * 1024 * 1024
        ),
        cost_estimate=pl.CostEstimate(flops=600_000_000, bytes_accessed=3_000_000, transcendentals=0),
    )(*operands)


def solution(mesh):
    placed = (
        P("cube", "wide", None),
        P("wide", "cube", None, None),
        P("wide", "cube", None),
        P(),
        P(),
        P(),
        P(),
    )
    return jax.shard_map(
        on_device,
        mesh=mesh,
        in_specs=placed,
        out_specs=(P("cube", "wide", None), P("wide", "cube", None)),
        check_vma=False,
    )
```

```python
import jax
import jax.numpy as jnp
from jax import lax
from jax.experimental import pallas as pl
from jax.experimental.pallas import tpu as pltpu
from jax.sharding import PartitionSpec as P

F32 = jnp.float32
BF16 = jnp.bfloat16
MESH = pl.DeviceIdType.MESH
HIGHEST = lax.Precision.HIGHEST
B = 128
Q = 512
PIV = 32
CYC = 8


def iota(shape, dim):
    return lax.broadcasted_iota(jnp.int32, shape, dim)


def kernel(
    x_hbm, l1_hbm, l2_hbm, lm_hbm, ll_hbm, pm_hbm, pv_hbm,
    panel_hbm, schur_hbm,
    x_v, l1_v, l2_v, lm_v, pm_v, ll_s, pv_s,
    zs, zo, zr, us, uk, ur, f2, f2r, tt, at, lt, cr, terms, tiles, msgs, packs, mat, linv, tr_v,
    in_sem, e1_send, e1_recv, e2_send, e2_recv, aa_send, aa_recv, ac_send,
    cr_send, cr_recv, pa_send, pb_send, pa_recv, zg_send, yg_send, pg_recv, cb_send, cb_recv,
    co_send, co_recv, cs_send, cs_recv,
):
    cube = lax.axis_index("cube")
    wide = lax.axis_index("wide")
    low = cube % 2
    high = cube // 2 % 2
    quarter = cube % 4
    group = cube - quarter
    z_hi = wide // 4
    y = wide % 4
    parent = cube // 2
    lane = iota((B, B), 1)

    def ring(a, b):
        m = (a - b + 4) % 4
        return m - m // 3 * 2

    def by_rows(part, home, at_z):
        return ring(part, at_z) <= ring(home, at_z)

    lm_base = pl.multiple_of(cube // 8 * 8, 8)
    pm_base = pl.multiple_of(parent // 8 * 8, 8)
    loads = [
        pltpu.make_async_copy(lm_hbm.at[pl.ds(lm_base, 8)], lm_v, in_sem.at[0]),
        pltpu.make_async_copy(ll_hbm, ll_s, in_sem.at[1]),
        pltpu.make_async_copy(x_hbm.at[0], x_v, in_sem.at[2]),
        pltpu.make_async_copy(l1_hbm, l1_v, in_sem.at[3]),
        pltpu.make_async_copy(pm_hbm.at[pl.ds(pm_base, 8)], pm_v, in_sem.at[4]),
        pltpu.make_async_copy(pv_hbm, pv_s, in_sem.at[5]),
        pltpu.make_async_copy(l2_hbm, l2_v, in_sem.at[6]),
    ]
    for load in loads:
        load.start()

    barrier = pltpu.get_barrier_semaphore()

    def greet(c, w):
        pl.semaphore_signal(barrier, inc=1, device_id=(c, w), device_id_type=MESH)

    @pl.loop(0, 15)
    def _(n):
        greet(cube, (wide + 8 + n + n // 8) % 16)

    for part in range(4):

        @pl.when(jnp.logical_not(by_rows(part, quarter, z_hi)))
        def _():
            for k in range(4):
                greet(group + part, 4 * quarter + k)

    greet(cube ^ 2, 4 * z_hi)
    for d in (2, 3, 1):
        for e in range(4):
            greet(cube ^ d, 4 * z_hi + (y + e) % 4)
    apart = ring(z_hi, quarter)
    greetings = 27 + 4 * (apart % 2 * 2 + apart // 2) + 4 * (1 - (y + 3) // 4)

    def one_hot(map_ref, live_ref, live_row, block):
        lanes = pl.multiple_of(block * B, B)
        entry = map_ref[:1, pl.ds(lanes, B)] - lanes
        live = live_ref[block, live_row] if live_ref is ll_s else live_ref[live_row, block]
        hit = (entry == iota((B, B), 0)) & (iota((B, B), 1) < live)
        return jnp.where(hit, 1.0, 0.0).astype(BF16)

    def map_quarter(values, row_hot, hots):
        top = values.astype(BF16)
        rest = (values - top.astype(F32)).astype(BF16)
        top = jnp.dot(row_hot, top, preferred_element_type=F32).astype(BF16)
        rest = jnp.dot(row_hot, rest, preferred_element_type=F32).astype(BF16)
        parts = []
        for i in range(4):
            both = jnp.concatenate((top[:, i * B : (i + 1) * B], rest[:, i * B : (i + 1) * B]), axis=0)
            got = lax.dot_general(both, hots[i], (((1,), (1,)), ((), ())), preferred_element_type=F32)
            parts.append(got[:B] + got[B:])
        return jnp.concatenate(parts, axis=1)

    loads[0].wait()
    loads[1].wait()
    lm_v[:1, :] = lm_v[pl.ds(cube - lm_base, 1), :]
    row_hot = one_hot(lm_v, ll_s, cube, wide)
    loads[2].wait()

    def leaf_quarter(at_quarter):
        hots = [one_hot(lm_v, ll_s, cube, at_quarter * 4 + i) for i in range(4)]
        values = x_v[:, pl.ds(pl.multiple_of(at_quarter * Q, Q), Q)]
        return map_quarter(values, row_hot, hots)

    def exchange1(n):
        return pltpu.make_async_remote_copy(
            src_ref=zs.at[n], dst_ref=zr.at[n], send_sem=e1_send.at[n], recv_sem=e1_recv.at[n],
            device_id=(cube ^ 1, wide), device_id_type=MESH,
        )

    for n in range(2):
        half = 1 - high if n == 0 else high
        zs[n] = leaf_quarter(2 * half + 1 - low)
        if n == 0:
            pl.semaphore_wait(barrier, greetings)
        exchange1(n).start()
    for n in range(2):
        half = 1 - high if n == 0 else high
        zo[n] = leaf_quarter(2 * half + low)

    for n in range(3, 7):
        loads[n].wait()
    pm_v[:1, :] = pm_v[pl.ds(parent - pm_base, 1), :]
    up_row_hot = one_hot(pm_v, pv_s, parent, wide)

    def upper_quarter(n):
        half = 1 - high if n == 0 else high
        first = jnp.where(half == 0, l1_v[:, 0, 0, :], l1_v[:, 0, 1, :])
        values = first + zo[n] + zr[n]
        hots = [one_hot(pm_v, pv_s, parent, (2 * half + low) * 4 + i) for i in range(4)]
        return map_quarter(values, up_row_hot, hots)

    def exchange2(i):
        rows = pl.ds(pl.multiple_of(i * 32, 32), 32)
        return pltpu.make_async_remote_copy(
            src_ref=us.at[rows], dst_ref=ur.at[rows], send_sem=e2_send.at[i], recv_sem=e2_recv.at[i],
            device_id=(cube ^ 2, wide), device_id_type=MESH,
        )

    exchange1(0).wait_recv()
    us[...] = upper_quarter(0)
    def rows_of(w):
        return pl.ds(pl.multiple_of(w * CYC, CYC), CYC)

    def corner_term():
        return pltpu.make_async_remote_copy(
            src_ref=us.at[pl.ds(0, PIV), pl.ds(0, B)], dst_ref=cr, send_sem=cr_send, recv_sem=cr_recv,
            device_id=(cube ^ 2, wide), device_id_type=MESH,
        )

    def pivot_term(j):
        return pltpu.make_async_remote_copy(
            src_ref=us.at[pl.ds(j * CYC, CYC)], dst_ref=terms.at[0], send_sem=pa_send.at[j], recv_sem=pa_recv.at[0],
            device_id=(cube ^ 2, 4 * z_hi + j), device_id_type=MESH,
        )

    def own_term(j):
        return pltpu.make_async_remote_copy(
            src_ref=uk.at[pl.ds(j * CYC, CYC)], dst_ref=terms.at[1], send_sem=pb_send.at[j], recv_sem=pa_recv.at[1],
            device_id=(cube, 4 * z_hi + j), device_id_type=MESH,
        )

    @pl.when(y == 0)
    def _():
        corner_term().start()
        for j in (2, 1, 3, 0):
            pivot_term(j).start()

    order = (2, 1, 3, 0)
    exchange2((z_hi + 2) % 4).start()

    @pl.when(y != 0)
    def _():
        exchange2((z_hi + 1) % 4).start()

    exchange1(1).wait_recv()
    uk[...] = upper_quarter(1) + l2_v[:, 0, :]

    def corner_to(w):
        return pltpu.make_async_remote_copy(
            src_ref=tiles.at[quarter, z_hi], dst_ref=tiles.at[quarter, z_hi],
            send_sem=co_send.at[w], recv_sem=co_recv.at[z_hi],
            device_id=(cube, w), device_id_type=MESH,
        )

    def along_z(d):
        return pltpu.make_async_remote_copy(
            src_ref=at.at[rows_of(wide)], dst_ref=at.at[rows_of(wide)],
            send_sem=zg_send.at[d], recv_sem=pg_recv.at[wide],
            device_id=(cube, (wide + 4 * d) % 16), device_id_type=MESH,
        )

    def along_y(piece_z, d):
        piece = 4 * piece_z + y
        return pltpu.make_async_remote_copy(
            src_ref=at.at[rows_of(piece)], dst_ref=at.at[rows_of(piece)],
            send_sem=yg_send.at[piece_z, d], recv_sem=pg_recv.at[piece],
            device_id=(cube, 4 * z_hi + (y + d) % 4), device_id_type=MESH,
        )

    def piece_from(piece):
        return pltpu.make_async_remote_copy(
            src_ref=at.at[rows_of(piece)], dst_ref=at.at[rows_of(piece)],
            send_sem=zg_send.at[0], recv_sem=pg_recv.at[piece],
            device_id=(cube, piece), device_id_type=MESH,
        )

    def term_from(n):
        return pltpu.make_async_remote_copy(
            src_ref=us.at[pl.ds(0, CYC)], dst_ref=terms.at[n], send_sem=pa_send.at[0], recv_sem=pa_recv.at[n],
            device_id=(cube ^ 2, 4 * z_hi), device_id_type=MESH,
        )

    @pl.when(y == 0)
    def _():
        for j in (2, 1, 3):
            own_term(j).start()
        corner_term().wait_recv()
        block = uk[:PIV, :B] + cr[...]
        tile = block[:CYC]
        for r in range(1, 4):
            moved = pltpu.roll(block[CYC * r : CYC * (r + 1)], PIV * r, 1)
            tile = jnp.where(lane[:CYC] >= PIV * r, moved, tile)
        tiles[quarter, z_hi] = tile

        @pl.loop(0, 15)
        def _(n):
            corner_to((wide + 8 + n + n // 8) % 16).start()

        term_from(0).wait_recv()
        at[rows_of(wide), :] = terms[0] + uk[:CYC, :]

    @pl.when(y != 0)
    def _():
        term_from(0).wait_recv()
        term_from(1).wait_recv()
        at[rows_of(wide), :] = terms[0] + terms[1]

    for d in (2, 1, 3):
        along_z(d).start()
    for d in (2, 1, 3):
        along_y(z_hi, d).start()

    @pl.when(y == 0)
    def _():
        exchange2((z_hi + 1) % 4).start()

    for o in order[2:]:
        exchange2((z_hi + o) % 4).start()

    def share_corner(d):
        return pltpu.make_async_remote_copy(
            src_ref=tiles.at[quarter], dst_ref=tiles.at[quarter],
            send_sem=cs_send.at[d], recv_sem=cs_recv.at[quarter],
            device_id=(cube ^ d, wide), device_id_type=MESH,
        )

    def corner_from(q):
        return pltpu.make_async_remote_copy(
            src_ref=tiles.at[quarter, q], dst_ref=tiles.at[quarter, q],
            send_sem=co_send.at[0], recv_sem=co_recv.at[q],
            device_id=(cube, 4 * q), device_id_type=MESH,
        )

    def spread_rows(w):
        return pltpu.make_async_remote_copy(
            src_ref=f2.at[rows_of(w)], dst_ref=f2r.at[z_hi, y],
            send_sem=aa_send.at[w], recv_sem=aa_recv.at[wide],
            device_id=(cube, w), device_id_type=MESH,
        )

    def spread_columns(w):
        return pltpu.make_async_remote_copy(
            src_ref=tt.at[:, w], dst_ref=f2r.at[quarter, :, :, pl.ds(pl.multiple_of(y * B, B), B)],
            send_sem=ac_send.at[w], recv_sem=aa_recv.at[4 * quarter + y],
            device_id=(group + z_hi, w), device_id_type=MESH,
        )

    def rows_from(part, k):
        return pltpu.make_async_remote_copy(
            src_ref=f2.at[rows_of(0)], dst_ref=f2r.at[part, k],
            send_sem=aa_send.at[0], recv_sem=aa_recv.at[4 * part + k],
            device_id=(cube, 4 * part + k), device_id_type=MESH,
        )

    def columns_from(part, k):
        return pltpu.make_async_remote_copy(
            src_ref=tt.at[:, 0], dst_ref=f2r.at[part, :, :, pl.ds(k * B, B)],
            send_sem=ac_send.at[0], recv_sem=aa_recv.at[4 * part + k],
            device_id=(group + part, 4 * quarter + k), device_id_type=MESH,
        )

    def start_rows(chunk):
        @pl.when(by_rows(z_hi, quarter, chunk))
        def _():
            for k in range(4):
                w = 4 * chunk + k

                @pl.when(w != wide)
                def _():
                    spread_rows(w).start()

    for o in order:
        chunk = (z_hi + o) % 4
        exchange2(chunk).wait_recv()
        rows = pl.ds(pl.multiple_of(chunk * 32, 32), 32)
        f2[rows, :] = uk[rows, :] + ur[rows, :]


    f2r[z_hi, y] = f2[rows_of(wide), :]

    @pl.when(z_hi != quarter)
    def _():
        for i in range(4):
            tt[i] = f2[:, i * B : (i + 1) * B].T.reshape(16, CYC, B)

    for q in range(4):

        @pl.when(wide != 4 * q)
        def _():
            corner_from(q).wait_recv()

    for d in (2, 3, 1):
        share_corner(d).start()

    for o in (1, 3, 2):
        piece_z = (z_hi + o) % 4
        piece_from(4 * piece_z + y).wait_recv()
        for d in (2, 1, 3):
            along_y(piece_z, d).start()

    for e in range(4):
        to_y = (y + e) % 4
        packed = jnp.zeros((CYC, B), F32)
        for r in range(4):
            rows = at[rows_of(4 * r + y), :]
            for i in range(4):
                first = PIV * r + CYC * i
                moved = pltpu.roll(rows[:, B * i : B * (i + 1)], (first + B - CYC * (4 * z_hi + to_y)) % B, 1)
                packed = jnp.where(lane[:CYC] >= first, moved, packed)
        packs[e] = packed

    def share(d, e):
        return pltpu.make_async_remote_copy(
            src_ref=packs.at[e], dst_ref=msgs.at[quarter, y], send_sem=cb_send.at[d, e], recv_sem=cb_recv.at[quarter, y],
            device_id=(cube ^ d, 4 * z_hi + (y + e) % 4), device_id_type=MESH,
        )

    def shared_from(d, e):
        other, other_y = quarter ^ d, (y + e) % 4
        return pltpu.make_async_remote_copy(
            src_ref=packs.at[0], dst_ref=msgs.at[other, other_y], send_sem=cb_send.at[d, e], recv_sem=cb_recv.at[other, other_y],
            device_id=(group + other, 4 * z_hi + other_y), device_id_type=MESH,
        )

    others = [(d, e) for d in (2, 3, 1, 0) for e in (2, 1, 3, 0) if d or e]
    for d, e in others:
        share(d, e).start()
    msgs[quarter, y] = packs[0]

    for o in order[:3]:
        start_rows((z_hi + o) % 4)

    @pl.when(z_hi != quarter)
    def _():
        for o in (1, 3, 0):
            chunk = (z_hi + o) % 4

            @pl.when(ring(z_hi, chunk) < ring(quarter, chunk))
            def _():
                for k in range(4):
                    spread_columns(4 * chunk + k).start()

    start_rows(z_hi)

    for d in range(1, 4):
        other = quarter ^ d
        pltpu.make_async_remote_copy(
            src_ref=tiles.at[other], dst_ref=tiles.at[other],
            send_sem=cs_send.at[d], recv_sem=cs_recv.at[other],
            device_id=(group + other, wide), device_id_type=MESH,
        ).wait_recv()

    def gathered(parts, r):
        got = parts[0]
        if r:
            got = pltpu.roll(got, B - PIV * r, 1)
        for c in range(1, 4):
            moved = parts[c] if c == r else pltpu.roll(parts[c], PIV * (c - r) % B, 1)
            got = jnp.where(lane[:PIV] >= PIV * c, moved, got)
        return got

    corners = [tiles[c].reshape(PIV, B) for c in range(4)]
    for r in range(4):
        got = gathered(corners, r)
        for q in range(4):
            mat[PIV * q + CYC * r : PIV * q + CYC * (r + 1), :B] = got[CYC * q : CYC * (q + 1)]
    mat[:, B:] = jnp.where(iota((B, B), 0) == lane, 1.0, 0.0)

    @pl.loop(0, 4)
    def _(step):
        left = mat[:PIV, :B]
        right = mat[:PIV, B:]
        row_id = iota((PIV, B), 0)
        diag = jnp.ones((PIV, B), F32)
        for first in range(0, PIV, CYC):
            columns = [jnp.broadcast_to(left[:, first + n : first + n + 1], (PIV, B)) for n in range(CYC)]
            for n in range(CYC):
                j = first + n
                pivot = columns[n][j : j + 1, :]
                diag = jnp.where(row_id == j, pivot, diag)
                factor = jnp.where(row_id > j, columns[n] * (1.0 / pivot), 0.0)
                for m in range(n + 1, CYC):
                    columns[m] = columns[m] - factor * columns[m][j : j + 1, :]
                left = left - factor * left[j : j + 1, :]
                right = right - factor * right[j : j + 1, :]
        scale = lax.rsqrt(diag)
        right = right * scale
        linv[pl.ds(pl.multiple_of(step * PIV, PIV), PIV), :] = right

        @pl.when(step < 3)
        def _():
            moved = pltpu.roll(left * scale, B - PIV, 1)
            moved = jnp.where(lane[:PIV] < B - PIV, moved, 0.0)
            both = jnp.concatenate((moved, right), axis=1)
            change = lax.dot_general(
                moved, both, (((0,), (0,)), ((), ())), precision=HIGHEST, preferred_element_type=F32
            )
            trail_left = pltpu.roll(mat[PIV:, :B], B - PIV, 1)
            trail_right = mat[PIV:, B:]
            mat[: B - PIV, :B] = trail_left - change[: B - PIV, :B]
            mat[: B - PIV, B:] = trail_right - change[: B - PIV, B:]

    @pl.loop(0, 16)
    def _(piece):
        @pl.when(piece % 4 != y)
        def _():
            piece_from(piece).wait_recv()

    lower = linv[...]
    lt[...] = jnp.dot(lower, at[...], precision=HIGHEST, preferred_element_type=F32)
    tr_v[...] = lt[:, pl.ds(pl.multiple_of(wide // 4 * B, B), B)].T
    panel_hbm[0] = tr_v[pl.ds(pl.multiple_of(wide % 4 * PIV, PIV), PIV), :]
    for d, e in others:
        shared_from(d, e).wait_recv()

    shared = [msgs[c].reshape(PIV, B) for c in range(4)]
    rows_t = jnp.concatenate([gathered(shared, r) for r in range(4)], axis=0)
    own_t = jnp.dot(lower, rows_t, precision=HIGHEST, preferred_element_type=F32)
    update = lax.dot_general(
        own_t, lt[...], (((0,), (0,)), ((), ())), precision=HIGHEST, preferred_element_type=F32
    )

    for part in range(4):
        as_rows = by_rows(part, quarter, z_hi)
        for k in range(4):

            @pl.when(as_rows & (wide != 4 * part + k))
            def _():
                rows_from(part, k).wait_recv()

            @pl.when(jnp.logical_not(as_rows))
            def _():
                columns_from(part, k).wait_recv()

    row = iota((B, Q), 0)
    inside = (row // CYC % 4 == 0) & (wide * CYC + row % CYC < PIV)
    dropped = inside | (iota((B, Q), 1) < PIV)
    schur_hbm[:, 0, :] = jnp.where(dropped, 0.0, f2r[...].reshape(B, Q) - update)

    for n in range(2):
        exchange1(n).wait_send()
    for i in range(4):
        exchange2(i).wait_send()

    @pl.when(y == 0)
    def _():
        corner_term().wait_send()
        for j in range(4):
            pivot_term(j).wait_send()
        for j in range(1, 4):
            own_term(j).wait_send()

        @pl.loop(1, 16)
        def _(d):
            corner_to((wide + d) % 16).wait_send()

    for d in range(1, 4):
        along_z(d).wait_send()
        share_corner(d).wait_send()
        for piece_z in range(4):
            along_y(piece_z, d).wait_send()

    for d, e in others:
        share(d, e).wait_send()

    for o in range(4):
        chunk = (z_hi + o) % 4

        @pl.when(by_rows(z_hi, quarter, chunk))
        def _():
            for k in range(4):
                w = 4 * chunk + k

                @pl.when(w != wide)
                def _():
                    spread_rows(w).wait_send()

        @pl.when(ring(z_hi, chunk) < ring(quarter, chunk))
        def _():
            for k in range(4):
                spread_columns(4 * chunk + k).wait_send()


def on_device(updates, entries1, entries2, leaf_maps, leaf_live, parent_maps, parent_live):
    operands = (updates, entries1, entries2, leaf_maps, leaf_live.T, parent_maps, parent_live)
    operands = tuple(pltpu.with_memory_space_constraint(o, pltpu.HBM) for o in operands)
    dma = pltpu.SemaphoreType.DMA
    vmem = pltpu.VMEM
    return pl.pallas_call(
        kernel,
        out_shape=(
            jax.ShapeDtypeStruct((1, PIV, B), F32),
            jax.ShapeDtypeStruct((B, 1, Q), F32),
        ),
        in_specs=[pl.BlockSpec(memory_space=pltpu.HBM)] * 7,
        out_specs=(pl.BlockSpec(memory_space=pltpu.VMEM),) * 2,
        scratch_shapes=[
            vmem((B, 4 * Q), F32), vmem((B, 1, 2, Q), F32), vmem((B, 1, Q), F32),
            vmem((8, 4 * Q), jnp.int32), vmem((8, 4 * Q), jnp.int32),
            pltpu.SMEM((16, 32), jnp.int32), pltpu.SMEM((16, 16), jnp.int32),
            vmem((2, B, Q), F32), vmem((2, B, Q), F32), vmem((2, B, Q), F32),
            vmem((B, Q), F32), vmem((B, Q), F32), vmem((B, Q), F32), vmem((B, Q), F32),
            vmem((4, 4, CYC, Q), F32), vmem((4, 16, CYC, B), F32), vmem((B, Q), F32), vmem((B, Q), F32),
            vmem((PIV, B), F32), vmem((2, CYC, Q), F32),
            vmem((4, 4, CYC, B), F32), vmem((4, 4, CYC, B), F32), vmem((4, CYC, B), F32), vmem((B, 2 * B), F32), vmem((B, B), F32),
            vmem((B, B), F32),
            dma((7,)), dma((2,)), dma((2,)), dma((4,)), dma((4,)), dma((16,)), dma((16,)), dma((16,)),
            dma, dma, dma((4,)), dma((4,)), dma((2,)), dma((4,)), dma((4, 4)), dma((16,)), dma((4, 4)), dma((4, 4)),
            dma((16,)), dma((4,)), dma((4,)), dma((4,)),
        ],
        compiler_params=pltpu.CompilerParams(
            collective_id=0, has_side_effects=True, vmem_limit_bytes=16 * 1024 * 1024
        ),
        cost_estimate=pl.CostEstimate(flops=600_000_000, bytes_accessed=3_000_000, transcendentals=0),
    )(*operands)


def solution(mesh):
    placed = (
        P("cube", "wide", None),
        P("wide", "cube", None, None),
        P("wide", "cube", None),
        P(),
        P(),
        P(),
        P(),
    )
    return jax.shard_map(
        on_device,
        mesh=mesh,
        in_specs=placed,
        out_specs=(P("cube", "wide", None), P("wide", "cube", None)),
        check_vma=False,
    )
```

```python
import jax
import jax.numpy as jnp
from jax import lax
from jax.experimental import pallas as pl
from jax.experimental.pallas import tpu as pltpu
from jax.sharding import PartitionSpec as P

F32 = jnp.float32
BF16 = jnp.bfloat16
MESH = pl.DeviceIdType.MESH
HIGHEST = lax.Precision.HIGHEST
B = 128
Q = 512
PIV = 32
CYC = 8


def iota(shape, dim):
    return lax.broadcasted_iota(jnp.int32, shape, dim)


def kernel(
    x_hbm, l1_hbm, l2_hbm, lm_hbm, ll_hbm, pm_hbm, pv_hbm,
    panel_hbm, schur_hbm,
    x_v, l1_v, l2_v, lm_v, pm_v, ll_s, pv_s,
    zs, zo, zr, us, uk, ur, f2, f2r, tt, at, lt, cr, terms, tiles, msgs, packs, mat, linv, tr_v,
    in_sem, e1_send, e1_recv, e2_send, e2_recv, aa_send, aa_recv, ac_send,
    cr_send, cr_recv, pa_send, pb_send, pa_recv, zg_send, yg_send, pg_recv, cb_send, cb_recv,
    co_send, co_recv, cs_send, cs_recv,
):
    cube = lax.axis_index("cube")
    wide = lax.axis_index("wide")
    low = cube % 2
    high = cube // 2 % 2
    quarter = cube % 4
    group = cube - quarter
    z_hi = wide // 4
    y = wide % 4
    parent = cube // 2
    lane = iota((B, B), 1)

    def ring(a, b):
        m = (a - b + 4) % 4
        return m - m // 3 * 2

    def by_rows(part, home, at_z):
        return ring(part, at_z) <= ring(home, at_z)

    lm_base = pl.multiple_of(cube // 8 * 8, 8)
    pm_base = pl.multiple_of(parent // 8 * 8, 8)
    loads = [
        pltpu.make_async_copy(lm_hbm.at[pl.ds(lm_base, 8)], lm_v, in_sem.at[0]),
        pltpu.make_async_copy(ll_hbm, ll_s, in_sem.at[1]),
        pltpu.make_async_copy(x_hbm.at[0], x_v, in_sem.at[2]),
        pltpu.make_async_copy(l1_hbm, l1_v, in_sem.at[3]),
        pltpu.make_async_copy(pm_hbm.at[pl.ds(pm_base, 8)], pm_v, in_sem.at[4]),
        pltpu.make_async_copy(pv_hbm, pv_s, in_sem.at[5]),
        pltpu.make_async_copy(l2_hbm, l2_v, in_sem.at[6]),
    ]
    for load in loads:
        load.start()

    barrier = pltpu.get_barrier_semaphore()

    def greet(c, w):
        pl.semaphore_signal(barrier, inc=1, device_id=(c, w), device_id_type=MESH)

    @pl.loop(0, 15)
    def _(n):
        greet(cube, (wide + 8 + n + n // 8) % 16)

    for part in range(4):

        @pl.when(jnp.logical_not(by_rows(part, quarter, z_hi)))
        def _():
            for k in range(4):
                greet(group + part, 4 * quarter + k)

    greet(cube ^ 2, 4 * z_hi)
    for d in (2, 3, 1):
        for e in range(4):
            greet(cube ^ d, 4 * z_hi + (y + e) % 4)
    apart = ring(z_hi, quarter)
    greetings = 27 + 4 * (apart % 2 * 2 + apart // 2) + 4 * (1 - (y + 3) // 4)

    def one_hot(map_ref, live_ref, live_row, block):
        lanes = pl.multiple_of(block * B, B)
        entry = map_ref[:1, pl.ds(lanes, B)] - lanes
        live = live_ref[block, live_row] if live_ref is ll_s else live_ref[live_row, block]
        hit = (entry == iota((B, B), 0)) & (iota((B, B), 1) < live)
        return jnp.where(hit, 1.0, 0.0).astype(BF16)

    def map_quarter(values, row_hot, hots):
        top = values.astype(BF16)
        rest = (values - top.astype(F32)).astype(BF16)
        top = jnp.dot(row_hot, top, preferred_element_type=F32).astype(BF16)
        rest = jnp.dot(row_hot, rest, preferred_element_type=F32).astype(BF16)
        parts = []
        for i in range(4):
            both = jnp.concatenate((top[:, i * B : (i + 1) * B], rest[:, i * B : (i + 1) * B]), axis=0)
            got = lax.dot_general(both, hots[i], (((1,), (1,)), ((), ())), preferred_element_type=F32)
            parts.append(got[:B] + got[B:])
        return jnp.concatenate(parts, axis=1)

    loads[0].wait()
    loads[1].wait()
    lm_v[:1, :] = lm_v[pl.ds(cube - lm_base, 1), :]
    row_hot = one_hot(lm_v, ll_s, cube, wide)
    loads[2].wait()

    def leaf_quarter(at_quarter):
        hots = [one_hot(lm_v, ll_s, cube, at_quarter * 4 + i) for i in range(4)]
        values = x_v[:, pl.ds(pl.multiple_of(at_quarter * Q, Q), Q)]
        return map_quarter(values, row_hot, hots)

    def exchange1(n):
        return pltpu.make_async_remote_copy(
            src_ref=zs.at[n], dst_ref=zr.at[n], send_sem=e1_send.at[n], recv_sem=e1_recv.at[n],
            device_id=(cube ^ 1, wide), device_id_type=MESH,
        )

    for n in range(2):
        half = 1 - high if n == 0 else high
        zs[n] = leaf_quarter(2 * half + 1 - low)
        if n == 0:
            pl.semaphore_wait(barrier, greetings)
        exchange1(n).start()
    for n in range(2):
        half = 1 - high if n == 0 else high
        zo[n] = leaf_quarter(2 * half + low)

    for n in range(3, 7):
        loads[n].wait()
    pm_v[:1, :] = pm_v[pl.ds(parent - pm_base, 1), :]
    up_row_hot = one_hot(pm_v, pv_s, parent, wide)

    def upper_quarter(n):
        half = 1 - high if n == 0 else high
        first = jnp.where(half == 0, l1_v[:, 0, 0, :], l1_v[:, 0, 1, :])
        values = first + zo[n] + zr[n]
        hots = [one_hot(pm_v, pv_s, parent, (2 * half + low) * 4 + i) for i in range(4)]
        return map_quarter(values, up_row_hot, hots)

    def exchange2(i):
        rows = pl.ds(pl.multiple_of(i * 32, 32), 32)
        return pltpu.make_async_remote_copy(
            src_ref=us.at[rows], dst_ref=ur.at[rows], send_sem=e2_send.at[i], recv_sem=e2_recv.at[i],
            device_id=(cube ^ 2, wide), device_id_type=MESH,
        )

    exchange1(0).wait_recv()
    us[...] = upper_quarter(0)
    def rows_of(w):
        return pl.ds(pl.multiple_of(w * CYC, CYC), CYC)

    def corner_term():
        return pltpu.make_async_remote_copy(
            src_ref=us.at[pl.ds(0, PIV), pl.ds(0, B)], dst_ref=cr, send_sem=cr_send, recv_sem=cr_recv,
            device_id=(cube ^ 2, wide), device_id_type=MESH,
        )

    def pivot_term(j):
        return pltpu.make_async_remote_copy(
            src_ref=us.at[pl.ds(j * CYC, CYC)], dst_ref=terms.at[0], send_sem=pa_send.at[j], recv_sem=pa_recv.at[0],
            device_id=(cube ^ 2, 4 * z_hi + j), device_id_type=MESH,
        )

    def own_term(j):
        return pltpu.make_async_remote_copy(
            src_ref=uk.at[pl.ds(j * CYC, CYC)], dst_ref=terms.at[1], send_sem=pb_send.at[j], recv_sem=pa_recv.at[1],
            device_id=(cube, 4 * z_hi + j), device_id_type=MESH,
        )

    @pl.when(y == 0)
    def _():
        corner_term().start()
        for j in (2, 1, 3, 0):
            pivot_term(j).start()

    order = (2, 1, 3, 0)
    exchange2((z_hi + 2) % 4).start()

    @pl.when(y != 0)
    def _():
        exchange2((z_hi + 1) % 4).start()

    exchange1(1).wait_recv()
    uk[...] = upper_quarter(1) + l2_v[:, 0, :]

    def corner_to(w):
        return pltpu.make_async_remote_copy(
            src_ref=tiles.at[quarter, z_hi], dst_ref=tiles.at[quarter, z_hi],
            send_sem=co_send.at[w], recv_sem=co_recv.at[z_hi],
            device_id=(cube, w), device_id_type=MESH,
        )

    def along_z(d):
        return pltpu.make_async_remote_copy(
            src_ref=at.at[rows_of(wide)], dst_ref=at.at[rows_of(wide)],
            send_sem=zg_send.at[d], recv_sem=pg_recv.at[wide],
            device_id=(cube, (wide + 4 * d) % 16), device_id_type=MESH,
        )

    def along_y(piece_z, d):
        piece = 4 * piece_z + y
        return pltpu.make_async_remote_copy(
            src_ref=at.at[rows_of(piece)], dst_ref=at.at[rows_of(piece)],
            send_sem=yg_send.at[piece_z, d], recv_sem=pg_recv.at[piece],
            device_id=(cube, 4 * z_hi + (y + d) % 4), device_id_type=MESH,
        )

    def piece_from(piece):
        return pltpu.make_async_remote_copy(
            src_ref=at.at[rows_of(piece)], dst_ref=at.at[rows_of(piece)],
            send_sem=zg_send.at[0], recv_sem=pg_recv.at[piece],
            device_id=(cube, piece), device_id_type=MESH,
        )

    def term_from(n):
        return pltpu.make_async_remote_copy(
            src_ref=us.at[pl.ds(0, CYC)], dst_ref=terms.at[n], send_sem=pa_send.at[0], recv_sem=pa_recv.at[n],
            device_id=(cube ^ 2, 4 * z_hi), device_id_type=MESH,
        )

    @pl.when(y == 0)
    def _():
        for j in (2, 1, 3):
            own_term(j).start()
        corner_term().wait_recv()
        block = uk[:PIV, :B] + cr[...]
        tile = block[:CYC]
        for r in range(1, 4):
            moved = pltpu.roll(block[CYC * r : CYC * (r + 1)], PIV * r, 1)
            tile = jnp.where(lane[:CYC] >= PIV * r, moved, tile)
        tiles[quarter, z_hi] = tile

        @pl.loop(0, 15)
        def _(n):
            corner_to((wide + 8 + n + n // 8) % 16).start()

        term_from(0).wait_recv()
        at[rows_of(wide), :] = terms[0] + uk[:CYC, :]

    @pl.when(y != 0)
    def _():
        term_from(0).wait_recv()
        term_from(1).wait_recv()
        at[rows_of(wide), :] = terms[0] + terms[1]

    for d in (2, 1, 3):
        along_z(d).start()
    for d in (2, 1, 3):
        along_y(z_hi, d).start()

    @pl.when(y == 0)
    def _():
        exchange2((z_hi + 1) % 4).start()

    for o in order[2:]:
        exchange2((z_hi + o) % 4).start()

    def share_corner(d):
        return pltpu.make_async_remote_copy(
            src_ref=tiles.at[quarter], dst_ref=tiles.at[quarter],
            send_sem=cs_send.at[d], recv_sem=cs_recv.at[quarter],
            device_id=(cube ^ d, wide), device_id_type=MESH,
        )

    def corner_from(q):
        return pltpu.make_async_remote_copy(
            src_ref=tiles.at[quarter, q], dst_ref=tiles.at[quarter, q],
            send_sem=co_send.at[0], recv_sem=co_recv.at[q],
            device_id=(cube, 4 * q), device_id_type=MESH,
        )

    def spread_rows(w):
        return pltpu.make_async_remote_copy(
            src_ref=f2.at[rows_of(w)], dst_ref=f2r.at[z_hi, y],
            send_sem=aa_send.at[w], recv_sem=aa_recv.at[wide],
            device_id=(cube, w), device_id_type=MESH,
        )

    def spread_columns(w):
        return pltpu.make_async_remote_copy(
            src_ref=tt.at[:, w], dst_ref=f2r.at[quarter, :, :, pl.ds(pl.multiple_of(y * B, B), B)],
            send_sem=ac_send.at[w], recv_sem=aa_recv.at[4 * quarter + y],
            device_id=(group + z_hi, w), device_id_type=MESH,
        )

    def rows_from(part, k):
        return pltpu.make_async_remote_copy(
            src_ref=f2.at[rows_of(0)], dst_ref=f2r.at[part, k],
            send_sem=aa_send.at[0], recv_sem=aa_recv.at[4 * part + k],
            device_id=(cube, 4 * part + k), device_id_type=MESH,
        )

    def columns_from(part, k):
        return pltpu.make_async_remote_copy(
            src_ref=tt.at[:, 0], dst_ref=f2r.at[part, :, :, pl.ds(k * B, B)],
            send_sem=ac_send.at[0], recv_sem=aa_recv.at[4 * part + k],
            device_id=(group + part, 4 * quarter + k), device_id_type=MESH,
        )

    def start_rows(chunk):
        @pl.when(by_rows(z_hi, quarter, chunk))
        def _():
            for k in range(4):
                w = 4 * chunk + k

                @pl.when(w != wide)
                def _():
                    spread_rows(w).start()

    for o in order:
        chunk = (z_hi + o) % 4
        exchange2(chunk).wait_recv()
        rows = pl.ds(pl.multiple_of(chunk * 32, 32), 32)
        f2[rows, :] = uk[rows, :] + ur[rows, :]


    f2r[z_hi, y] = f2[rows_of(wide), :]

    @pl.when(z_hi != quarter)
    def _():
        for i in range(4):
            tt[i] = f2[:, i * B : (i + 1) * B].T.reshape(16, CYC, B)

    for q in range(4):

        @pl.when(wide != 4 * q)
        def _():
            corner_from(q).wait_recv()

    for d in (2, 3, 1):
        share_corner(d).start()

    for o in (1, 3, 2):
        piece_z = (z_hi + o) % 4
        piece_from(4 * piece_z + y).wait_recv()
        for d in (2, 1, 3):
            along_y(piece_z, d).start()

    for e in range(4):
        to_y = (y + e) % 4
        packed = jnp.zeros((CYC, B), F32)
        for r in range(4):
            rows = at[rows_of(4 * r + y), :]
            for i in range(4):
                first = PIV * r + CYC * i
                moved = pltpu.roll(rows[:, B * i : B * (i + 1)], (first + B - CYC * (4 * z_hi + to_y)) % B, 1)
                packed = jnp.where(lane[:CYC] >= first, moved, packed)
        packs[e] = packed

    def share(d, e):
        return pltpu.make_async_remote_copy(
            src_ref=packs.at[e], dst_ref=msgs.at[quarter, y], send_sem=cb_send.at[d, e], recv_sem=cb_recv.at[quarter, y],
            device_id=(cube ^ d, 4 * z_hi + (y + e) % 4), device_id_type=MESH,
        )

    def shared_from(d, e):
        other, other_y = quarter ^ d, (y + e) % 4
        return pltpu.make_async_remote_copy(
            src_ref=packs.at[0], dst_ref=msgs.at[other, other_y], send_sem=cb_send.at[d, e], recv_sem=cb_recv.at[other, other_y],
            device_id=(group + other, 4 * z_hi + other_y), device_id_type=MESH,
        )

    others = [(d, e) for d in (2, 3, 1, 0) for e in (2, 1, 3, 0) if d or e]
    for d, e in others:
        share(d, e).start()
    msgs[quarter, y] = packs[0]

    for o in order:
        start_rows((z_hi + o) % 4)

    @pl.when(z_hi != quarter)
    def _():
        for o in (1, 3, 0):
            chunk = (z_hi + o) % 4

            @pl.when(ring(z_hi, chunk) < ring(quarter, chunk))
            def _():
                for k in range(4):
                    spread_columns(4 * chunk + k).start()

    for d in range(1, 4):
        other = quarter ^ d
        pltpu.make_async_remote_copy(
            src_ref=tiles.at[other], dst_ref=tiles.at[other],
            send_sem=cs_send.at[d], recv_sem=cs_recv.at[other],
            device_id=(group + other, wide), device_id_type=MESH,
        ).wait_recv()

    def gathered(parts, r):
        got = parts[0]
        if r:
            got = pltpu.roll(got, B - PIV * r, 1)
        for c in range(1, 4):
            moved = parts[c] if c == r else pltpu.roll(parts[c], PIV * (c - r) % B, 1)
            got = jnp.where(lane[:PIV] >= PIV * c, moved, got)
        return got

    corners = [tiles[c].reshape(PIV, B) for c in range(4)]
    for r in range(4):
        got = gathered(corners, r)
        for q in range(4):
            mat[PIV * q + CYC * r : PIV * q + CYC * (r + 1), :B] = got[CYC * q : CYC * (q + 1)]
    mat[:, B:] = jnp.where(iota((B, B), 0) == lane, 1.0, 0.0)

    @pl.loop(0, 4)
    def _(step):
        left = mat[:PIV, :B]
        right = mat[:PIV, B:]
        row_id = iota((PIV, B), 0)
        diag = jnp.ones((PIV, B), F32)
        for first in range(0, PIV, CYC):
            columns = [jnp.broadcast_to(left[:, first + n : first + n + 1], (PIV, B)) for n in range(CYC)]
            for n in range(CYC):
                j = first + n
                pivot = columns[n][j : j + 1, :]
                diag = jnp.where(row_id == j, pivot, diag)
                inverse = pl.reciprocal(pivot, approx=True)
                inverse = inverse * (2.0 - pivot * inverse)
                factor = jnp.where(row_id > j, columns[n] * inverse, 0.0)
                for m in range(n + 1, CYC):
                    columns[m] = columns[m] - factor * columns[m][j : j + 1, :]
                left = left - factor * left[j : j + 1, :]
                right = right - factor * right[j : j + 1, :]
        scale = lax.rsqrt(diag)
        right = right * scale
        linv[pl.ds(pl.multiple_of(step * PIV, PIV), PIV), :] = right

        @pl.when(step < 3)
        def _():
            moved = pltpu.roll(left * scale, B - PIV, 1)
            moved = jnp.where(lane[:PIV] < B - PIV, moved, 0.0)
            both = jnp.concatenate((moved, right), axis=1)
            change = lax.dot_general(
                moved, both, (((0,), (0,)), ((), ())), precision=HIGHEST, preferred_element_type=F32
            )
            trail_left = pltpu.roll(mat[PIV:, :B], B - PIV, 1)
            trail_right = mat[PIV:, B:]
            mat[: B - PIV, :B] = trail_left - change[: B - PIV, :B]
            mat[: B - PIV, B:] = trail_right - change[: B - PIV, B:]

    @pl.loop(0, 16)
    def _(piece):
        @pl.when(piece % 4 != y)
        def _():
            piece_from(piece).wait_recv()

    lower = linv[...]
    lt[...] = jnp.dot(lower, at[...], precision=HIGHEST, preferred_element_type=F32)
    tr_v[...] = lt[:, pl.ds(pl.multiple_of(wide // 4 * B, B), B)].T
    panel_hbm[0] = tr_v[pl.ds(pl.multiple_of(wide % 4 * PIV, PIV), PIV), :]
    for d, e in others:
        shared_from(d, e).wait_recv()

    shared = [msgs[c].reshape(PIV, B) for c in range(4)]
    rows_t = jnp.concatenate([gathered(shared, r) for r in range(4)], axis=0)
    own_t = jnp.dot(lower, rows_t, precision=HIGHEST, preferred_element_type=F32)
    update = lax.dot_general(
        own_t, lt[...], (((0,), (0,)), ((), ())), precision=HIGHEST, preferred_element_type=F32
    )

    for part in range(4):
        as_rows = by_rows(part, quarter, z_hi)
        for k in range(4):

            @pl.when(as_rows & (wide != 4 * part + k))
            def _():
                rows_from(part, k).wait_recv()

            @pl.when(jnp.logical_not(as_rows))
            def _():
                columns_from(part, k).wait_recv()

    row = iota((B, Q), 0)
    inside = (row // CYC % 4 == 0) & (wide * CYC + row % CYC < PIV)
    dropped = inside | (iota((B, Q), 1) < PIV)
    schur_hbm[:, 0, :] = jnp.where(dropped, 0.0, f2r[...].reshape(B, Q) - update)

    for n in range(2):
        exchange1(n).wait_send()
    for i in range(4):
        exchange2(i).wait_send()

    @pl.when(y == 0)
    def _():
        corner_term().wait_send()
        for j in range(4):
            pivot_term(j).wait_send()
        for j in range(1, 4):
            own_term(j).wait_send()

        @pl.loop(1, 16)
        def _(d):
            corner_to((wide + d) % 16).wait_send()

    for d in range(1, 4):
        along_z(d).wait_send()
        share_corner(d).wait_send()
        for piece_z in range(4):
            along_y(piece_z, d).wait_send()

    for d, e in others:
        share(d, e).wait_send()

    for o in range(4):
        chunk = (z_hi + o) % 4

        @pl.when(by_rows(z_hi, quarter, chunk))
        def _():
            for k in range(4):
                w = 4 * chunk + k

                @pl.when(w != wide)
                def _():
                    spread_rows(w).wait_send()

        @pl.when(ring(z_hi, chunk) < ring(quarter, chunk))
        def _():
            for k in range(4):
                spread_columns(4 * chunk + k).wait_send()


def on_device(updates, entries1, entries2, leaf_maps, leaf_live, parent_maps, parent_live):
    operands = (updates, entries1, entries2, leaf_maps, leaf_live.T, parent_maps, parent_live)
    operands = tuple(pltpu.with_memory_space_constraint(o, pltpu.HBM) for o in operands)
    dma = pltpu.SemaphoreType.DMA
    vmem = pltpu.VMEM
    return pl.pallas_call(
        kernel,
        out_shape=(
            jax.ShapeDtypeStruct((1, PIV, B), F32),
            jax.ShapeDtypeStruct((B, 1, Q), F32),
        ),
        in_specs=[pl.BlockSpec(memory_space=pltpu.HBM)] * 7,
        out_specs=(pl.BlockSpec(memory_space=pltpu.VMEM),) * 2,
        scratch_shapes=[
            vmem((B, 4 * Q), F32), vmem((B, 1, 2, Q), F32), vmem((B, 1, Q), F32),
            vmem((8, 4 * Q), jnp.int32), vmem((8, 4 * Q), jnp.int32),
            pltpu.SMEM((16, 32), jnp.int32), pltpu.SMEM((16, 16), jnp.int32),
            vmem((2, B, Q), F32), vmem((2, B, Q), F32), vmem((2, B, Q), F32),
            vmem((B, Q), F32), vmem((B, Q), F32), vmem((B, Q), F32), vmem((B, Q), F32),
            vmem((4, 4, CYC, Q), F32), vmem((4, 16, CYC, B), F32), vmem((B, Q), F32), vmem((B, Q), F32),
            vmem((PIV, B), F32), vmem((2, CYC, Q), F32),
            vmem((4, 4, CYC, B), F32), vmem((4, 4, CYC, B), F32), vmem((4, CYC, B), F32), vmem((B, 2 * B), F32), vmem((B, B), F32),
            vmem((B, B), F32),
            dma((7,)), dma((2,)), dma((2,)), dma((4,)), dma((4,)), dma((16,)), dma((16,)), dma((16,)),
            dma, dma, dma((4,)), dma((4,)), dma((2,)), dma((4,)), dma((4, 4)), dma((16,)), dma((4, 4)), dma((4, 4)),
            dma((16,)), dma((4,)), dma((4,)), dma((4,)),
        ],
        compiler_params=pltpu.CompilerParams(
            collective_id=0, has_side_effects=True, vmem_limit_bytes=16 * 1024 * 1024
        ),
        cost_estimate=pl.CostEstimate(flops=600_000_000, bytes_accessed=3_000_000, transcendentals=0),
    )(*operands)


def solution(mesh):
    placed = (
        P("cube", "wide", None),
        P("wide", "cube", None, None),
        P("wide", "cube", None),
        P(),
        P(),
        P(),
        P(),
    )
    return jax.shard_map(
        on_device,
        mesh=mesh,
        in_specs=placed,
        out_specs=(P("cube", "wide", None), P("wide", "cube", None)),
        check_vma=False,
    )
```
